128 devices in a mesh: dp: 16 (over z, y), ctx: 2 (over core), tensor: 4 (over x).
Axes of the slice: x: 4, y: 4, z: 4, core: 2. Of those that a mesh axis runs over, the one named last changes fastest.
Arguments:
- patches: bfloat16 [30720, 768], P(('dp', 'ctx')), may hold values from -6 to 6
- text_features: bfloat16 [64, 16, 768], P('dp', 'ctx'), may hold values from -6 to 6
- patch_weight: bfloat16 [768, 768], P(None, 'tensor'), may hold values from -0.21875 to 0.21875
- patch_bias: float32 [768], P('tensor'), may hold values from -3 to 3
- text_weight: bfloat16 [768, 768], P(None, 'tensor'), may hold values from -0.21875 to 0.21875
- text_bias: float32 [768], P('tensor'), may hold values from -3 to 3
- readout: bfloat16 [768], P('tensor'), may hold values from -6 to 6
- mix_gain: float32 [2, 768], replicated, may hold values from 0.5 to 1.5
- mix_shift: float32 [2, 768], replicated, may hold values from -2 to 2
- heads_in_weight: bfloat16 [2, 768, 3, 768], P(None, None, None, 'tensor'), may hold values from -0.21875 to 0.21875
- heads_out_weight: bfloat16 [2, 768, 768], P(None, 'tensor'), may hold values from -3 to 3
- feed_gain: float32 [2, 768], replicated, may hold values from 0.5 to 1.5
- feed_shift: float32 [2, 768], replicated, may hold values from -2 to 2
- up_weight: bfloat16 [2, 768, 3072], P(None, None, 'tensor'), may hold values from -0.21875 to 0.21875
- up_bias: float32 [2, 3072], P(None, 'tensor'), may hold values from -3 to 3
- down_weight: bfloat16 [2, 3072, 768], P(None, 'tensor'), may hold values from -0.109375 to 0.109375
- timesteps: int32 [64, 512], P('dp'), may hold values from 0 to 15, as said below
- datasets: int32 [64], P('dp'), may hold values from 0 to 24
- dataset_weights: int32 [25], replicated, may hold values from 1 to 4
- action_mask: int32 [64, 16], P('dp', 'ctx'), may hold values 0 or 1
- cotangent: bfloat16 [64, 512, 768], P('dp', 'ctx'), may hold values from -6 to 6
Outputs:
- activations: bfloat16 [64, 512, 768], P('dp', 'ctx', 'tensor')
- patches_gradient: float32 [30720, 768], P(('dp', 'ctx'), 'tensor')
- text_gradient: float32 [64, 16, 768], P('dp', 'ctx', 'tensor')
- patch_weight_gradient: float32 [768, 768], P(None, 'tensor')
- patch_bias_gradient: float32 [768], P('tensor')
- text_weight_gradient: float32 [768, 768], P(None, 'tensor')
- text_bias_gradient: float32 [768], P('tensor')
- readout_gradient: float32 [768], P('tensor')
- mix_gain_gradient: float32 [2, 768], P(None, 'tensor')
- mix_shift_gradient: float32 [2, 768], P(None, 'tensor')
- heads_in_gradient: float32 [2, 768, 3, 768], P(None, None, None, 'tensor')
- heads_out_gradient: float32 [2, 768, 768], P(None, 'tensor')
- feed_gain_gradient: float32 [2, 768], P(None, 'tensor')
- feed_shift_gradient: float32 [2, 768], P(None, 'tensor')
- up_weight_gradient: float32 [2, 768, 3072], P(None, None, 'tensor')
- up_bias_gradient: float32 [2, 3072], P(None, 'tensor')
- down_weight_gradient: float32 [2, 3072, 768], P(None, 'tensor')
The draws below stay inside these ranges and needn't reach their ends.
Inputs may be any that keep to these rules, and one draw needn't show every extreme that they name: `timesteps`: each item's row starts at 0 and never falls, rising by 0 or 1 from one position to the next and ending at the maximum; positions 192 to 320 share one value.
All inputs are finite; a program needn't handle non-finite values. No bound on the sum of `action_mask` on one device may be relied on, other than what follows from the above.
Results may differ from the reference program's by a relative error of at most 0.028.
Values may be sent and summed in bfloat16 or wider, within the bound.
A program may use at most 192 MiB of HBM per device.

```python
import math
import jax
import jax.numpy as jnp
from jax import lax

D = 768
HEADS = 12
HEAD_DIM = 64
FF = 3072
LANG = 768
PIX = 768
NL = 2
L = 512
IMG_GROUP = 30
NDS = 25
SEQ_DEV = 4
GROUP = 32
GROUPS = 16
ITEMS = 64
IMG_ROWS = 30720
PIECE = 60
N_DP = 16
N_CTX = 2


def draw_timesteps(key, part):
    key = jax.random.fold_in(key, 11)
    places = jnp.arange(L)
    steady = (places == 0) | (places > L // 2 - L // 8) & (places <= L // 2 + L // 8)
    rises = max((L - 1 - 2 * (L // 8)) // 24, 2)
    rolls = jax.random.randint(key, (ITEMS, L), 0, 1048576)
    ranked = rolls * L + places[None, :]
    ranked = jnp.where(steady[None, :], -1, ranked)
    order = jnp.argsort(-ranked, axis=1, stable=True)
    chosen = order[:, :rises]
    rows_index = jnp.arange(ITEMS)[:, None]
    flags = jnp.zeros((ITEMS, L), jnp.int32).at[rows_index, chosen].set(1)
    return jnp.cumsum(flags, axis=1).astype(jnp.int32)


def set_ends(values, rng, smallest, high):
    shape = values.shape
    index_at = [jax.random.randint(jax.random.fold_in(rng, axis), (), 0, shape[axis]) for axis in range(len(shape))]
    values = values.at[tuple(index_at)].set(smallest)
    longest = shape.index(max(shape))
    index_at[longest] = (index_at[longest] + 1) % shape[longest]
    return values.at[tuple(index_at)].set(high)


def shard_levels(own_key, shape, cuts, low, high):
    level = 1.0
    for axis_at, blocks in cuts:
        heights = jax.random.uniform(jax.random.fold_in(jax.random.fold_in(own_key, 6), axis_at), (blocks,), jnp.float32, low / len(cuts), high / len(cuts))
        level = level * jnp.repeat(jnp.exp(heights), shape[axis_at] // blocks).reshape((-1,) + (1,) * (len(shape) - 1 - axis_at))
    return level


def noise(rng, extent, scale, most, split=(), dtype=jnp.bfloat16):
    result = jax.random.normal(rng, extent, jnp.float32) * scale
    if len(split) > 0:
        result = shard_levels(rng, extent, split, -0.22, 0.18) * result
    return jnp.clip(result, min=-most, max=most).astype(dtype)


def setup_inputs(seed: int = 0) -> dict:
    key_list = jax.random.split(jax.random.key(seed), 22)
    return {
        "patches": noise(key_list[0], (IMG_ROWS, PIX), 1.0, 6.0, ((0, 32),)),
        "text_features": noise(key_list[1], (ITEMS, GROUPS, LANG), 1.0, 6.0, ((0, 16), (1, 2))),
        "patch_weight": noise(key_list[2], (PIX, D), PIX ** -0.5, 0.21875, ((1, 4),)),
        "patch_bias": noise(key_list[3], (D,), 0.5, 3.0, ((0, 4),), jnp.float32),
        "text_weight": noise(key_list[4], (LANG, D), LANG ** -0.5, 0.21875, ((1, 4),)),
        "text_bias": noise(key_list[5], (D,), 0.5, 3.0, ((0, 4),), jnp.float32),
        "readout": noise(key_list[6], (D,), 1.0, 6.0, ((0, 4),)),
        "mix_gain": jnp.clip(1.0 + 0.1 * jax.random.normal(key_list[7], (NL, D), jnp.float32), 0.5, 1.5),
        "mix_shift": noise(key_list[8], (NL, D), 0.3, 2.0, (), jnp.float32),
        "heads_in_weight": noise(key_list[9], (NL, D, 3, D), D ** -0.5, 0.21875, ((3, 4),)),
        "heads_out_weight": noise(key_list[10], (NL, D, D), (max(3 * D // L, 1)) ** -0.5, 3.0, ((1, 4),)),
        "feed_gain": jnp.clip(1.0 + 0.1 * jax.random.normal(key_list[11], (NL, D), jnp.float32), 0.5, 1.5),
        "feed_shift": noise(key_list[12], (NL, D), 0.3, 2.0, (), jnp.float32),
        "up_weight": noise(key_list[13], (NL, D, FF), D ** -0.5, 0.21875, ((2, 4),)),
        "up_bias": noise(key_list[14], (NL, FF), 0.5, 3.0, ((1, 4),), jnp.float32),
        "down_weight": noise(key_list[15], (NL, FF, D), FF ** -0.5, 0.109375, ((1, 4),)),
        "timesteps": draw_timesteps(jax.random.fold_in(key_list[21], 71), 0),
        "datasets": set_ends(jax.random.randint(key_list[17], (ITEMS,), 0, NDS), jax.random.fold_in(key_list[17], 1), 0, NDS - 1).astype(jnp.int32),
        "dataset_weights": set_ends(jax.random.randint(key_list[18], (NDS,), 1, 5), jax.random.fold_in(key_list[18], 1), 1, 4).astype(jnp.int32),
        "action_mask": set_ends((jax.random.randint(key_list[19], (ITEMS, GROUPS), 0, 4) < 3).astype(jnp.int32), jax.random.fold_in(key_list[19], 1), 0, 1),
        "cotangent": noise(key_list[20], (ITEMS, L, D), 1.0, 6.0, ((0, 16), (1, 2))),
    }


@jax.custom_vjp
def low(v):
    return lax.optimization_barrier(v.astype(jnp.bfloat16)).astype(jnp.float32)

@jax.custom_vjp
def low_back(v):
    return v

def low_keep(v):
    return (low(v), None)

def low_pass(kept, grad):
    return (grad,)

def back_keep(v):
    return (v, None)

def back_low(kept, grad):
    return (low(grad),)
low.defvjp(low_keep, low_pass)
low_back.defvjp(back_keep, back_low)
HIGH = lax.Precision.HIGHEST
EPS = 1e-06
MASKED = -1e+30

def product(left, right):
    return jnp.dot(left, right, precision=HIGH, preferred_element_type=jnp.float32)

def normalize(stream, gain_row, shift_row):
    row_mean = lax.optimization_barrier(jnp.mean(stream, axis=-1, keepdims=True))
    centred = stream - row_mean
    spread = lax.optimization_barrier(jnp.mean(centred * centred, axis=-1, keepdims=True))
    return centred * lax.rsqrt(spread + EPS) * gain_row + shift_row

def attend(triple, stamps):
    queries = triple[:, 0].reshape(L, HEADS, HEAD_DIM)
    keys = triple[:, 1].reshape(L, HEADS, HEAD_DIM)
    values = triple[:, 2].reshape(L, HEADS, HEAD_DIM)
    scores = jnp.einsum('qhd,khd->hqk', queries, keys, precision=HIGH) * HEAD_DIM ** (-0.5)
    scores = low_back(scores)
    visible = stamps[None, :] <= stamps[:, None]
    scores = jnp.where(visible[None], scores, MASKED)
    top = lax.optimization_barrier(jnp.max(scores, axis=-1, keepdims=True))
    weights = jnp.exp(scores - top)
    weights = weights / lax.optimization_barrier(jnp.sum(weights, axis=-1, keepdims=True))
    weights = low(weights)
    return jnp.einsum('hqk,khd->qhd', weights, values, precision=HIGH).reshape(L, D)

def attend_bundle(inputs):
    triple, stamps = inputs
    return jax.vmap(attend)(triple, stamps)

def block(stream, timesteps, mix_gain, mix_shift, heads_in_weight, heads_out_weight, feed_gain, feed_shift, up_weight, up_bias, down_weight):
    normed = low(normalize(stream, mix_gain, mix_shift))
    triple = low_back(low(product(normed, heads_in_weight.reshape(D, 3 * D))))
    bundle = math.gcd(ITEMS, max(4096 // L, 1))
    stacked = triple.reshape(ITEMS // bundle, bundle, L, 3, D)
    stamps = timesteps.reshape(ITEMS // bundle, bundle, L)
    mixed = lax.map(jax.checkpoint(attend_bundle), (stacked, stamps))
    mixed = low_back(low(mixed.reshape(ITEMS * L, D)))
    middle = stream + low_back(product(mixed, heads_out_weight))
    feed_normed = low(normalize(middle, feed_gain, feed_shift))
    pre_act = low_back(product(feed_normed, up_weight) + up_bias)
    hidden = low(jax.nn.gelu(pre_act, approximate=True))
    return middle + low_back(product(hidden, down_weight))

def reference(patches, text_features, patch_weight, patch_bias, text_weight, text_bias, readout, mix_gain, mix_shift, heads_in_weight, heads_out_weight, feed_gain, feed_shift, up_weight, up_bias, down_weight, timesteps, datasets, dataset_weights, action_mask, cotangent):
    floats = tuple((array.astype(jnp.float32) for array in (patches, text_features, patch_weight, patch_bias, text_weight, text_bias, readout, mix_gain, mix_shift, heads_in_weight, heads_out_weight, feed_gain, feed_shift, up_weight, up_bias, down_weight)))

    def forward(patches, text_features, patch_weight, patch_bias, text_weight, text_bias, readout, mix_gain, mix_shift, heads_in_weight, heads_out_weight, feed_gain, feed_shift, up_weight, up_bias, down_weight):
        picture = low_back(low(product(patches, patch_weight) + patch_bias))
        picture = picture.reshape(N_DP, N_CTX, N_DP, PIECE, D).transpose(2, 1, 0, 3, 4)
        picture = picture.reshape(N_DP, N_CTX, SEQ_DEV, GROUPS // N_CTX, IMG_GROUP, D).transpose(0, 2, 1, 3, 4, 5)
        picture = picture.reshape(ITEMS, GROUPS, IMG_GROUP, D)
        words = low_back(low(product(text_features.reshape(ITEMS * GROUPS, LANG), text_weight) + text_bias))
        words = words.reshape(ITEMS, GROUPS, 1, D)
        marker = jnp.broadcast_to(readout, (ITEMS, GROUPS, 1, D))
        stream = jnp.concatenate([picture, words, marker], axis=2).reshape(ITEMS * L, D)
        for which in range(NL):
            stream = block(stream, timesteps, mix_gain[which], mix_shift[which], heads_in_weight[which], heads_out_weight[which], feed_gain[which], feed_shift[which], up_weight[which], up_bias[which], down_weight[which])
        return stream.reshape(ITEMS, L, D)
    item_weight = dataset_weights[datasets].astype(jnp.float32)
    readout_scale = item_weight[:, None] * action_mask.astype(jnp.float32)
    upstream = cotangent.astype(jnp.float32).reshape(ITEMS, GROUPS, GROUP, D)
    upstream = upstream.at[:, :, IMG_GROUP + 1, :].multiply(readout_scale[:, :, None])
    outputs, pullback = jax.vjp(forward, *floats)
    grads = pullback(upstream.reshape(ITEMS, L, D))
    return (outputs.astype(jnp.bfloat16), grads[0], grads[1], grads[2], grads[3], grads[4], grads[5], grads[6], grads[7], grads[8], grads[9], grads[10], grads[11], grads[12], grads[13], grads[14], grads[15])
```

```python
import jax
import jax.numpy as jnp
from jax import lax
from jax.experimental import pallas as pl
from jax.experimental.pallas import tpu as pltpu
from jax.sharding import PartitionSpec as P

HEAD_DIM = 64
HEADS = 12
NL = 2
L = 512
HALF = 256
D = 768
DEV = 192
IMG_GROUP = 30
EPS = 1e-06
MASKED = -1e30
MESH = pl.DeviceIdType.MESH
BF = jnp.bfloat16
F32 = jnp.float32

STEM = 384
LAYER = 2304
ROWS = STEM + NL * LAYER

GATHER_UNITS = [
    (0, 128, 512, 512),
    (1152, 256, 512, 0),
    (1920, 256, 0, 512),
    (2688, 256, 512, 0),
    (3456, 256, 0, 512),
    (4224, 256, 512, 0),
]

GRAD_ROWS = NL * LAYER + 512


def place():
    d = lax.axis_index("dp")
    c = lax.axis_index("ctx")
    t = lax.axis_index("tensor")
    return d // 4, d % 4, c, t


def peer(axis, r):
    z, y, c, t = place()
    if axis == "x":
        return (z * 4 + y, c, (t + r) % 4)
    if axis == "y":
        return (z * 4 + (y + r) % 4, c, t)
    return (((z + r) % 4) * 4 + y, c, t)


def sibling():
    z, y, c, t = place()
    return (z * 4 + y, 1 - c, t)


def greet(stem):
    z, y, c, t = place()
    bar = pltpu.get_barrier_semaphore()
    for axis in "xyz":
        for r in (1, 2, 3):
            pl.semaphore_signal(bar, inc=1, device_id=peer(axis, r), device_id_type=MESH)
    pl.semaphore_signal(bar, inc=1, device_id=sibling(), device_id_type=MESH)
    if stem is None:
        pl.semaphore_wait(bar, 10)
        return

    def hello(i, carry):
        if stem == "in":
            other = (t * 4 + i // 4, c, i % 4)
        else:
            other = (i, c, z)
        me = (z * 4 + y == other[0]) & (t == other[2])

        @pl.when(jnp.logical_not(me))
        def _():
            pl.semaphore_signal(bar, inc=1, device_id=other, device_id_type=MESH)

        return carry

    lax.fori_loop(0, 16, hello, 0)
    own = t == z

    @pl.when(own)
    def _():
        pl.semaphore_wait(bar, 25)

    @pl.when(jnp.logical_not(own))
    def _():
        pl.semaphore_wait(bar, 26)


def remote(src, dst, send, recv, device):
    return pltpu.make_async_remote_copy(
        src_ref=src, dst_ref=dst, send_sem=send, recv_sem=recv, device_id=device, device_id_type=MESH
    )


class Gather:
    def __init__(self, buf, send, recv):
        self.buf, self.send, self.recv = buf, send, recv

    def x_copies(self, unit, sem, row, rows):
        return [
            remote(
                self.buf.at[0, pl.ds(row, rows)],
                self.buf.at[r, pl.ds(row, rows)],
                self.send.at[unit, sem + r - 1],
                self.recv.at[unit, sem + r - 1],
                peer("x", -r),
            )
            for r in (1, 2, 3)
        ]

    def plane_copies(self, unit, sem, device, row, rows):
        region = self.buf.at[pl.ds(1, 3), pl.ds(row, rows)]
        return remote(region, region, self.send.at[unit, sem], self.recv.at[unit, sem], device)

    def stage(self, unit, which):
        first, nx, nyz, nzy = GATHER_UNITS[unit]
        z, y, c, t = place()
        m = lambda v: pl.multiple_of(v, 16)
        out = []
        if which == 0:
            return self.x_copies(unit, 0, m(first + c * (nx // 2)), nx // 2)
        if which == 4:
            parts = [(first, nx), (first + nx, nyz), (first + nx + nyz, nzy)]
            for k, (row, rows) in enumerate(parts):
                if rows:
                    out.append(self.plane_copies(unit, 21 + k, sibling(), m(row + c * (rows // 2)), rows // 2))
            return out
        for sem, slow, fast, row, rows in (
            (3, ("z", z), ("y", y), first + nx, nyz),
            (12, ("y", y), ("z", z), first + nx + nyz, nzy),
        ):
            if not rows:
                continue
            row = row + c * 256 + slow[1] * 64
            if which == 1:
                out += self.x_copies(unit, sem, m(row + fast[1] * 16), 16)
            for r in (1, 2, 3):
                if which == 2:
                    out.append(self.plane_copies(unit, sem + 2 + r, peer(fast[0], -r), m(row + fast[1] * 16), 16))
                if which == 3:
                    out.append(self.plane_copies(unit, sem + 5 + r, peer(slow[0], -r), m(row), 64))
        return out

    def start(self, unit, which):
        for copy in self.stage(unit, which):
            copy.start()

    def arrived(self, unit, which):
        for copy in self.stage(unit, which):
            copy.wait_recv()

    def finish(self, unit):
        for which in range(5):
            for copy in self.stage(unit, which):
                copy.wait_send()


def scatter_patches(stage, out, send, recv, own, mode):
    z, y, c, t = place()
    rows = pl.ds(pl.multiple_of(t * 16, 16), 16)

    def each(i, carry):
        to_me = (z * 4 + y == i) & (t == z)
        local = pltpu.make_async_copy(stage.at[i], out.at[y, rows], own)
        away = remote(stage.at[i], out.at[y, rows], send.at[i], recv.at[y * 4 + t], (i, c, z))

        @pl.when(to_me)
        def _():
            local.start() if mode == "start" else local.wait()

        @pl.when(jnp.logical_not(to_me))
        def _():
            away.start() if mode == "start" else away.wait_send()

        return carry

    def arrive(i, carry):
        from_me = (t == z) & (i // 4 == y) & (i % 4 == t)
        there = pl.ds(pl.multiple_of((i % 4) * 16, 16), 16)

        @pl.when(jnp.logical_not(from_me))
        def _():
            region = out.at[i // 4, there]
            remote(region, region, send.at[i], recv.at[i], (i, c, z)).wait_recv()

        return carry

    lax.fori_loop(0, 16, each, 0)
    if mode == "wait":
        lax.fori_loop(0, 16, arrive, 0)


def dot_nt(a, b):
    return lax.dot_general(a, b, (((1,), (1,)), ((), ())), preferred_element_type=F32)


def dot_tn(a, b):
    return lax.dot_general(a, b, (((0,), (0,)), ((), ())), preferred_element_type=F32)


def dot_nn(a, b):
    return jnp.dot(a, b, preferred_element_type=F32)


def row_blocks(size, body):
    def step(i, carry):
        body(pl.ds(pl.multiple_of(i * size, size), size))
        return carry

    lax.fori_loop(0, HALF // size, step, 0)


def norm_rows(src, gain, shift, dst):
    def body(rows):
        x = src[rows]
        mean = jnp.mean(x, axis=-1, keepdims=True)
        centred = x - mean
        spread = jnp.mean(centred * centred, axis=-1, keepdims=True)
        dst[rows] = (centred * lax.rsqrt(spread + EPS) * gain + shift).astype(BF)

    row_blocks(64, body)


GELU_A = 0.7978845608028654
GELU_B = 0.044715


def gather_kernel(
    patch_w,
    text_w,
    in_w,
    out_w,
    up_w,
    down_w,
    vectors,
    gains,
    stamps_q,
    stamps_k,
    patches,
    words,
    w_out,
    patch_out,
    vec_out,
    xs_out,
    mid_out,
    nrm_out,
    fn_out,
    tri_out,
    kvo_out,
    mix_out,
    lse_out,
    pre_out,
    act_out,
    buf,
    vec,
    gain,
    stamp_q,
    stamp_k,
    pstage,
    prow,
    word,
    xs,
    mid,
    nrm,
    fn,
    tri,
    kvo,
    mix,
    lse,
    pre,
    act,
    bias,
    hid,
    local,
    send,
    recv,
    psend,
    precv,
    own,
    vsend,
    vrecv,
    ksend,
    krecv,
    saved,
):
    z, y, c, t = place()
    early = [
        pltpu.make_async_copy(patches.at[:, pl.ds(pl.multiple_of(t * 16, 16), 16)], pstage, local.at[0]),
        pltpu.make_async_copy(vectors, vec.at[0], local.at[1]),
    ]
    sources = [(patch_w, 0, 192), (text_w, 192, 192)]
    for which in range(NL):
        base = STEM + which * LAYER
        sources += [
            (in_w.at[which], base, 576),
            (out_w.at[which], base + 576, 192),
            (up_w.at[which], base + 768, 768),
            (down_w.at[which], base + 1536, 768),
        ]
    loads = [
        pltpu.make_async_copy(ref, buf.at[0, pl.ds(row, rows)], local.at[2 + k])
        for k, (ref, row, rows) in enumerate(sources)
    ]
    late = [
        pltpu.make_async_copy(words, word, local.at[12]),
        pltpu.make_async_copy(gains, gain, local.at[13]),
        pltpu.make_async_copy(stamps_q, stamp_q, local.at[14]),
        pltpu.make_async_copy(stamps_k, stamp_k, local.at[15]),
    ]
    for copy in early + loads + late:
        copy.start()
    greet("in")
    early[0].wait()
    scatter_patches(pstage, prow, psend, precv, own, "start")
    early[1].wait()
    vec_copies = [
        remote(vec.at[0], vec.at[r], vsend.at[r - 1], vrecv.at[r - 1], peer("x", -r)) for r in (1, 2, 3)
    ]
    for copy in vec_copies:
        copy.start()
    units = [[0, 1, 2, 3], [4], [5], [6, 7], [8], [9]]
    g = Gather(buf, send, recv)
    for unit, members in enumerate(units):
        for k in members:
            loads[k].wait()
        g.start(unit, 1)
    for unit in range(6):
        g.start(unit, 0)
    for unit in range(6):
        g.arrived(unit, 1)
        g.start(unit, 2)
    for unit in range(6):
        g.arrived(unit, 2)
        g.start(unit, 3)
    for copy in late:
        copy.wait()

    lse[...] = jnp.zeros_like(lse)

    def see(i, carry):
        rows = pl.ds(pl.multiple_of(i * 64, 64), 64)
        bias[rows] = jnp.where(stamp_k[rows, 0:1] <= stamp_q[0:1, :], 0.0, MASKED)
        return carry

    lax.fori_loop(0, 8, see, 0)

    scatter_patches(pstage, prow, psend, precv, own, "wait")
    for copy in vec_copies:
        copy.wait()

    saves = []

    def save(k, src, dst):
        copy = pltpu.make_async_copy(src, dst, saved.at[k])
        copy.start()
        saves.append(copy)

    def ready(unit):
        g.arrived(unit, 0)
        g.arrived(unit, 3)
        g.start(unit, 4)
        g.arrived(unit, 4)

    ready(0)
    place_in = lax.broadcasted_iota(jnp.int32, (HALF, 1), 0) % (IMG_GROUP + 2)
    parts = []
    for a in range(4):
        s = (a - t) % 4
        picture = dot_nt(prow[...].reshape(HALF, D), buf[s, 0:192]) + vec[s, 2:3, 0:192]
        language = dot_nt(word[...], buf[s, 192:384]) + vec[s, 3:4, 0:192]
        mark = vec[s, 4:5, 0:192]
        part = jnp.where(place_in < IMG_GROUP, picture, jnp.where(place_in == IMG_GROUP, language, mark))
        parts.append(part.astype(BF).astype(F32))
    xs[0] = jnp.concatenate(parts, axis=1)
    save(0, prow, patch_out)
    save(1, vec, vec_out)

    for which in range(NL):
        base = STEM + which * LAYER
        if which:
            ready(3)
        norm_rows(xs.at[which], gain[which : which + 1], gain[2 + which : 3 + which], nrm.at[which])

        def project(s, carry):
            triple = dot_nt(buf[s, base : base + 576], nrm[which])
            tri[which, s] = triple.astype(BF)
            remote(
                tri.at[which, s, pl.ds(192, 384)],
                kvo.at[which, s],
                ksend.at[which, s],
                krecv.at[which, s],
                sibling(),
            ).start()
            return carry

        lax.fori_loop(0, 4, project, 0)
        mid[which] = xs[which]

        def attend(s, carry):
            remote(
                tri.at[which, s, pl.ds(192, 384)],
                kvo.at[which, s],
                ksend.at[which, s],
                krecv.at[which, s],
                sibling(),
            ).wait_recv()
            for h in range(3):
                at = 64 * h
                q = tri[which, s, at : at + 64] * jnp.asarray(HEAD_DIM**-0.5, BF)
                one = dot_tn(tri[which, s, 192 + at : 256 + at], q) + bias[0:256]
                two = dot_tn(kvo[which, s, at : at + 64], q) + bias[256:512]
                top = jnp.maximum(jnp.max(one, axis=0, keepdims=True), jnp.max(two, axis=0, keepdims=True))
                one = jnp.exp(one - top)
                two = jnp.exp(two - top)
                total = jnp.sum(one, axis=0, keepdims=True) + jnp.sum(two, axis=0, keepdims=True)
                lse[which, s, h : h + 1] = top + jnp.log(total)
                scale = 1.0 / total
                one = (one * scale).astype(BF)
                two = (two * scale).astype(BF)
                mixed = dot_nn(tri[which, s, 384 + at : 448 + at], one)
                mixed = mixed + dot_nn(kvo[which, s, 192 + at : 256 + at], two)
                mix[which, s, at : at + 64] = mixed.astype(BF)
            mid[which] += dot_tn(mix[which, s], buf[s, base + 576 : base + 768])
            return carry

        lax.fori_loop(0, 4, attend, 0)
        norm_rows(mid.at[which], gain[4 + which : 5 + which], gain[6 + which : 7 + which], fn.at[which])
        ready(1 + 3 * which)

        def lift(s, carry):
            pre[which, s] = dot_nn(fn[which], buf[s, base + 768 : base + 1536]) + vec[s, which : which + 1]
            return carry

        lax.fori_loop(0, 4, lift, 0)
        xs[which + 1] = mid[which]
        ready(2 + 3 * which)

        def lower(s, carry):
            def body(rows):
                x = pre[which, s, rows]
                hid[rows] = (0.5 * x * (1.0 + jnp.tanh(GELU_A * (x + GELU_B * x * x * x)))).astype(BF)

            row_blocks(64, body)
            xs[which + 1] += dot_nn(hid[...], buf[s, base + 1536 : base + 2304])
            return carry

        lax.fori_loop(0, 4, lower, 0)
        save(2 + which, pre.at[which], pre_out.at[which])

    save(4, buf, w_out)
    save(5, xs.at[pl.ds(0, 2)], xs_out)
    save(6, mid, mid_out)
    save(7, nrm, nrm_out)
    save(8, fn, fn_out)
    save(9, tri, tri_out)
    save(10, kvo, kvo_out)
    save(11, mix, mix_out)
    save(12, lse, lse_out)
    flipped = xs[2].astype(BF).T
    for a in range(4):
        act[a] = flipped[192 * a : 192 * a + 192]
    save(13, act, act_out)
    for which in range(NL):
        for s in range(4):
            remote(
                tri.at[which, s, pl.ds(192, 384)],
                kvo.at[which, s],
                ksend.at[which, s],
                krecv.at[which, s],
                sibling(),
            ).wait_send()
    for unit in range(6):
        g.finish(unit)
    for copy in saves:
        copy.wait()


def forward_call(*args):
    any_ = pl.BlockSpec(memory_space=pl.ANY)
    sds = jax.ShapeDtypeStruct
    shapes = [
        ((4, ROWS, D), BF),
        ((4, 64, D), BF),
        ((4, 8, D), F32),
        ((2, HALF, D), F32),
        ((2, HALF, D), F32),
        ((2, HALF, D), BF),
        ((2, HALF, D), BF),
        ((2, 4, 576, HALF), BF),
        ((2, 4, 384, HALF), BF),
        ((2, 4, 192, HALF), BF),
        ((2, 4, 8, HALF), F32),
        ((2, 4, HALF, D), F32),
        ((4, 192, HALF), BF),
    ]
    dma = pltpu.SemaphoreType.DMA
    return pl.pallas_call(
        gather_kernel,
        out_shape=tuple(sds(s, d) for s, d in shapes),
        in_specs=[any_] * 12,
        out_specs=(any_,) * len(shapes),
        scratch_shapes=[
            pltpu.VMEM((4, ROWS, D), BF),
            pltpu.VMEM((4, 8, D), F32),
            pltpu.VMEM((8, D), F32),
            pltpu.VMEM((8, HALF), jnp.int32),
            pltpu.VMEM((L, 128), jnp.int32),
            pltpu.VMEM((16, 16, D), BF),
            pltpu.VMEM((4, 64, D), BF),
            pltpu.VMEM((HALF, D), BF),
            pltpu.VMEM((3, HALF, D), F32),
            pltpu.VMEM((2, HALF, D), F32),
            pltpu.VMEM((2, HALF, D), BF),
            pltpu.VMEM((2, HALF, D), BF),
            pltpu.VMEM((2, 4, 576, HALF), BF),
            pltpu.VMEM((2, 4, 384, HALF), BF),
            pltpu.VMEM((2, 4, 192, HALF), BF),
            pltpu.VMEM((2, 4, 8, HALF), F32),
            pltpu.VMEM((2, 4, HALF, D), F32),
            pltpu.VMEM((4, 192, HALF), BF),
            pltpu.VMEM((L, HALF), F32),
            pltpu.VMEM((HALF, D), BF),
            dma((16,)),
            dma((6, 24)),
            dma((6, 24)),
            dma((16,)),
            dma((16,)),
            dma,
            dma((3,)),
            dma((3,)),
            dma((2, 4)),
            dma((2, 4)),
            dma((14,)),
        ],
        compiler_params=pltpu.CompilerParams(
            collective_id=0, has_side_effects=True, vmem_limit_bytes=63 * 2**20
        ),
    )(*args)


def prepare(
    patches,
    text_features,
    patch_weight,
    patch_bias,
    text_weight,
    text_bias,
    readout,
    mix_gain,
    mix_shift,
    heads_in_weight,
    heads_out_weight,
    feed_gain,
    feed_shift,
    up_weight,
    up_bias,
    down_weight,
    timesteps,
):
    t = lax.axis_index("tensor")
    c = lax.axis_index("ctx")
    wide = lambda v: jnp.pad(v.astype(F32), (0, D - DEV))[None]
    vectors = jnp.concatenate(
        [up_bias, wide(patch_bias), wide(text_bias), wide(readout), jnp.zeros((3, D), F32)], axis=0
    )
    gains = jnp.concatenate([mix_gain, mix_shift, feed_gain, feed_shift], axis=0)
    stamps = lax.dynamic_slice_in_dim(timesteps, t, 1, 0).reshape(2, HALF)
    mine = lax.dynamic_slice_in_dim(stamps, c, 1, 0)
    other = lax.dynamic_slice_in_dim(stamps, 1 - c, 1, 0)
    stamps_q = jnp.broadcast_to(mine, (8, HALF))
    stamps_k = jnp.broadcast_to(jnp.concatenate([mine, other], 1).reshape(L, 1), (L, 128))
    spaced = jnp.pad(patches.reshape(16, 2, IMG_GROUP, D), ((0, 0), (0, 0), (0, 2), (0, 0))).reshape(16, 64, D)
    words = lax.dynamic_slice_in_dim(text_features, t, 1, 0).reshape(8, 1, D)
    words = jnp.pad(words, ((0, 0), (IMG_GROUP, 1), (0, 0))).reshape(HALF, D)
    return (
        patch_weight.T,
        text_weight.T,
        heads_in_weight.transpose(0, 2, 3, 1).reshape(NL, 3 * DEV, D),
        heads_out_weight,
        up_weight,
        down_weight,
        vectors,
        gains,
        stamps_q,
        stamps_k,
        spaced,
        words,
    )


SUM_UNITS = [
    (256, 512, "z"),
    (256, 512, "y"),
    (256, 512, "z"),
    (256, 512, "y"),
    (256, 512, "z"),
    (256, 512, "y"),
    (0, 512, "z"),
]
NU = len(SUM_UNITS)
RING = 4
DOWN, UP, ATT, STEMS = 0, 1, 2, 6


class Sums:
    def __init__(self, grads, core_in, xr, pr, yr, qr, zb, tr, xs, ps, qs, fx, fp, out, send, recv, local, credit):
        self.grads, self.core_in = grads, core_in
        self.xr, self.pr, self.yr, self.qr, self.zb, self.tr = xr, pr, yr, qr, zb, tr
        self.xs, self.ps, self.qs, self.fx, self.fp = xs, ps, qs, fx, fp
        self.out, self.send, self.recv, self.local, self.credit = out, send, recv, local, credit

    def where(self, u):
        nx, npl, slow = SUM_UNITS[u]
        z, y, c, t = place()
        m = lambda v: pl.multiple_of(v, 16)
        fast = "y" if slow == "z" else "z"
        at = {"z": z, "y": y}
        return nx, npl, slow, fast, at, c, t, m

    def core(self, u):
        nx, npl, slow, fast, at, c, t, m = self.where(u)
        g, into = self.grads.at[u % 3], self.core_in.at[u % 2]
        out = []
        if nx:
            out.append(
                remote(
                    g.at[:, pl.ds(m((1 - c) * 128), 128)],
                    into.at[:, pl.ds(0, 128)],
                    self.send.at[u, 0],
                    self.recv.at[u, 0],
                    sibling(),
                )
            )
        out.append(
            remote(
                g.at[:, pl.ds(m(nx + (1 - c) * 256), 256)],
                into.at[:, pl.ds(128, 256)],
                self.send.at[u, 1],
                self.recv.at[u, 1],
                sibling(),
            )
        )
        return out

    def first(self, u):
        nx, npl, slow, fast, at, c, t, m = self.where(u)
        g = self.grads.at[u % 3]
        out = []
        for r in (1, 2, 3):
            if nx:
                out.append(
                    remote(
                        g.at[r, pl.ds(m(c * 128), 128)],
                        self.xr.at[u % RING, r - 1],
                        self.send.at[u, 1 + r],
                        self.recv.at[u, 1 + r],
                        peer("x", r),
                    )
                )
            block = (at[slow] + r) % 4
            out.append(
                remote(
                    g.at[:, pl.ds(m(nx + c * 256 + block * 64), 64)],
                    self.pr.at[u % RING, r - 1],
                    self.send.at[u, 4 + r],
                    self.recv.at[u, 4 + r],
                    peer(slow, r),
                )
            )
        return out

    def second(self, u):
        nx, npl, slow, fast, at, c, t, m = self.where(u)
        out = []
        for r in (1, 2, 3):
            if nx:
                block = (at["y"] + r) % 4
                out.append(
                    remote(
                        self.xs.at[u % 3, pl.ds(m(block * 32), 32)],
                        self.yr.at[u % RING, r - 1],
                        self.send.at[u, 7 + r],
                        self.recv.at[u, 7 + r],
                        peer("y", r),
                    )
                )
            block = (at[fast] + r) % 4
            out.append(
                remote(
                    self.ps.at[u % 3, :, pl.ds(m(block * 16), 16)],
                    self.qr.at[u % RING, r - 1],
                    self.send.at[u, 10 + r],
                    self.recv.at[u, 10 + r],
                    peer(fast, r),
                )
            )
        return out

    def third(self, u):
        nx, npl, slow, fast, at, c, t, m = self.where(u)
        out = []
        for r in (1, 2, 3):
            if nx:
                mine = self.zb.at[u % RING, at["z"]]
                out.append(remote(mine, mine, self.send.at[u, 13 + r], self.recv.at[u, 13 + r], peer("z", r)))
            out.append(
                remote(
                    self.qs.at[u % 3, r],
                    self.tr.at[u, r - 1],
                    self.send.at[u, 16 + r],
                    self.recv.at[u, 16 + r],
                    peer("x", r),
                )
            )
        return out

    def rows(self, u):
        nx, npl, slow, fast, at, c, t, m = self.where(u)
        base = u * D
        return (
            pl.ds(m(base + c * 128), 128),
            pl.ds(m(base + c * 128 + at["y"] * 32), 32),
            pl.ds(m(base + nx + c * 256), 256),
            pl.ds(m(base + nx + c * 256 + at[slow] * 64), 64),
            pl.ds(m(base + nx + c * 256 + at[slow] * 64 + at[fast] * 16), 16),
        )

    def fourth(self, u):
        nx, npl, slow, fast, at, c, t, m = self.where(u)
        _, x_own, _, _, p_own = self.rows(u)
        out = []
        for r in (1, 2, 3):
            if nx:
                out.append(
                    remote(
                        self.fx.at[u],
                        self.out.at[x_own],
                        self.send.at[u, 19 + r],
                        self.recv.at[u, 19 + r],
                        peer("y", r),
                    )
                )
            out.append(
                remote(
                    self.fp.at[u],
                    self.out.at[p_own],
                    self.send.at[u, 22 + r],
                    self.recv.at[u, 22 + r],
                    peer(fast, r),
                )
            )
        return out

    def own(self, u):
        nx = SUM_UNITS[u][0]
        _, x_own, _, _, p_own = self.rows(u)
        out = [pltpu.make_async_copy(self.fp.at[u], self.out.at[p_own], self.local.at[u, 0])]
        if nx:
            out.append(pltpu.make_async_copy(self.fx.at[u], self.out.at[x_own], self.local.at[u, 1]))
        return out

    def fifth(self, u):
        nx, npl, slow, fast, at, c, t, m = self.where(u)
        region = self.out.at[self.rows(u)[3]]
        return [
            remote(region, region, self.send.at[u, 25 + r], self.recv.at[u, 25 + r], peer(slow, r))
            for r in (1, 2, 3)
        ]

    def sixth(self, u):
        nx = SUM_UNITS[u][0]
        x_all, _, p_all, _, _ = self.rows(u)
        region = self.out.at[p_all]
        out = [remote(region, region, self.send.at[u, 29], self.recv.at[u, 29], sibling())]
        if nx:
            region = self.out.at[x_all]
            out.append(remote(region, region, self.send.at[u, 30], self.recv.at[u, 30], sibling()))
        return out

    def step(self, k, u):
        nx, npl, slow, fast, at, c, t, m = self.where(u)
        b, ring, rot = u % 3, u % RING, u % 3
        grads = self.grads
        if k == 0:
            if u >= 2:
                pl.semaphore_wait(self.credit, 1)
            for copy in self.core(u):
                copy.start()
        if k == 1:
            for copy in self.core(u):
                copy.wait_recv()
            parts = ([(0, 0, 128)] if nx else []) + [(nx, 128, 256)]
            for first, there, count in parts:

                def add(i, carry):
                    s = i // (count // 64)
                    o = (i % (count // 64)) * 64
                    mine = pl.ds(m(first + c * count + o), 64)
                    its = pl.ds(m(there + o), 64)
                    total = grads[b, s, mine].astype(F32) + self.core_in[u % 2, s, its].astype(F32)
                    grads[b, s, mine] = total.astype(BF)
                    return carry

                lax.fori_loop(0, 4 * (count // 64), add, 0)
            if u + 2 < NU:
                pl.semaphore_signal(self.credit, inc=1, device_id=sibling(), device_id_type=MESH)
            for copy in self.first(u):
                copy.start()
        if k == 2:
            for copy in self.first(u):
                copy.wait_recv()
            if nx:

                def addx(i, carry):
                    o = pl.ds(m(i * 32), 32)
                    total = grads[b, 0, pl.ds(m(c * 128 + i * 32), 32)].astype(F32)
                    for r in range(3):
                        total = total + self.xr[ring, r, o].astype(F32)
                    self.xs[rot, o] = total.astype(BF)
                    return carry

                lax.fori_loop(0, 4, addx, 0)

            def addp(i, carry):
                s = i // 2
                o = pl.ds(m((i % 2) * 32), 32)
                row = nx + c * 256 + at[slow] * 64 + (i % 2) * 32
                total = grads[b, s, pl.ds(m(row), 32)].astype(F32)
                for r in range(3):
                    total = total + self.pr[ring, r, s, o].astype(F32)
                self.ps[rot, s, o] = total.astype(BF)
                return carry

            lax.fori_loop(0, 8, addp, 0)
            for copy in self.core(u) + self.first(u):
                copy.wait_send()
            for copy in self.second(u):
                copy.start()
        if k == 3:
            for copy in self.second(u):
                copy.wait_recv()
            if nx:
                total = self.xs[rot, pl.ds(m(at["y"] * 32), 32)].astype(F32)
                for r in range(3):
                    total = total + self.yr[ring, r].astype(F32)
                self.zb[ring, at["z"]] = total.astype(BF)

            def addq(s, carry):
                total = self.ps[rot, s, pl.ds(m(at[fast] * 16), 16)].astype(F32)
                for r in range(3):
                    total = total + self.qr[ring, r, s].astype(F32)
                self.qs[rot, s] = total.astype(BF)
                return carry

            lax.fori_loop(0, 4, addq, 0)
            for copy in self.second(u):
                copy.wait_send()
            for copy in self.third(u):
                copy.start()
        if k == 4:
            for copy in self.third(u):
                copy.wait_recv()
            if nx:
                total = self.zb[ring, 0].astype(F32)
                for r in (1, 2, 3):
                    total = total + self.zb[ring, r].astype(F32)
                self.fx[u] = total.astype(BF)
            total = self.qs[rot, 0].astype(F32)
            for r in range(3):
                total = total + self.tr[u, r].astype(F32)
            self.fp[u] = total.astype(BF)
            for copy in self.third(u):
                copy.wait_send()
            for copy in self.own(u) + self.fourth(u):
                copy.start()
        if k == 5:
            for copy in self.fourth(u):
                copy.wait_recv()
            for copy in self.own(u):
                copy.wait()
            for copy in self.fifth(u):
                copy.start()
        if k == 6:
            for copy in self.fifth(u):
                copy.wait_recv()
            for copy in self.sixth(u):
                copy.start()
        if k == 7:
            for copy in self.sixth(u):
                copy.wait_recv()
            for copy in self.fourth(u) + self.fifth(u) + self.sixth(u):
                copy.wait_send()


def norm_back(x, grad, base, gain, out, sums, gain_row, shift_row):
    zero = jnp.zeros((1, D), F32)
    sums[gain_row : gain_row + 1] = zero
    sums[shift_row : shift_row + 1] = zero

    def body(rows):
        v = x[rows]
        g = grad[rows]
        mean = jnp.mean(v, axis=-1, keepdims=True)
        centred = v - mean
        spread = jnp.mean(centred * centred, axis=-1, keepdims=True)
        inv = lax.rsqrt(spread + EPS)
        hat = centred * inv
        sums[gain_row : gain_row + 1] += jnp.sum(g * hat, axis=0, keepdims=True)
        sums[shift_row : shift_row + 1] += jnp.sum(g, axis=0, keepdims=True)
        d = g * gain
        first = jnp.mean(d, axis=-1, keepdims=True)
        second = jnp.mean(d * hat, axis=-1, keepdims=True)
        out[rows] = base[rows] + inv * (d - first - hat * second)

    row_blocks(32, body)


def returns(act, act_out, pgs, pg_out, tgs, tg_out, send, recv, own, mode, which):
    z, y, c, t = place()
    d = z * 4 + y
    if which == 0:
        for r in (1, 2, 3):
            a = (t + r) % 4
            copy = remote(act.at[a], act_out.at[t], send.at[r], recv.at[r], (d, c, a))
            copy.start() if mode == "start" else copy.wait()
        copy = pltpu.make_async_copy(act.at[t], act_out.at[t], own.at[0])
        copy.start() if mode == "start" else copy.wait()
        return
    for r in (1, 2, 3):
        a = (t + r) % 4
        copy = remote(tgs.at[a], tg_out.at[t], send.at[4 + r], recv.at[4 + r], (d, c, a))
        copy.start() if mode == "start" else copy.wait()
    copy = pltpu.make_async_copy(tgs.at[t], tg_out.at[t], own.at[1])
    copy.start() if mode == "start" else copy.wait()

    def each(i, carry):
        a, yy = i % 4, i // 4
        to_me = (t == z) & (yy == y) & (a == t)
        src = pgs.at[a, pl.ds(pl.multiple_of(yy * 64, 64), 64)]
        local = pltpu.make_async_copy(src, pg_out.at[d], own.at[2])
        away = remote(src, pg_out.at[d], send.at[8 + i], recv.at[8 + d], (t * 4 + yy, c, a))

        @pl.when(to_me)
        def _():
            local.start() if mode == "start" else local.wait()

        @pl.when(jnp.logical_not(to_me))
        def _():
            away.start() if mode == "start" else away.wait_send()

        return carry

    lax.fori_loop(0, 16, each, 0)
    if mode == "wait":

        def arrive(i, carry):
            from_me = (t == z) & (i == d)

            @pl.when(jnp.logical_not(from_me))
            def _():
                remote(pg_out.at[i], pg_out.at[i], send.at[8 + i], recv.at[8 + i], (i, c, z)).wait_recv()

            return carry

        lax.fori_loop(0, 16, arrive, 0)


def backward_kernel(
    w_in,
    patch_in,
    xs_in,
    mid_in,
    nrm_in,
    fn_in,
    tri_in,
    kvo_in,
    mix_in,
    lse_in,
    pre_in,
    act_in,
    gains,
    stamps_q,
    stamps_k,
    words,
    cotangent,
    row_scale,
    out,
    act_out,
    pg_out,
    tg_out,
    wb,
    gain,
    stamp_q,
    stamp_k,
    prow,
    word,
    cot,
    rscale,
    xs,
    mid,
    nrm,
    fn,
    tri,
    kvo,
    mix,
    lse,
    pre,
    bias,
    up,
    low,
    back,
    hgrad,
    hid,
    pgrad,
    fnt,
    kvg,
    kvs,
    rkv,
    tgrad,
    sums,
    vec,
    pgs,
    tgs,
    grads,
    core_in,
    xr,
    pr,
    yr,
    qr,
    zb,
    tr,
    sxs,
    sps,
    sqs,
    fx,
    fp,
    wsem,
    lsem,
    send,
    recv,
    local,
    credit,
    ksend,
    krecv,
    rsend,
    rrecv,
    rown,
):
    z, y, c, t = place()
    copy_in = pltpu.make_async_copy

    def section(row, rows, s):
        return copy_in(w_in.at[s, pl.ds(row, rows)], wb.at[s, pl.ds(0, rows)], wsem.at[s])

    sections = []
    for which in (1, 0):
        base = STEM + which * LAYER
        sections += [(base + 1536, 768), (base + 768, 768), (base, 768)]
    sections.append((0, STEM))

    def acts(which):
        return [
            copy_in(pre_in.at[which], pre, lsem.at[0]),
            copy_in(fn_in.at[which], fn, lsem.at[1]),
            copy_in(mid_in.at[which], mid, lsem.at[2]),
            copy_in(tri_in.at[which], tri, lsem.at[3]),
            copy_in(kvo_in.at[which], kvo, lsem.at[4]),
            copy_in(mix_in.at[which], mix, lsem.at[5]),
            copy_in(lse_in.at[which], lse, lsem.at[6]),
            copy_in(nrm_in.at[which], nrm, lsem.at[7]),
            copy_in(xs_in.at[which], xs, lsem.at[8]),
        ]

    head = [
        copy_in(cotangent.at[t], cot, lsem.at[9]),
        copy_in(row_scale, rscale, lsem.at[10]),
    ]
    for copy in head:
        copy.start()
    for s in range(4):
        section(*sections[0], s).start()
    loads = acts(1)
    for copy in loads:
        copy.start()
    rest = [
        copy_in(gains, gain, lsem.at[11]),
        copy_in(stamps_q, stamp_q, lsem.at[12]),
        copy_in(stamps_k, stamp_k, lsem.at[13]),
        copy_in(patch_in, prow, lsem.at[14]),
        copy_in(words, word, lsem.at[15]),
    ]
    for copy in rest:
        copy.start()
    greet("out")
    returns(act_in, act_out, pgs, pg_out, tgs, tg_out, rsend, rrecv, rown, "start", 0)
    total = Sums(
        grads, core_in, xr, pr, yr, qr, zb, tr, sxs, sps, sqs, fx, fp, out, send, recv, local, credit
    )

    def comm(*steps):
        for k, u in steps:
            total.step(k, u)

    for copy in head:
        copy.wait()

    def first_up(rows):
        up[rows] = cot[rows].astype(F32) * rscale[rows, 0:1]

    row_blocks(64, first_up)
    vec[...] = jnp.zeros_like(vec)
    sums[...] = jnp.zeros_like(sums)
    for copy in rest:
        copy.wait()

    def see(i, carry):
        rows = pl.ds(pl.multiple_of(i * 64, 64), 64)
        bias[rows] = jnp.where(stamp_k[rows, 0:1] <= stamp_q[0:1, :], 0.0, MASKED)
        return carry

    lax.fori_loop(0, 8, see, 0)

    plan = {
        (1, "down"): [(0, 0)],
        (1, "up"): [(1, 0), (0, 1)],
        (1, "att1"): [(1, 1)],
        (1, "att2"): [(2, 0)],
        (1, "in"): [(0, 2), (2, 1), (3, 0)],
        (0, "down"): [(0, 3), (1, 2), (3, 1), (4, 0)],
        (0, "up"): [(2, 2), (0, 4), (1, 3), (4, 1), (5, 0)],
        (0, "att1"): [(6, 0), (1, 4), (2, 3), (3, 2), (5, 1)],
        (0, "att2"): [(6, 1), (4, 2), (3, 3)],
        (0, "in"): [(0, 5), (2, 4), (1, 5), (5, 2)],
    }
    for which in (1, 0):
        u0 = 0 if which else 3
        loads = acts(which)
        loads[0].wait()

        def round_up(rows):
            low[rows] = up[rows].astype(BF)

        row_blocks(64, round_up)
        b = u0 % 3
        after = sections[u0 + 1]

        def down(s, carry):
            section(*sections[u0], s).wait()
            hgrad[...] = dot_nt(low[...], wb[s])
            section(*after, s).start()

            def body(rows):
                x = pre[s, rows]
                th = jnp.tanh(GELU_A * (x + GELU_B * x * x * x))
                hid[rows] = (0.5 * x * (1.0 + th)).astype(BF)
                slope = 0.5 * (1.0 + th) + 0.5 * x * (1.0 - th * th) * (GELU_A * (1.0 + 3.0 * GELU_B * x * x))
                pgrad[s, rows] = (hgrad[rows] * slope).astype(BF)

            row_blocks(32, body)
            for j in range(3):
                grads[b, s, 256 * j : 256 * j + 256] = dot_tn(hid[:, 256 * j : 256 * j + 256], low[...]).astype(BF)
            vec[s, which : which + 1] = jnp.sum(pgrad[s].astype(F32), axis=0, keepdims=True)
            return carry

        lax.fori_loop(0, 4, down, 0)
        if which:
            acts(0)[0].start()
        comm(*plan[which, "down"])

        b = (u0 + 1) % 3
        after = sections[u0 + 2]
        loads[1].wait()
        fnt[...] = fn[...].T
        back[...] = jnp.zeros_like(back)

        def lift(s, carry):
            section(*sections[u0 + 1], s).wait()
            back[...] += dot_nt(pgrad[s], wb[s])
            section(*after, s).start()
            for j in range(3):
                grads[b, s, 256 * j : 256 * j + 256] = dot_nn(fnt[256 * j : 256 * j + 256], pgrad[s]).astype(BF)
            return carry

        lax.fori_loop(0, 4, lift, 0)
        if which:
            acts(0)[1].start()
        comm(*plan[which, "up"])

        loads[2].wait()
        norm_back(mid, back, up, gain[4 + which : 5 + which], up, sums, 6 + which, 8 + which)
        if which:
            acts(0)[2].start()
        row_blocks(64, round_up)
        for k in (3, 4, 5, 6):
            loads[k].wait()
        b = (u0 + 2) % 3
        after = sections[u0 + 3]

        def share(s):
            return remote(kvs.at[which, s], rkv.at[which, s], ksend.at[which, s], krecv.at[which, s], sibling())

        def attend(s, carry):
            section(*sections[u0 + 2], s).wait()
            grads[b, s, 576:768] = dot_nn(mix[s], low[...]).astype(BF)
            mixed = dot_nt(wb[s, 576:768], low[...]).astype(BF)
            for h in range(3):
                at = 64 * h
                q = tri[s, at : at + 64] * jnp.asarray(HEAD_DIM**-0.5, BF)
                do = mixed[at : at + 64]
                k1, v1 = tri[s, 192 + at : 256 + at], tri[s, 384 + at : 448 + at]
                k2, v2 = kvo[s, at : at + 64], kvo[s, 192 + at : 256 + at]
                log_total = lse[s, h : h + 1]
                p1 = jnp.exp(dot_tn(k1, q) + bias[0:256] - log_total)
                p2 = jnp.exp(dot_tn(k2, q) + bias[256:512] - log_total)
                d1 = dot_tn(v1, do)
                d2 = dot_tn(v2, do)
                delta = jnp.sum(p1 * d1, axis=0, keepdims=True) + jnp.sum(p2 * d2, axis=0, keepdims=True)
                g1 = (p1 * (d1 - delta)).astype(BF)
                g2 = (p2 * (d2 - delta)).astype(BF)
                dq = (dot_nn(k1, g1) + dot_nn(k2, g2)) * HEAD_DIM**-0.5
                tgrad[s, at : at + 64] = dq.astype(BF)
                kvg[s, at : at + 64] = dot_nt(q, g1)
                kvs[which, s, at : at + 64] = dot_nt(q, g2).astype(BF)
                kvg[s, 192 + at : 256 + at] = dot_nt(do, p1.astype(BF))
                kvs[which, s, 192 + at : 256 + at] = dot_nt(do, p2.astype(BF)).astype(BF)
            share(s).start()
            return carry

        lax.fori_loop(0, 2, attend, 0)
        comm(*plan[which, "att1"])
        lax.fori_loop(2, 4, attend, 0)
        if which:
            for k in (3, 4, 5, 6):
                acts(0)[k].start()
        comm(*plan[which, "att2"])
        loads[7].wait()
        back[...] = jnp.zeros_like(back)

        def lead(s, carry):
            share(s).wait_recv()
            tgrad[s, 192:576] = (kvg[s] + rkv[which, s].astype(F32)).astype(BF)
            grads[b, s, 0:576] = dot_nn(tgrad[s], nrm[...]).astype(BF)
            back[...] += dot_tn(tgrad[s], wb[s, 0:576])
            section(*after, s).start()
            return carry

        lax.fori_loop(0, 4, lead, 0)
        if which:
            acts(0)[7].start()
        comm(*plan[which, "in"])
        loads[8].wait()
        norm_back(xs, back, up, gain[which : which + 1], up, sums, 2 + which, 4 + which)
        if which:
            acts(0)[8].start()

    row_blocks(64, round_up)
    place_in = lax.broadcasted_iota(jnp.int32, (HALF, 1), 0) % (IMG_GROUP + 2)
    rounded = low[...].astype(F32)
    sums[10:11] = jnp.sum(jnp.where(place_in < IMG_GROUP, rounded, 0.0), axis=0, keepdims=True)
    sums[11:12] = jnp.sum(jnp.where(place_in == IMG_GROUP, rounded, 0.0), axis=0, keepdims=True)
    sums[12:13] = jnp.sum(jnp.where(place_in > IMG_GROUP, up[...], 0.0), axis=0, keepdims=True)
    fnt[...] = low[...].T
    b = STEMS % 3
    back[...] = jnp.zeros_like(back)
    hgrad[...] = jnp.zeros_like(hgrad)
    for a in range(4):
        s = (a - t) % 4
        section(*sections[6], s).wait()
        mine = fnt[192 * a : 192 * a + 192]
        grads[b, s, 0:192] = dot_nn(mine, prow[...].reshape(HALF, D)).astype(BF)
        grads[b, s, 192:384] = dot_nn(mine, word[...]).astype(BF)
        vec[s, 2:16] = sums[2:16]
        grads[b, s, 384:400] = vec[s].astype(BF)
        grads[b, s, 400:512] = jnp.zeros((112, D), BF)
        back[...] += dot_tn(mine, wb[s, 0:192])
        hgrad[...] += dot_tn(mine, wb[s, 192:384])
    comm((0, 6))
    for a in range(4):
        pgs[a] = back[:, 192 * a : 192 * a + 192].astype(BF)
    for h in range(8):
        row = hgrad[32 * h + 30 : 32 * h + 31]
        for a in range(4):
            tgs[a, h : h + 1] = row[:, 192 * a : 192 * a + 192]
    returns(act_in, act_out, pgs, pg_out, tgs, tg_out, rsend, rrecv, rown, "start", 1)
    comm((6, 2), (4, 3), (3, 4), (2, 5), (1, 6), (5, 3), (4, 4), (3, 5), (2, 6), (6, 3), (5, 4), (4, 5), (3, 6))
    comm((6, 4), (5, 5), (4, 6), (6, 5), (5, 6), (6, 6))
    returns(act_in, act_out, pgs, pg_out, tgs, tg_out, rsend, rrecv, rown, "wait", 0)
    returns(act_in, act_out, pgs, pg_out, tgs, tg_out, rsend, rrecv, rown, "wait", 1)
    for which in range(NL):
        for s in range(4):
            remote(kvs.at[which, s], rkv.at[which, s], ksend.at[which, s], krecv.at[which, s], sibling()).wait_send()
    for u in range(NU):
        total.step(7, u)


def backward_call(*args):
    any_ = pl.BlockSpec(memory_space=pl.ANY)
    sds = jax.ShapeDtypeStruct
    dma = pltpu.SemaphoreType.DMA
    v = pltpu.VMEM
    return pl.pallas_call(
        backward_kernel,
        out_shape=(
            sds((6 * D + 512, D), BF),
            sds((4, 192, HALF), BF),
            sds((16, 64, 192), BF),
            sds((4, 8, 192), F32),
        ),
        in_specs=[any_] * 18,
        out_specs=(any_,) * 4,
        scratch_shapes=[
            v((4, D, D), BF),
            v((8, D), F32),
            v((8, HALF), jnp.int32),
            v((L, 128), jnp.int32),
            v((4, 64, D), BF),
            v((HALF, D), BF),
            v((HALF, D), BF),
            v((HALF, 128), F32),
            v((HALF, D), F32),
            v((HALF, D), F32),
            v((HALF, D), BF),
            v((HALF, D), BF),
            v((4, 576, HALF), BF),
            v((4, 384, HALF), BF),
            v((4, 192, HALF), BF),
            v((4, 8, HALF), F32),
            v((4, HALF, D), F32),
            v((L, HALF), F32),
            v((HALF, D), F32),
            v((HALF, D), BF),
            v((HALF, D), F32),
            v((HALF, D), F32),
            v((HALF, D), BF),
            v((4, HALF, D), BF),
            v((D, HALF), BF),
            v((4, 384, HALF), F32),
            v((2, 4, 384, HALF), BF),
            v((2, 4, 384, HALF), BF),
            v((4, 576, HALF), BF),
            v((16, D), F32),
            v((4, 16, D), F32),
            v((4, HALF, DEV), BF),
            v((4, 8, DEV), F32),
            v((3, 4, D, D), BF),
            v((2, 4, 384, D), BF),
            v((RING, 3, 128, D), BF),
            v((RING, 3, 4, 64, D), BF),
            v((RING, 3, 32, D), BF),
            v((RING, 3, 4, 16, D), BF),
            v((RING, 4, 32, D), BF),
            v((NU, 3, 16, D), BF),
            v((3, 128, D), BF),
            v((3, 4, 64, D), BF),
            v((3, 4, 16, D), BF),
            v((NU, 32, D), BF),
            v((NU, 16, D), BF),
            dma((4,)),
            dma((16,)),
            dma((NU, 31)),
            dma((NU, 31)),
            dma((NU, 2)),
            pltpu.SemaphoreType.REGULAR,
            dma((2, 4)),
            dma((2, 4)),
            dma((24,)),
            dma((24,)),
            dma((3,)),
        ],
        compiler_params=pltpu.CompilerParams(
            collective_id=1, has_side_effects=True, vmem_limit_bytes=63 * 2**20
        ),
    )(*args)


def shards(*args):
    (datasets, dataset_weights, action_mask, cotangent) = args[17:]
    t = lax.axis_index("tensor")
    ops = prepare(*args[:17])
    gains, stamps_q, stamps_k, words = ops[7], ops[8], ops[9], ops[11]
    kept = forward_call(*ops)
    mask = lax.dynamic_slice_in_dim(action_mask, t, 1, 0)[0]
    dataset = lax.dynamic_slice_in_dim(datasets, t, 1, 0)[0]
    weight = jnp.sum(jnp.where(jnp.arange(dataset_weights.shape[0]) == dataset, dataset_weights, 0))
    scale = weight.astype(F32) * mask.astype(F32)
    last = jnp.arange(IMG_GROUP + 2) == IMG_GROUP + 1
    row_scale = jnp.where(last[None, :], scale[:, None], 1.0).reshape(HALF, 1)
    row_scale = jnp.broadcast_to(row_scale, (HALF, 128))
    out, act, pg, tg = backward_call(
        kept[0], kept[1], *kept[3:], gains, stamps_q, stamps_k, words, cotangent, row_scale
    )
    part = lambda u, a, b: out[u * D + a : u * D + b].astype(F32)
    heads_in = jnp.stack([part(5, 0, 576), part(2, 0, 576)]).reshape(NL, 3, DEV, D).transpose(0, 3, 1, 2)
    heads_out = jnp.stack([part(5, 576, 768), part(2, 576, 768)])
    up_grad = jnp.stack([part(4, 0, 768), part(1, 0, 768)])
    down_grad = jnp.stack([part(3, 0, 768), part(0, 0, 768)])
    vectors = part(6, 384, 400)
    own = lax.dynamic_slice_in_dim(vectors, t * DEV, DEV, 1)
    pg = pg.reshape(16, 2, IMG_GROUP + 2, DEV)[:, :, :IMG_GROUP].reshape(960, DEV).astype(F32)
    return (
        act.transpose(0, 2, 1),
        pg,
        tg,
        part(6, 0, 192).T,
        own[10],
        part(6, 192, 384).T,
        own[11],
        own[12],
        own[2:4],
        own[4:6],
        heads_in,
        heads_out,
        own[6:8],
        own[8:10],
        up_grad,
        vectors[0:2],
        down_grad,
    )


def solution(mesh):
    in_specs = (
        P(("dp", "ctx"), None),
        P("dp", "ctx", None),
        P(None, "tensor"),
        P("tensor"),
        P(None, "tensor"),
        P("tensor"),
        P("tensor"),
        P(),
        P(),
        P(None, None, None, "tensor"),
        P(None, "tensor", None),
        P(),
        P(),
        P(None, None, "tensor"),
        P(None, "tensor"),
        P(None, "tensor", None),
        P("dp", None),
        P("dp"),
        P(),
        P("dp", "ctx"),
        P("dp", "ctx", None),
    )
    out_specs = (
        P("dp", "ctx", "tensor"),
        P(("dp", "ctx"), "tensor"),
        P("dp", "ctx", "tensor"),
        P(None, "tensor"),
        P("tensor"),
        P(None, "tensor"),
        P("tensor"),
        P("tensor"),
        P(None, "tensor"),
        P(None, "tensor"),
        P(None, None, None, "tensor"),
        P(None, "tensor", None),
        P(None, "tensor"),
        P(None, "tensor"),
        P(None, None, "tensor"),
        P(None, "tensor"),
        P(None, "tensor", None),
    )
    return jax.shard_map(shards, mesh=mesh, in_specs=in_specs, out_specs=out_specs, check_vma=False)
```

```python
import jax
import jax.numpy as jnp
from jax import lax
from jax.experimental import pallas as pl
from jax.experimental.pallas import tpu as pltpu
from jax.sharding import PartitionSpec as P

HEAD_DIM = 64
HEADS = 12
NL = 2
L = 512
HALF = 256
D = 768
DEV = 192
IMG_GROUP = 30
EPS = 1e-06
MASKED = -1e30
MESH = pl.DeviceIdType.MESH
BF = jnp.bfloat16
F32 = jnp.float32

STEM = 384
LAYER = 2304
ROWS = STEM + NL * LAYER

GATHER_UNITS = [
    (0, 128, 512, 512),
    (1152, 256, 512, 0),
    (1920, 256, 0, 512),
    (2688, 256, 512, 0),
    (3456, 256, 0, 512),
    (4224, 256, 512, 0),
]

PIECES = [(0, 0), (0, 1), (1, 0), (2, 1), (3, 0), (4, 1), (5, 0)]

GRAD_ROWS = NL * LAYER + 512


def place():
    d = lax.axis_index("dp")
    c = lax.axis_index("ctx")
    t = lax.axis_index("tensor")
    return d // 4, d % 4, c, t


def peer(axis, r):
    z, y, c, t = place()
    if axis == "x":
        return (z * 4 + y, c, (t + r) % 4)
    if axis == "y":
        return (z * 4 + (y + r) % 4, c, t)
    return (((z + r) % 4) * 4 + y, c, t)


def sibling():
    z, y, c, t = place()
    return (z * 4 + y, 1 - c, t)


def greet(stem):
    z, y, c, t = place()
    bar = pltpu.get_barrier_semaphore()
    for axis in "xyz":
        for r in (1, 2, 3):
            pl.semaphore_signal(bar, inc=1, device_id=peer(axis, r), device_id_type=MESH)
    pl.semaphore_signal(bar, inc=1, device_id=sibling(), device_id_type=MESH)
    count = 4 if stem == "in" else 16

    def hello(i, carry):
        if stem == "in":
            other = (t * 4 + i, c, z)
        else:
            other = (i, c, z)
        me = (z * 4 + y == other[0]) & (t == other[2])

        @pl.when(jnp.logical_not(me))
        def _():
            pl.semaphore_signal(bar, inc=1, device_id=other, device_id_type=MESH)

        return carry

    lax.fori_loop(0, count, hello, 0)
    own = t == z

    @pl.when(own)
    def _():
        pl.semaphore_wait(bar, 9 + count)

    @pl.when(jnp.logical_not(own))
    def _():
        pl.semaphore_wait(bar, 10 + count)


def remote(src, dst, send, recv, device):
    return pltpu.make_async_remote_copy(
        src_ref=src, dst_ref=dst, send_sem=send, recv_sem=recv, device_id=device, device_id_type=MESH
    )


class Gather:
    def __init__(self, buf, pieces, send, recv):
        self.buf, self.pieces, self.send, self.recv = buf, pieces, send, recv

    def copy(self, unit, sem, src, dst, device):
        return remote(src, dst, self.send.at[unit, sem], self.recv.at[unit, sem], device)

    def planes(self, unit):
        first, nx, nyz, nzy = GATHER_UNITS[unit]
        z, y, c, t = place()
        out = []
        if nyz:
            out.append((4, "z", z, "y", y, first + nx + c * 256, PIECES.index((unit, 0))))
        if nzy:
            out.append((14, "y", y, "z", z, first + nx + nyz + c * 256, PIECES.index((unit, 1))))
        return out

    def stage(self, unit, which):
        first, nx, nyz, nzy = GATHER_UNITS[unit]
        z, y, c, t = place()
        m = lambda v: pl.multiple_of(v, 16)
        buf = self.buf
        n = nx // 2
        row = first + c * n
        out = []
        if which == 0:
            rows = pl.ds(m(row), n)
            out.append(self.copy(unit, 0, buf.at[0, rows], buf.at[1, rows], peer("x", -1)))
            out.append(self.copy(unit, 1, buf.at[0, rows], buf.at[3, rows], peer("x", 1)))
        if which == 4:
            rows = pl.ds(m(row), n // 2)
            out.append(self.copy(unit, 2, buf.at[1, rows], buf.at[2, rows], peer("x", -1)))
            rows = pl.ds(m(row + n // 2), n // 2)
            out.append(self.copy(unit, 3, buf.at[3, rows], buf.at[2, rows], peer("x", 1)))
        if which == 5:
            for k, (at, rows) in enumerate([(first, nx), (first + nx, nyz), (first + nx + nyz, nzy)]):
                if rows:
                    region = buf.at[pl.ds(1, 3), pl.ds(m(at + c * (rows // 2)), rows // 2)]
                    out.append(self.copy(unit, 24 + k, region, region, sibling()))
        for sem, slow, p, fast, q, row, k in self.planes(unit):
            block = lambda p, o, rows: buf.at[pl.ds(1, 3), pl.ds(m(row + p * 64 + o), rows)]
            if which == 1:
                rows = pl.ds(m(row + p * 64 + q * 16), 16)
                for r in (1, 2, 3):
                    out.append(self.copy(unit, sem + r - 1, self.pieces.at[k], buf.at[r, rows], peer("x", -r)))
            if which == 2:
                region = block(p, q * 16, 16)
                for r in (1, 2, 3):
                    out.append(self.copy(unit, sem + 2 + r, region, region, peer(fast, -r)))
            if which == 3:
                region = block(p, 0, 64)
                out.append(self.copy(unit, sem + 6, region, region, peer(slow, -1)))
                out.append(self.copy(unit, sem + 7, region, region, peer(slow, 1)))
            if which == 4:
                region = block((p + 1) % 4, 0, 32)
                out.append(self.copy(unit, sem + 8, region, region, peer(slow, -1)))
                region = block((p + 3) % 4, 32, 32)
                out.append(self.copy(unit, sem + 9, region, region, peer(slow, 1)))
        return out

    def start(self, unit, which):
        for copy in self.stage(unit, which):
            copy.start()

    def arrived(self, unit, which):
        for copy in self.stage(unit, which):
            copy.wait_recv()

    def finish(self, unit):
        for which in range(6):
            for copy in self.stage(unit, which):
                copy.wait_send()


def scatter_patches(stage, out, send, recv, own, mode):
    z, y, c, t = place()

    def each(i, carry):
        me = (t == z) & (i == y)
        local = pltpu.make_async_copy(stage.at[i], out.at[y], own)
        away = remote(stage.at[i], out.at[y], send.at[i], recv.at[y], (t * 4 + i, c, z))
        back = remote(stage.at[i], out.at[i], send.at[i], recv.at[i], (t * 4 + i, c, z))

        @pl.when(me)
        def _():
            local.start() if mode == "start" else local.wait()

        @pl.when(jnp.logical_not(me))
        def _():
            if mode == "start":
                away.start()
            else:
                back.wait_send()
                back.wait_recv()

        return carry

    lax.fori_loop(0, 4, each, 0)


def dot_nt(a, b):
    return lax.dot_general(a, b, (((1,), (1,)), ((), ())), preferred_element_type=F32)


def dot_tn(a, b):
    return lax.dot_general(a, b, (((0,), (0,)), ((), ())), preferred_element_type=F32)


def dot_nn(a, b):
    return jnp.dot(a, b, preferred_element_type=F32)


def row_blocks(size, body):
    for i in range(HALF // size):
        body(pl.ds(i * size, size))


def norm_rows(src, gain, shift, dst):
    def body(rows):
        x = src[rows]
        mean = jnp.mean(x, axis=-1, keepdims=True)
        centred = x - mean
        spread = jnp.mean(centred * centred, axis=-1, keepdims=True)
        dst[rows] = (centred * lax.rsqrt(spread + EPS) * gain + shift).astype(BF)

    row_blocks(HALF, body)


GELU_A = 0.7978845608028654
GELU_B = 0.044715


PLAN = {
    "start": [
        ("pieces", 0), ("x", 0), ("pieces", 1), ("plane", 0), ("pieces", 2), ("x", 1), ("pass", 0), ("plane", 1),
        ("pieces", 3), ("share", 0), ("x", 2), ("plane", 2), ("ready", 0),
    ],
    (0, "in"): [("pass", 1), ("pieces", 4)],
    (0, "att0"): [("x", 3), ("plane", 3), ("pass", 2)],
    (0, "att1"): [("share", 1), ("x", 4), ("pieces", 5), ("plane", 4)],
    (0, "up"): [("pass", 3), ("share", 2), ("x", 5), ("plane", 5), ("ready", 1)],
    (0, "down"): [("pass", 4), ("share", 3), ("ready", 2)],
    (1, "in"): [("ready", 3), ("share", 4)],
    (1, "att0"): [("pass", 5)],
    (1, "att1"): [("share", 5)],
    (1, "up"): [("ready", 4)],
    (1, "down"): [("ready", 5)],
}


def gather_kernel(
    patch_w,
    text_w,
    in_w,
    out_w,
    up_w,
    down_w,
    vectors,
    gains,
    stamps_q,
    stamps_k,
    patches,
    words,
    w_out,
    patch_out,
    vec_out,
    xs_out,
    mid_out,
    nrm_out,
    fn_out,
    tri_out,
    kvo_out,
    mix_out,
    lse_out,
    pre_out,
    act_out,
    buf,
    vec,
    gain,
    stamp_q,
    stamp_k,
    pstage,
    prow,
    word,
    xs,
    mid,
    nrm,
    fn,
    tri,
    kvo,
    mix,
    lse,
    pre,
    act,
    bias,
    hid,
    pieces,
    local,
    send,
    recv,
    psend,
    precv,
    own,
    vsend,
    vrecv,
    ksend,
    krecv,
    saved,
):
    z, y, c, t = place()
    g = Gather(buf, pieces, send, recv)
    sources = [(patch_w, 0, 192), (text_w, 192, 192)]
    for which in range(NL):
        base = STEM + which * LAYER
        sources += [
            (in_w.at[which], base, 576),
            (out_w.at[which], base + 576, 192),
            (up_w.at[which], base + 768, 768),
            (down_w.at[which], base + 1536, 768),
        ]
    loads = [
        pltpu.make_async_copy(ref, buf.at[0, pl.ds(row, rows)], local.at[2 + k])
        for k, (ref, row, rows) in enumerate(sources)
    ]
    first = [
        pltpu.make_async_copy(patches, pstage, local.at[0]),
        pltpu.make_async_copy(vectors, vec.at[0], local.at[1]),
    ]
    late = [
        pltpu.make_async_copy(words, word, local.at[12]),
        pltpu.make_async_copy(gains, gain, local.at[13]),
        pltpu.make_async_copy(stamps_q, stamp_q, local.at[14]),
        pltpu.make_async_copy(stamps_k, stamp_k, local.at[15]),
    ]
    for k, (unit, colour) in enumerate(PIECES):
        spot = {sem: (row, p, q) for sem, _, p, _, q, row, _ in g.planes(unit)}
        row, p, q = spot[4 + 10 * colour]
        row = row + p * 64 + q * 16
        low = GATHER_UNITS[unit][0] + sum(GATHER_UNITS[unit][1 : 2 + colour])
        for ref, at, rows in sources:
            if at < low + 512 and at + rows > low:

                @pl.when((row >= at) & (row < at + rows))
                def _(ref=ref, at=at, rows=rows):
                    there = jnp.clip(row - at, 0, rows - 16)
                    src = ref.at[pl.ds(pl.multiple_of(there, 16), 16)]
                    pltpu.make_async_copy(src, pieces.at[k], local.at[16 + k]).start()

    for copy in first + loads + late:
        copy.start()
    greet("in")
    for k, (unit, colour) in enumerate(PIECES):
        pltpu.make_async_copy(up_w.at[0, pl.ds(0, 16)], pieces.at[k], local.at[16 + k]).wait()
        if PIECES[k + 1 : k + 2] and PIECES[k + 1][0] == unit:
            continue
        g.start(unit, 1)
    for copy in first:
        copy.wait()
    scatter_patches(pstage, prow, psend, precv, own, "start")
    vec_copies = [
        remote(vec.at[0], vec.at[r], vsend.at[r - 1], vrecv.at[r - 1], peer("x", -r)) for r in (1, 2, 3)
    ]
    for copy in vec_copies:
        copy.start()
    members = [[0, 1, 2, 3], [4], [5], [6, 7], [8], [9]]

    def pieces_on(unit):
        g.arrived(unit, 1)
        g.start(unit, 2)

    def x_on(unit):
        for k in members[unit]:
            loads[k].wait()
        g.start(unit, 0)

    def plane_on(unit):
        g.arrived(unit, 2)
        g.start(unit, 3)

    def pass_on(unit):
        g.arrived(unit, 0)
        g.arrived(unit, 3)
        g.start(unit, 4)

    def share(unit):
        g.arrived(unit, 4)
        g.start(unit, 5)

    saves = []

    def save(k, src, dst):
        copy = pltpu.make_async_copy(src, dst, saved.at[k])
        copy.start()
        saves.append(copy)

    def ready(unit):
        g.arrived(unit, 5)
        rows = pl.ds(GATHER_UNITS[unit][0], sum(GATHER_UNITS[unit][1:]))
        save(14 + unit, buf.at[:, rows], w_out.at[:, rows])

    act_of = {
        "pieces": pieces_on,
        "x": x_on,
        "plane": plane_on,
        "pass": pass_on,
        "share": share,
        "ready": ready,
    }

    def tick(*steps):
        for name, unit in steps:
            act_of[name](unit)

    tick(*PLAN["start"][:5])
    for copy in late:
        copy.wait()

    lse[...] = jnp.zeros_like(lse)

    def see(i, carry):
        rows = pl.ds(pl.multiple_of(i * 64, 64), 64)
        bias[rows] = jnp.where(stamp_k[rows, 0:1] <= stamp_q[0:1, :], 0.0, MASKED)
        return carry

    lax.fori_loop(0, 8, see, 0)

    tick(*PLAN["start"][5:])
    scatter_patches(pstage, prow, psend, precv, own, "wait")
    for copy in vec_copies:
        copy.wait()
    place_in = lax.broadcasted_iota(jnp.int32, (HALF, 1), 0) % (IMG_GROUP + 2)
    parts = []
    for a in range(4):
        s = (a - t) % 4
        picture = dot_nt(prow[...].reshape(HALF, D), buf[s, 0:192]) + vec[s, 2:3, 0:192]
        language = dot_nt(word[...], buf[s, 192:384]) + vec[s, 3:4, 0:192]
        mark = vec[s, 4:5, 0:192]
        part = jnp.where(place_in < IMG_GROUP, picture, jnp.where(place_in == IMG_GROUP, language, mark))
        parts.append(part.astype(BF).astype(F32))
    xs[0] = jnp.concatenate(parts, axis=1)
    save(0, prow, patch_out)
    save(1, vec, vec_out)

    for which in range(NL):
        base = STEM + which * LAYER
        k0 = 20 + 9 * which
        save(k0, xs.at[which], xs_out.at[which])
        tick(*PLAN[which, "in"])
        norm_rows(xs.at[which], gain[which : which + 1], gain[2 + which : 3 + which], nrm.at[which])

        def project(s, carry):
            triple = dot_nt(buf[s, base : base + 576], nrm[which])
            tri[which, s] = triple.astype(BF)
            remote(
                tri.at[which, s, pl.ds(192, 384)],
                kvo.at[which, s],
                ksend.at[which, s],
                krecv.at[which, s],
                sibling(),
            ).start()
            return carry

        lax.fori_loop(0, 4, project, 0)
        save(k0 + 1, nrm.at[which], nrm_out.at[which])
        save(k0 + 2, tri.at[which], tri_out.at[which])
        mid[which] = xs[which]

        def attend(s, carry):
            remote(
                tri.at[which, s, pl.ds(192, 384)],
                kvo.at[which, s],
                ksend.at[which, s],
                krecv.at[which, s],
                sibling(),
            ).wait_recv()
            for h in range(3):
                at = 64 * h
                q = tri[which, s, at : at + 64] * jnp.asarray(HEAD_DIM**-0.5, BF)
                one = dot_tn(tri[which, s, 192 + at : 256 + at], q) + bias[0:256]
                two = dot_tn(kvo[which, s, at : at + 64], q) + bias[256:512]
                top = jnp.maximum(jnp.max(one, axis=0, keepdims=True), jnp.max(two, axis=0, keepdims=True))
                one = jnp.exp(one - top)
                two = jnp.exp(two - top)
                total = jnp.sum(one, axis=0, keepdims=True) + jnp.sum(two, axis=0, keepdims=True)
                lse[which, s, h : h + 1] = top + jnp.log(total)
                scale = 1.0 / total
                one = (one * scale).astype(BF)
                two = (two * scale).astype(BF)
                mixed = dot_nn(tri[which, s, 384 + at : 448 + at], one)
                mixed = mixed + dot_nn(kvo[which, s, 192 + at : 256 + at], two)
                mix[which, s, at : at + 64] = mixed.astype(BF)
            mid[which] += dot_tn(mix[which, s], buf[s, base + 576 : base + 768])
            return carry

        tick(*PLAN[which, "att0"])
        lax.fori_loop(0, 2, attend, 0)
        tick(*PLAN[which, "att1"])
        lax.fori_loop(2, 4, attend, 0)
        save(k0 + 3, kvo.at[which], kvo_out.at[which])
        save(k0 + 4, mix.at[which], mix_out.at[which])
        save(k0 + 5, lse.at[which], lse_out.at[which])
        save(k0 + 6, mid.at[which], mid_out.at[which])
        norm_rows(mid.at[which], gain[4 + which : 5 + which], gain[6 + which : 7 + which], fn.at[which])
        tick(*PLAN[which, "up"])

        def lift(s, carry):
            pre[which, s] = dot_nn(fn[which], buf[s, base + 768 : base + 1536]) + vec[s, which : which + 1]
            return carry

        save(k0 + 7, fn.at[which], fn_out.at[which])
        lax.fori_loop(0, 4, lift, 0)
        save(k0 + 8, pre.at[which], pre_out.at[which])
        xs[which + 1] = mid[which]
        tick(*PLAN[which, "down"])

        def lower(s, carry):
            def body(rows):
                x = pre[which, s, rows]
                hid[rows] = (0.5 * x * (1.0 + jnp.tanh(GELU_A * (x + GELU_B * x * x * x)))).astype(BF)

            row_blocks(HALF, body)
            xs[which + 1] += dot_nn(hid[...], buf[s, base + 1536 : base + 2304])
            return carry

        lax.fori_loop(0, 4, lower, 0)

    flipped = xs[2].astype(BF).T
    for a in range(4):
        act[a] = flipped[192 * a : 192 * a + 192]
    save(13, act, act_out)
    for which in range(NL):
        for s in range(4):
            remote(
                tri.at[which, s, pl.ds(192, 384)],
                kvo.at[which, s],
                ksend.at[which, s],
                krecv.at[which, s],
                sibling(),
            ).wait_send()
    for unit in range(6):
        g.finish(unit)
    for copy in saves:
        copy.wait()


def forward_call(*args):
    any_ = pl.BlockSpec(memory_space=pl.ANY)
    sds = jax.ShapeDtypeStruct
    shapes = [
        ((4, ROWS, D), BF),
        ((4, 64, D), BF),
        ((4, 8, D), F32),
        ((2, HALF, D), F32),
        ((2, HALF, D), F32),
        ((2, HALF, D), BF),
        ((2, HALF, D), BF),
        ((2, 4, 576, HALF), BF),
        ((2, 4, 384, HALF), BF),
        ((2, 4, 192, HALF), BF),
        ((2, 4, 8, HALF), F32),
        ((2, 4, HALF, D), F32),
        ((4, 192, HALF), BF),
    ]
    dma = pltpu.SemaphoreType.DMA
    return pl.pallas_call(
        gather_kernel,
        out_shape=tuple(sds(s, d) for s, d in shapes),
        in_specs=[any_] * 12,
        out_specs=(any_,) * len(shapes),
        scratch_shapes=[
            pltpu.VMEM((4, ROWS, D), BF),
            pltpu.VMEM((4, 8, D), F32),
            pltpu.VMEM((8, D), F32),
            pltpu.VMEM((8, HALF), jnp.int32),
            pltpu.VMEM((L, 128), jnp.int32),
            pltpu.VMEM((4, 64, D), BF),
            pltpu.VMEM((4, 64, D), BF),
            pltpu.VMEM((HALF, D), BF),
            pltpu.VMEM((3, HALF, D), F32),
            pltpu.VMEM((2, HALF, D), F32),
            pltpu.VMEM((2, HALF, D), BF),
            pltpu.VMEM((2, HALF, D), BF),
            pltpu.VMEM((2, 4, 576, HALF), BF),
            pltpu.VMEM((2, 4, 384, HALF), BF),
            pltpu.VMEM((2, 4, 192, HALF), BF),
            pltpu.VMEM((2, 4, 8, HALF), F32),
            pltpu.VMEM((2, 4, HALF, D), F32),
            pltpu.VMEM((4, 192, HALF), BF),
            pltpu.VMEM((L, HALF), F32),
            pltpu.VMEM((HALF, D), BF),
            pltpu.VMEM((7, 16, D), BF),
            dma((23,)),
            dma((6, 27)),
            dma((6, 27)),
            dma((4,)),
            dma((4,)),
            dma,
            dma((3,)),
            dma((3,)),
            dma((2, 4)),
            dma((2, 4)),
            dma((38,)),
        ],
        compiler_params=pltpu.CompilerParams(
            collective_id=0, has_side_effects=True, vmem_limit_bytes=63 * 2**20
        ),
    )(*args)


def prepare(
    patches,
    text_features,
    patch_weight,
    patch_bias,
    text_weight,
    text_bias,
    readout,
    mix_gain,
    mix_shift,
    heads_in_weight,
    heads_out_weight,
    feed_gain,
    feed_shift,
    up_weight,
    up_bias,
    down_weight,
    timesteps,
):
    t = lax.axis_index("tensor")
    c = lax.axis_index("ctx")
    wide = lambda v: jnp.pad(v.astype(F32), (0, D - DEV))[None]
    vectors = jnp.concatenate(
        [up_bias, wide(patch_bias), wide(text_bias), wide(readout), jnp.zeros((3, D), F32)], axis=0
    )
    gains = jnp.concatenate([mix_gain, mix_shift, feed_gain, feed_shift], axis=0)
    stamps = lax.dynamic_slice_in_dim(timesteps, t, 1, 0).reshape(2, HALF)
    mine = lax.dynamic_slice_in_dim(stamps, c, 1, 0)
    other = lax.dynamic_slice_in_dim(stamps, 1 - c, 1, 0)
    stamps_q = jnp.broadcast_to(mine, (8, HALF))
    stamps_k = jnp.broadcast_to(jnp.concatenate([mine, other], 1).reshape(L, 1), (L, 128))
    spaced = lax.dynamic_slice_in_dim(patches, t * 240, 240, 0).reshape(4, 2, IMG_GROUP, D)
    spaced = jnp.pad(spaced, ((0, 0), (0, 0), (0, 2), (0, 0))).reshape(4, 64, D)
    words = lax.dynamic_slice_in_dim(text_features, t, 1, 0).reshape(8, 1, D)
    words = jnp.pad(words, ((0, 0), (IMG_GROUP, 1), (0, 0))).reshape(HALF, D)
    return (
        patch_weight.T,
        text_weight.T,
        heads_in_weight.transpose(0, 2, 3, 1).reshape(NL, 3 * DEV, D),
        heads_out_weight,
        up_weight,
        down_weight,
        vectors,
        gains,
        stamps_q,
        stamps_k,
        spaced,
        words,
    )


SUM_UNITS = [
    (256, 512, "z"),
    (768, 0, "z"),
    (256, 512, "y"),
    (256, 512, "z"),
    (768, 0, "z"),
    (256, 512, "y"),
    (0, 512, "z"),
]
NU = len(SUM_UNITS)
STEMS = 6


class Sums:
    def __init__(self, grads, core_in, big, small, out, send, recv, local, credit):
        self.grads, self.core_in, self.big, self.small = grads, core_in, big, small
        self.out, self.send, self.recv, self.local, self.credit = out, send, recv, local, credit

    def where(self, u):
        nx, npl, slow = SUM_UNITS[u]
        z, y, c, t = place()
        fast = "y" if slow == "z" else "z"
        m = lambda v: pl.multiple_of(v, 16)
        return nx // 2, npl // 2, nx + c * (npl // 2), slow, fast, {"z": z, "y": y}, c, t, m

    def copy(self, u, sem, src, dst, device):
        return remote(src, dst, self.send.at[u, sem], self.recv.at[u, sem], device)

    def core(self, u, s):
        n, p, _, slow, fast, at, c, t, m = self.where(u)
        g, into = self.grads.at[u % 3], self.core_in.at[u % 2]
        out = []
        if n:
            src = g.at[s, pl.ds(m((1 - c) * n), n)]
            out.append(self.copy(u, s, src, into.at[s, pl.ds(0, n)], sibling()))
        if p:
            src = g.at[s, pl.ds(m(2 * n + (1 - c) * p), p)]
            out.append(self.copy(u, 4 + s, src, into.at[s, pl.ds(n, p)], sibling()))
        return out

    def begin(self, u):
        if u >= 2:
            pl.semaphore_wait(self.credit, 1)

    def give(self, u, s):
        for copy in self.core(u, s):
            copy.start()

    def cores(self, u):
        return [copy for s in range(4) for copy in self.core(u, s)]

    def across(self, u):
        n, p, row, slow, fast, at, c, t, m = self.where(u)
        g, big = self.grads.at[u % 3], self.big[u % 3]
        out = []
        if n:
            h = n // 2
            out.append(self.copy(u, 8, g.at[2, pl.ds(m(c * n), h)], big["xa"].at[0], peer("x", 1)))
            out.append(self.copy(u, 9, g.at[2, pl.ds(m(c * n + h), h)], big["xa"].at[1], peer("x", -1)))
        if p:
            block = row + (at[slow] + 2) % 4 * 64
            out.append(self.copy(u, 10, g.at[:, pl.ds(m(block), 32)], big["pa"].at[0], peer(slow, 1)))
            out.append(self.copy(u, 11, g.at[:, pl.ds(m(block + 32), 32)], big["pa"].at[1], peer(slow, -1)))
        return out

    def beside(self, u):
        n, p, row, slow, fast, at, c, t, m = self.where(u)
        g, big = self.grads.at[u % 3], self.big[u % 3]
        out = []
        if n:
            rows = pl.ds(m(c * n), n)
            out.append(self.copy(u, 12, g.at[1, rows], big["xr"].at[0], peer("x", 1)))
            out.append(self.copy(u, 13, g.at[3, rows], big["xr"].at[1], peer("x", -1)))
        if p:
            for k, r in ((0, 1), (1, 3)):
                block = row + (at[slow] + r) % 4 * 64
                out.append(self.copy(u, 14 + k, g.at[:, pl.ds(m(block), 64)], big["pr"].at[k], peer(slow, r)))
        return out

    def second(self, u):
        n, p, row, slow, fast, at, c, t, m = self.where(u)
        big, small = self.big[u % 3], self.small[u]
        out = []
        for r in (1, 2, 3):
            if n:
                block = pl.ds(m((at["y"] + r) % 4 * (n // 4)), n // 4)
                out.append(self.copy(u, 15 + r, big["xs"].at[block], small["yr"].at[r - 1], peer("y", r)))
            if p:
                block = pl.ds(m((at[fast] + r) % 4 * 16), 16)
                out.append(self.copy(u, 18 + r, big["ps"].at[:, block], small["qr"].at[r - 1], peer(fast, r)))
        return out

    def third(self, u):
        n, p, row, slow, fast, at, c, t, m = self.where(u)
        small = self.small[u]
        out = []
        for r in (1, 2, 3):
            if n:
                mine = small["zb"].at[at["z"]]
                out.append(self.copy(u, 21 + r, mine, mine, peer("z", r)))
            if p:
                out.append(self.copy(u, 24 + r, small["qs"].at[r], small["tr"].at[r - 1], peer("x", r)))
        return out

    def rows(self, u):
        n, p, row, slow, fast, at, c, t, m = self.where(u)
        base = u * D
        return (
            pl.ds(m(base + c * n), n),
            pl.ds(m(base + c * n + at["y"] * (n // 4)), n // 4),
            pl.ds(m(base + row), p),
            pl.ds(m(base + row + at[slow] * 64), 64),
            pl.ds(m(base + row + at[slow] * 64 + at[fast] * 16), 16),
        )

    def fourth(self, u):
        n, p, row, slow, fast, at, c, t, m = self.where(u)
        small = self.small[u]
        _, x_own, _, _, p_own = self.rows(u)
        out = []
        for r in (1, 2, 3):
            if n:
                out.append(self.copy(u, 27 + r, small["fx"], self.out.at[x_own], peer("y", r)))
            if p:
                out.append(self.copy(u, 30 + r, small["fp"], self.out.at[p_own], peer(fast, r)))
        return out

    def own(self, u):
        n, p = self.where(u)[:2]
        _, x_own, _, _, p_own = self.rows(u)
        out = []
        if n:
            out.append(pltpu.make_async_copy(self.small[u]["fx"], self.out.at[x_own], self.local.at[u, 0]))
        if p:
            out.append(pltpu.make_async_copy(self.small[u]["fp"], self.out.at[p_own], self.local.at[u, 1]))
        return out

    def fifth(self, u):
        n, p, row, slow, fast, at, c, t, m = self.where(u)
        if not p:
            return []
        region = self.out.at[self.rows(u)[3]]
        return [self.copy(u, 33 + r, region, region, peer(slow, r)) for r in (1, 2, 3)]

    def sixth(self, u):
        n, p = self.where(u)[:2]
        x_all, _, p_all, _, _ = self.rows(u)
        out = []
        if n:
            region = self.out.at[x_all]
            out.append(self.copy(u, 37, region, region, sibling()))
        if p:
            region = self.out.at[p_all]
            out.append(self.copy(u, 38, region, region, sibling()))
        return out

    def add(self, u, count, size, terms, result):
        def step(i, carry):
            total = None
            for ref, index in terms(i):
                v = ref[index].astype(F32)
                total = v if total is None else total + v
            ref, index = result(i)
            ref[index] = total.astype(BF)
            return carry

        if count == 1:
            step(0, 0)
        else:
            lax.fori_loop(0, count, step, 0)

    def step(self, k, u):
        n, p, row, slow, fast, at, c, t, m = self.where(u)
        g, big, small = self.grads.at[u % 3], self.big[u % 3], self.small[u]
        if k == 1:
            for copy in self.cores(u):
                copy.wait_recv()
            for first, there, rows in ((c * n, 0, n), (row, n, p)):
                if rows:
                    per = rows // 128
                    mine = lambda i: (g, (i // per, pl.ds(m(first + i % per * 128), 128)))
                    its = lambda i: (self.core_in.at[u % 2], (i // per, pl.ds(m(there + i % per * 128), 128)))
                    self.add(u, 4 * per, 128, lambda i: [mine(i), its(i)], mine)
            if u + 2 < NU:
                pl.semaphore_signal(self.credit, inc=1, device_id=sibling(), device_id_type=MESH)
            for copy in self.across(u):
                copy.start()
        if k == 2:
            for copy in self.across(u):
                copy.wait_recv()
            if n:
                h = n // 2
                for k, slot, first in ((0, 1, c * n), (1, 3, c * n + h)):
                    mine = lambda i: (g, (slot, pl.ds(m(first + i * 64), 64)))
                    its = lambda i: (big["xa"], (k, pl.ds(m(i * 64), 64)))
                    self.add(u, h // 64, 64, lambda i: [mine(i), its(i)], mine)
            if p:
                for k, r in ((0, 1), (1, 3)):
                    first = row + (at[slow] + r) % 4 * 64 + 32 * k
                    mine = lambda i: (g, (i, pl.ds(m(first), 32)))
                    its = lambda i: (big["pa"], (k, i))
                    self.add(u, 4, 32, lambda i: [mine(i), its(i)], mine)
            for copy in self.beside(u):
                copy.start()
        if k == 3:
            for copy in self.beside(u):
                copy.wait_recv()
            if n:
                self.add(
                    u,
                    n // 64,
                    64,
                    lambda i: [(g, (0, pl.ds(m(c * n + i * 64), 64)))]
                    + [(big["xr"], (r, pl.ds(m(i * 64), 64))) for r in range(2)],
                    lambda i: (big["xs"], pl.ds(m(i * 64), 64)),
                )
            if p:
                first = row + at[slow] * 64
                self.add(
                    u,
                    4,
                    64,
                    lambda i: [(g, (i, pl.ds(m(first), 64)))] + [(big["pr"], (r, i)) for r in range(2)],
                    lambda i: (big["ps"], i),
                )
            for copy in self.second(u):
                copy.start()
            for copy in self.cores(u) + self.across(u) + self.beside(u):
                copy.wait_send()
        if k == 4:
            for copy in self.second(u):
                copy.wait_recv()
            if n:
                own = pl.ds(m(at["y"] * (n // 4)), n // 4)
                self.add(
                    u,
                    1,
                    n // 4,
                    lambda i: [(big["xs"], own)] + [(small["yr"], r) for r in range(3)],
                    lambda i: (small["zb"], at["z"]),
                )
            if p:
                own = pl.ds(m(at[fast] * 16), 16)
                self.add(
                    u,
                    4,
                    16,
                    lambda i: [(big["ps"], (i, own))] + [(small["qr"], (r, i)) for r in range(3)],
                    lambda i: (small["qs"], i),
                )
            for copy in self.third(u):
                copy.start()
            for copy in self.second(u):
                copy.wait_send()
        if k == 5:
            for copy in self.third(u):
                copy.wait_recv()
            if n:
                self.add(
                    u, 1, n // 4, lambda i: [(small["zb"], r) for r in range(4)], lambda i: (small["fx"], slice(None))
                )
            if p:
                self.add(
                    u,
                    1,
                    16,
                    lambda i: [(small["qs"], 0)] + [(small["tr"], r) for r in range(3)],
                    lambda i: (small["fp"], slice(None)),
                )
            for copy in self.fourth(u) + self.own(u):
                copy.start()
        if k == 6:
            for copy in self.fourth(u):
                copy.wait_recv()
            for copy in self.own(u):
                copy.wait()
            for copy in self.fifth(u) if p else self.sixth(u):
                copy.start()
        if k == 7 and p:
            for copy in self.fifth(u):
                copy.wait_recv()
            for copy in self.sixth(u):
                copy.start()
        if k == 8:
            for copy in self.sixth(u):
                copy.wait_recv()
            for copy in self.third(u) + self.fourth(u) + self.fifth(u) + self.sixth(u):
                copy.wait_send()


def big_shapes():
    out = []
    for nx, npl, _ in SUM_UNITS[:3]:
        n, p = nx // 2, npl // 2
        shapes = {}
        if n:
            shapes |= {"xa": (2, n // 2, D), "xr": (2, n, D), "xs": (n, D)}
        if p:
            shapes |= {"pa": (2, 4, 32, D), "pr": (2, 4, 64, D), "ps": (4, 64, D)}
        out.append(shapes)
    return out


def small_shapes():
    out = []
    for nx, npl, _ in SUM_UNITS:
        q = nx // 8
        shapes = {}
        if nx:
            shapes |= {"yr": (3, q, D), "zb": (4, q, D), "fx": (q, D)}
        if npl:
            shapes |= {"qr": (3, 4, 16, D), "qs": (4, 16, D), "tr": (3, 16, D), "fp": (16, D)}
        out.append(shapes)
    return out


def norm_back(x, grad, base, gain, out, sums, gain_row, shift_row):
    zero = jnp.zeros((1, D), F32)
    sums[gain_row : gain_row + 1] = zero
    sums[shift_row : shift_row + 1] = zero

    def body(rows):
        v = x[rows]
        g = grad[rows]
        mean = jnp.mean(v, axis=-1, keepdims=True)
        centred = v - mean
        spread = jnp.mean(centred * centred, axis=-1, keepdims=True)
        inv = lax.rsqrt(spread + EPS)
        hat = centred * inv
        sums[gain_row : gain_row + 1] += jnp.sum(g * hat, axis=0, keepdims=True)
        sums[shift_row : shift_row + 1] += jnp.sum(g, axis=0, keepdims=True)
        d = g * gain
        first = jnp.mean(d, axis=-1, keepdims=True)
        second = jnp.mean(d * hat, axis=-1, keepdims=True)
        out[rows] = base[rows] + inv * (d - first - hat * second)

    row_blocks(HALF, body)


def returns(act, act_out, pgs, pg_out, tgs, tg_out, send, recv, own, mode, which):
    z, y, c, t = place()
    d = z * 4 + y
    if which == 0:
        for r in (1, 2, 3):
            a = (t + r) % 4
            copy = remote(act.at[a], act_out.at[t], send.at[r], recv.at[r], (d, c, a))
            copy.start() if mode == "start" else copy.wait()
        copy = pltpu.make_async_copy(act.at[t], act_out.at[t], own.at[0])
        copy.start() if mode == "start" else copy.wait()
        return
    for r in (1, 2, 3):
        a = (t + r) % 4
        copy = remote(tgs.at[a], tg_out.at[t], send.at[4 + r], recv.at[4 + r], (d, c, a))
        copy.start() if mode == "start" else copy.wait()
    copy = pltpu.make_async_copy(tgs.at[t], tg_out.at[t], own.at[1])
    copy.start() if mode == "start" else copy.wait()

    def each(i, carry):
        a, yy = i % 4, i // 4
        to_me = (t == z) & (yy == y) & (a == t)
        src = pgs.at[a, pl.ds(pl.multiple_of(yy * 64, 64), 64)]
        local = pltpu.make_async_copy(src, pg_out.at[d], own.at[2])
        away = remote(src, pg_out.at[d], send.at[8 + i], recv.at[8 + d], (t * 4 + yy, c, a))

        @pl.when(to_me)
        def _():
            local.start() if mode == "start" else local.wait()

        @pl.when(jnp.logical_not(to_me))
        def _():
            away.start() if mode == "start" else away.wait_send()

        return carry

    lax.fori_loop(0, 16, each, 0)
    if mode == "wait":

        def arrive(i, carry):
            from_me = (t == z) & (i == d)

            @pl.when(jnp.logical_not(from_me))
            def _():
                remote(pg_out.at[i], pg_out.at[i], send.at[8 + i], recv.at[8 + i], (i, c, z)).wait_recv()

            return carry

        lax.fori_loop(0, 16, arrive, 0)


SUM_PLAN = {
    (1, "down"): [(1, 0)],
    (1, "up"): [(2, 0), (1, 1)],
    (1, "att1"): [],
    (1, "att2"): [(3, 0), (2, 1)],
    (1, "in"): [(1, 2), (4, 0)],
    (0, "down"): [(1, 3), (5, 0), (2, 2), (3, 1)],
    (0, "up"): [(2, 3), (1, 4), (6, 0), (3, 2)],
    (0, "att1"): [(4, 1), (2, 4), (3, 3), (7, 0)],
    (0, "att2"): [(4, 2), (5, 1)],
    (0, "in"): [(1, 5), (4, 3), (6, 1), (5, 2), (3, 4)],
    "stem": [(1, 6), (2, 5), (5, 3), (6, 2), (4, 4), (2, 6)],
    "end": [
        (3, 5), (3, 6), (7, 2), (6, 3), (5, 4), (4, 5), (4, 6), (7, 3), (6, 4), (5, 5), (5, 6), (6, 5), (6, 6), (7, 5),
        (7, 6),
    ],
}


def backward_kernel(
    w_in,
    patch_in,
    xs_in,
    mid_in,
    nrm_in,
    fn_in,
    tri_in,
    kvo_in,
    mix_in,
    lse_in,
    pre_in,
    act_in,
    gains,
    stamps_q,
    stamps_k,
    words,
    cotangent,
    row_scale,
    out,
    act_out,
    pg_out,
    tg_out,
    wb,
    gain,
    stamp_q,
    stamp_k,
    prow,
    word,
    cot,
    rscale,
    xs,
    mid,
    nrm,
    fn,
    tri,
    kvo,
    mix,
    lse,
    pre,
    bias,
    up,
    low,
    back,
    hgrad,
    hid,
    pgrad,
    fnt,
    kvg,
    kvs,
    rkv,
    tgrad,
    sums,
    vec,
    pgs,
    tgs,
    grads,
    core_in,
    big,
    small,
    wsem,
    lsem,
    send,
    recv,
    local,
    credit,
    ksend,
    krecv,
    rsend,
    rrecv,
    rown,
):
    z, y, c, t = place()
    copy_in = pltpu.make_async_copy

    def section(row, rows, s):
        return copy_in(w_in.at[s, pl.ds(row, rows)], wb.at[s, pl.ds(0, rows)], wsem.at[s])

    sections = []
    for which in (1, 0):
        base = STEM + which * LAYER
        sections += [(base + 1536, 768), (base + 768, 768), (base, 768)]
    sections.append((0, STEM))

    def acts(which):
        return [
            copy_in(pre_in.at[which], pre, lsem.at[0]),
            copy_in(fn_in.at[which], fn, lsem.at[1]),
            copy_in(mid_in.at[which], mid, lsem.at[2]),
            copy_in(tri_in.at[which], tri, lsem.at[3]),
            copy_in(kvo_in.at[which], kvo, lsem.at[4]),
            copy_in(mix_in.at[which], mix, lsem.at[5]),
            copy_in(lse_in.at[which], lse, lsem.at[6]),
            copy_in(nrm_in.at[which], nrm, lsem.at[7]),
            copy_in(xs_in.at[which], xs, lsem.at[8]),
        ]

    head = [
        copy_in(cotangent.at[t], cot, lsem.at[9]),
        copy_in(row_scale, rscale, lsem.at[10]),
    ]
    for copy in head:
        copy.start()
    for s in range(4):
        section(*sections[0], s).start()
    loads = acts(1)
    for copy in loads:
        copy.start()
    rest = [
        copy_in(gains, gain, lsem.at[11]),
        copy_in(stamps_q, stamp_q, lsem.at[12]),
        copy_in(stamps_k, stamp_k, lsem.at[13]),
        copy_in(patch_in, prow, lsem.at[14]),
        copy_in(words, word, lsem.at[15]),
    ]
    for copy in rest:
        copy.start()
    greet("out")
    returns(act_in, act_out, pgs, pg_out, tgs, tg_out, rsend, rrecv, rown, "start", 0)
    total = Sums(grads, core_in, big, small, out, send, recv, local, credit)

    def comm(key):
        for k, u in SUM_PLAN[key]:
            total.step(k, u)

    for copy in head:
        copy.wait()

    def first_up(rows):
        up[rows] = cot[rows].astype(F32) * rscale[rows, 0:1]

    row_blocks(HALF, first_up)
    vec[...] = jnp.zeros_like(vec)
    sums[...] = jnp.zeros_like(sums)
    for copy in rest:
        copy.wait()

    def see(i, carry):
        rows = pl.ds(pl.multiple_of(i * 64, 64), 64)
        bias[rows] = jnp.where(stamp_k[rows, 0:1] <= stamp_q[0:1, :], 0.0, MASKED)
        return carry

    lax.fori_loop(0, 8, see, 0)

    for which in (1, 0):
        u0 = 0 if which else 3
        loads = acts(which)
        loads[0].wait()

        def round_up(rows):
            low[rows] = up[rows].astype(BF)

        row_blocks(HALF, round_up)
        b = u0 % 3
        after = sections[u0 + 1]

        def down(s, carry):
            section(*sections[u0], s).wait()
            hgrad[...] = dot_nt(low[...], wb[s])
            section(*after, s).start()

            def body(rows):
                x = pre[s, rows]
                th = jnp.tanh(GELU_A * (x + GELU_B * x * x * x))
                hid[rows] = (0.5 * x * (1.0 + th)).astype(BF)
                slope = 0.5 * (1.0 + th) + 0.5 * x * (1.0 - th * th) * (GELU_A * (1.0 + 3.0 * GELU_B * x * x))
                pgrad[s, rows] = (hgrad[rows] * slope).astype(BF)

            row_blocks(HALF, body)
            for j in range(3):
                grads[b, s, 256 * j : 256 * j + 256] = dot_tn(hid[:, 256 * j : 256 * j + 256], low[...]).astype(BF)
            total.give(u0, s)
            vec[s, which : which + 1] = jnp.sum(pgrad[s].astype(F32), axis=0, keepdims=True)
            return carry

        total.begin(u0)
        lax.fori_loop(0, 4, down, 0)
        if which:
            acts(0)[0].start()
        comm((which, "down"))

        b = (u0 + 1) % 3
        after = sections[u0 + 2]
        loads[1].wait()
        fnt[...] = fn[...].T
        back[...] = jnp.zeros_like(back)

        def lift(s, carry):
            section(*sections[u0 + 1], s).wait()
            back[...] += dot_nt(pgrad[s], wb[s])
            section(*after, s).start()
            for j in range(3):
                grads[b, s, 256 * j : 256 * j + 256] = dot_nn(fnt[256 * j : 256 * j + 256], pgrad[s]).astype(BF)
            total.give(u0 + 1, s)
            return carry

        total.begin(u0 + 1)
        lax.fori_loop(0, 4, lift, 0)
        if which:
            acts(0)[1].start()
        comm((which, "up"))

        loads[2].wait()
        norm_back(mid, back, up, gain[4 + which : 5 + which], up, sums, 6 + which, 8 + which)
        if which:
            acts(0)[2].start()
        row_blocks(HALF, round_up)
        for k in (3, 4, 5, 6):
            loads[k].wait()
        b = (u0 + 2) % 3
        after = sections[u0 + 3]

        def share(s):
            return remote(kvs.at[which, s], rkv.at[which, s], ksend.at[which, s], krecv.at[which, s], sibling())

        def attend(s, carry):
            section(*sections[u0 + 2], s).wait()
            grads[b, s, 576:768] = dot_nn(mix[s], low[...]).astype(BF)
            mixed = dot_nt(wb[s, 576:768], low[...]).astype(BF)
            for h in range(3):
                at = 64 * h
                q = tri[s, at : at + 64] * jnp.asarray(HEAD_DIM**-0.5, BF)
                do = mixed[at : at + 64]
                k1, v1 = tri[s, 192 + at : 256 + at], tri[s, 384 + at : 448 + at]
                k2, v2 = kvo[s, at : at + 64], kvo[s, 192 + at : 256 + at]
                log_total = lse[s, h : h + 1]
                p1 = jnp.exp(dot_tn(k1, q) + bias[0:256] - log_total)
                p2 = jnp.exp(dot_tn(k2, q) + bias[256:512] - log_total)
                d1 = dot_tn(v1, do)
                d2 = dot_tn(v2, do)
                delta = jnp.sum(p1 * d1, axis=0, keepdims=True) + jnp.sum(p2 * d2, axis=0, keepdims=True)
                g1 = (p1 * (d1 - delta)).astype(BF)
                g2 = (p2 * (d2 - delta)).astype(BF)
                dq = (dot_nn(k1, g1) + dot_nn(k2, g2)) * HEAD_DIM**-0.5
                tgrad[s, at : at + 64] = dq.astype(BF)
                kvg[s, at : at + 64] = dot_nt(q, g1)
                kvs[which, s, at : at + 64] = dot_nt(q, g2).astype(BF)
                kvg[s, 192 + at : 256 + at] = dot_nt(do, p1.astype(BF))
                kvs[which, s, 192 + at : 256 + at] = dot_nt(do, p2.astype(BF)).astype(BF)
            share(s).start()
            return carry

        lax.fori_loop(0, 2, attend, 0)
        comm((which, "att1"))
        lax.fori_loop(2, 4, attend, 0)
        if which:
            for k in (3, 4, 5, 6):
                acts(0)[k].start()
        comm((which, "att2"))
        loads[7].wait()
        back[...] = jnp.zeros_like(back)

        def lead(s, carry):
            share(s).wait_recv()
            tgrad[s, 192:576] = (kvg[s] + rkv[which, s].astype(F32)).astype(BF)
            grads[b, s, 0:576] = dot_nn(tgrad[s], nrm[...]).astype(BF)
            total.give(u0 + 2, s)
            back[...] += dot_tn(tgrad[s], wb[s, 0:576])
            section(*after, s).start()
            return carry

        total.begin(u0 + 2)
        lax.fori_loop(0, 4, lead, 0)
        if which:
            acts(0)[7].start()
        comm((which, "in"))
        loads[8].wait()
        norm_back(xs, back, up, gain[which : which + 1], up, sums, 2 + which, 4 + which)
        if which:
            acts(0)[8].start()

    row_blocks(HALF, round_up)
    place_in = lax.broadcasted_iota(jnp.int32, (HALF, 1), 0) % (IMG_GROUP + 2)
    rounded = low[...].astype(F32)
    sums[10:11] = jnp.sum(jnp.where(place_in < IMG_GROUP, rounded, 0.0), axis=0, keepdims=True)
    sums[11:12] = jnp.sum(jnp.where(place_in == IMG_GROUP, rounded, 0.0), axis=0, keepdims=True)
    sums[12:13] = jnp.sum(jnp.where(place_in > IMG_GROUP, up[...], 0.0), axis=0, keepdims=True)
    fnt[...] = low[...].T
    b = STEMS % 3
    back[...] = jnp.zeros_like(back)
    hgrad[...] = jnp.zeros_like(hgrad)
    total.begin(STEMS)
    for a in range(4):
        s = (a - t) % 4
        section(*sections[6], s).wait()
        mine = fnt[192 * a : 192 * a + 192]
        grads[b, s, 0:192] = dot_nn(mine, prow[...].reshape(HALF, D)).astype(BF)
        grads[b, s, 192:384] = dot_nn(mine, word[...]).astype(BF)
        vec[s, 2:16] = sums[2:16]
        grads[b, s, 384:400] = vec[s].astype(BF)
        grads[b, s, 400:512] = jnp.zeros((112, D), BF)
        back[...] += dot_tn(mine, wb[s, 0:192])
        hgrad[...] += dot_tn(mine, wb[s, 192:384])
    for s in range(4):
        total.give(STEMS, s)
    comm("stem")
    for a in range(4):
        pgs[a] = back[:, 192 * a : 192 * a + 192].astype(BF)
    for h in range(8):
        row = hgrad[32 * h + 30 : 32 * h + 31]
        for a in range(4):
            tgs[a, h : h + 1] = row[:, 192 * a : 192 * a + 192]
    returns(act_in, act_out, pgs, pg_out, tgs, tg_out, rsend, rrecv, rown, "start", 1)
    comm("end")
    returns(act_in, act_out, pgs, pg_out, tgs, tg_out, rsend, rrecv, rown, "wait", 0)
    returns(act_in, act_out, pgs, pg_out, tgs, tg_out, rsend, rrecv, rown, "wait", 1)
    for which in range(NL):
        for s in range(4):
            remote(kvs.at[which, s], rkv.at[which, s], ksend.at[which, s], krecv.at[which, s], sibling()).wait_send()
    for u in range(NU):
        total.step(8, u)


def backward_call(*args):
    any_ = pl.BlockSpec(memory_space=pl.ANY)
    sds = jax.ShapeDtypeStruct
    dma = pltpu.SemaphoreType.DMA
    v = pltpu.VMEM
    return pl.pallas_call(
        backward_kernel,
        out_shape=(
            sds((6 * D + 512, D), BF),
            sds((4, 192, HALF), BF),
            sds((16, 64, 192), BF),
            sds((4, 8, 192), F32),
        ),
        in_specs=[any_] * 18,
        out_specs=(any_,) * 4,
        scratch_shapes=[
            v((4, D, D), BF),
            v((8, D), F32),
            v((8, HALF), jnp.int32),
            v((L, 128), jnp.int32),
            v((4, 64, D), BF),
            v((HALF, D), BF),
            v((HALF, D), BF),
            v((HALF, 128), F32),
            v((HALF, D), F32),
            v((HALF, D), F32),
            v((HALF, D), BF),
            v((HALF, D), BF),
            v((4, 576, HALF), BF),
            v((4, 384, HALF), BF),
            v((4, 192, HALF), BF),
            v((4, 8, HALF), F32),
            v((4, HALF, D), F32),
            v((L, HALF), F32),
            v((HALF, D), F32),
            v((HALF, D), BF),
            v((HALF, D), F32),
            v((HALF, D), F32),
            v((HALF, D), BF),
            v((4, HALF, D), BF),
            v((D, HALF), BF),
            v((4, 384, HALF), F32),
            v((2, 4, 384, HALF), BF),
            v((2, 4, 384, HALF), BF),
            v((4, 576, HALF), BF),
            v((16, D), F32),
            v((4, 16, D), F32),
            v((4, HALF, DEV), BF),
            v((4, 8, DEV), F32),
            v((3, 4, D, D), BF),
            v((2, 4, 384, D), BF),
            [{k: v(shape, BF) for k, shape in shapes.items()} for shapes in big_shapes()],
            [{k: v(shape, BF) for k, shape in shapes.items()} for shapes in small_shapes()],
            dma((4,)),
            dma((16,)),
            dma((NU, 39)),
            dma((NU, 39)),
            dma((NU, 2)),
            pltpu.SemaphoreType.REGULAR,
            dma((2, 4)),
            dma((2, 4)),
            dma((24,)),
            dma((24,)),
            dma((3,)),
        ],
        compiler_params=pltpu.CompilerParams(
            collective_id=1, has_side_effects=True, vmem_limit_bytes=63 * 2**20
        ),
    )(*args)


def shards(*args):
    (datasets, dataset_weights, action_mask, cotangent) = args[17:]
    t = lax.axis_index("tensor")
    ops = prepare(*args[:17])
    gains, stamps_q, stamps_k, words = ops[7], ops[8], ops[9], ops[11]
    kept = forward_call(*ops)
    mask = lax.dynamic_slice_in_dim(action_mask, t, 1, 0)[0]
    dataset = lax.dynamic_slice_in_dim(datasets, t, 1, 0)[0]
    weight = jnp.sum(jnp.where(jnp.arange(dataset_weights.shape[0]) == dataset, dataset_weights, 0))
    scale = weight.astype(F32) * mask.astype(F32)
    last = jnp.arange(IMG_GROUP + 2) == IMG_GROUP + 1
    row_scale = jnp.where(last[None, :], scale[:, None], 1.0).reshape(HALF, 1)
    row_scale = jnp.broadcast_to(row_scale, (HALF, 128))
    out, act, pg, tg = backward_call(
        kept[0], kept[1], *kept[3:], gains, stamps_q, stamps_k, words, cotangent, row_scale
    )
    part = lambda u, a, b: out[u * D + a : u * D + b].astype(F32)
    heads_in = jnp.stack([part(5, 0, 576), part(2, 0, 576)]).reshape(NL, 3, DEV, D).transpose(0, 3, 1, 2)
    heads_out = jnp.stack([part(5, 576, 768), part(2, 576, 768)])
    up_grad = jnp.stack([part(4, 0, 768), part(1, 0, 768)])
    down_grad = jnp.stack([part(3, 0, 768), part(0, 0, 768)])
    vectors = part(6, 384, 400)
    own = lax.dynamic_slice_in_dim(vectors, t * DEV, DEV, 1)
    pg = pg.reshape(16, 2, IMG_GROUP + 2, DEV)[:, :, :IMG_GROUP].reshape(960, DEV).astype(F32)
    return (
        act.transpose(0, 2, 1),
        pg,
        tg,
        part(6, 0, 192).T,
        own[10],
        part(6, 192, 384).T,
        own[11],
        own[12],
        own[2:4],
        own[4:6],
        heads_in,
        heads_out,
        own[6:8],
        own[8:10],
        up_grad,
        vectors[0:2],
        down_grad,
    )


def solution(mesh):
    in_specs = (
        P(("dp", "ctx"), None),
        P("dp", "ctx", None),
        P(None, "tensor"),
        P("tensor"),
        P(None, "tensor"),
        P("tensor"),
        P("tensor"),
        P(),
        P(),
        P(None, None, None, "tensor"),
        P(None, "tensor", None),
        P(),
        P(),
        P(None, None, "tensor"),
        P(None, "tensor"),
        P(None, "tensor", None),
        P("dp", None),
        P("dp"),
        P(),
        P("dp", "ctx"),
        P("dp", "ctx", None),
    )
    out_specs = (
        P("dp", "ctx", "tensor"),
        P(("dp", "ctx"), "tensor"),
        P("dp", "ctx", "tensor"),
        P(None, "tensor"),
        P("tensor"),
        P(None, "tensor"),
        P("tensor"),
        P("tensor"),
        P(None, "tensor"),
        P(None, "tensor"),
        P(None, None, None, "tensor"),
        P(None, "tensor", None),
        P(None, "tensor"),
        P(None, "tensor"),
        P(None, None, "tensor"),
        P(None, "tensor"),
        P(None, "tensor", None),
    )
    return jax.shard_map(shards, mesh=mesh, in_specs=in_specs, out_specs=out_specs, check_vma=False)
```

```python
import jax
import jax.numpy as jnp
from jax import lax
from jax.experimental import pallas as pl
from jax.experimental.pallas import tpu as pltpu
from jax.sharding import PartitionSpec as P

HEAD_DIM = 64
HEADS = 12
NL = 2
L = 512
HALF = 256
D = 768
DEV = 192
IMG_GROUP = 30
EPS = 1e-06
MASKED = -1e30
MESH = pl.DeviceIdType.MESH
BF = jnp.bfloat16
F32 = jnp.float32

STEM = 384
LAYER = 2304
ROWS = STEM + NL * LAYER

GATHER_UNITS = [
    (0, 128, 512, 512),
    (1152, 256, 512, 0),
    (1920, 256, 0, 512),
    (2688, 256, 512, 0),
    (3456, 256, 0, 512),
    (4224, 256, 512, 0),
]

PIECES = [(0, 0), (0, 1), (1, 0), (2, 1), (3, 0), (4, 1), (5, 0)]

GRAD_ROWS = NL * LAYER + 512


def place():
    d = lax.axis_index("dp")
    c = lax.axis_index("ctx")
    t = lax.axis_index("tensor")
    return d // 4, d % 4, c, t


def peer(axis, r):
    z, y, c, t = place()
    if axis == "x":
        return (z * 4 + y, c, (t + r) % 4)
    if axis == "y":
        return (z * 4 + (y + r) % 4, c, t)
    return (((z + r) % 4) * 4 + y, c, t)


def sibling():
    z, y, c, t = place()
    return (z * 4 + y, 1 - c, t)


def greet(stem):
    z, y, c, t = place()
    bar = pltpu.get_barrier_semaphore()
    for axis in "xyz":
        for r in (1, 2, 3):
            pl.semaphore_signal(bar, inc=1, device_id=peer(axis, r), device_id_type=MESH)
    pl.semaphore_signal(bar, inc=1, device_id=sibling(), device_id_type=MESH)
    count = 4 if stem == "in" else 16

    def hello(i, carry):
        if stem == "in":
            other = (t * 4 + i, c, z)
        else:
            other = (i, c, z)
        me = (z * 4 + y == other[0]) & (t == other[2])

        @pl.when(jnp.logical_not(me))
        def _():
            pl.semaphore_signal(bar, inc=1, device_id=other, device_id_type=MESH)

        return carry

    lax.fori_loop(0, count, hello, 0)
    own = t == z

    @pl.when(own)
    def _():
        pl.semaphore_wait(bar, 9 + count)

    @pl.when(jnp.logical_not(own))
    def _():
        pl.semaphore_wait(bar, 10 + count)


def remote(src, dst, send, recv, device):
    return pltpu.make_async_remote_copy(
        src_ref=src, dst_ref=dst, send_sem=send, recv_sem=recv, device_id=device, device_id_type=MESH
    )


class Gather:
    def __init__(self, buf, pieces, send, recv):
        self.buf, self.pieces, self.send, self.recv = buf, pieces, send, recv

    def copy(self, unit, sem, src, dst, device):
        return remote(src, dst, self.send.at[unit, sem], self.recv.at[unit, sem], device)

    def planes(self, unit):
        first, nx, nyz, nzy = GATHER_UNITS[unit]
        z, y, c, t = place()
        out = []
        if nyz:
            out.append((4, "z", z, "y", y, first + nx + c * 256, PIECES.index((unit, 0))))
        if nzy:
            out.append((14, "y", y, "z", z, first + nx + nyz + c * 256, PIECES.index((unit, 1))))
        return out

    def stage(self, unit, which):
        first, nx, nyz, nzy = GATHER_UNITS[unit]
        z, y, c, t = place()
        m = lambda v: pl.multiple_of(v, 16)
        buf = self.buf
        n = nx // 2
        row = first + c * n
        out = []
        if which == 0:
            rows = pl.ds(m(row), n)
            out.append(self.copy(unit, 0, buf.at[0, rows], buf.at[1, rows], peer("x", -1)))
            out.append(self.copy(unit, 1, buf.at[0, rows], buf.at[3, rows], peer("x", 1)))
        if which == 4:
            rows = pl.ds(m(row), n // 2)
            out.append(self.copy(unit, 2, buf.at[1, rows], buf.at[2, rows], peer("x", -1)))
            rows = pl.ds(m(row + n // 2), n // 2)
            out.append(self.copy(unit, 3, buf.at[3, rows], buf.at[2, rows], peer("x", 1)))
        if which == 5:
            for k, (at, rows) in enumerate([(first, nx), (first + nx, nyz), (first + nx + nyz, nzy)]):
                if rows:
                    region = buf.at[pl.ds(1, 3), pl.ds(m(at + c * (rows // 2)), rows // 2)]
                    out.append(self.copy(unit, 24 + k, region, region, sibling()))
        for sem, slow, p, fast, q, row, k in self.planes(unit):
            block = lambda p, o, rows: buf.at[pl.ds(1, 3), pl.ds(m(row + p * 64 + o), rows)]
            if which == 1:
                rows = pl.ds(m(row + p * 64 + q * 16), 16)
                for r in (1, 2, 3):
                    out.append(self.copy(unit, sem + r - 1, self.pieces.at[k], buf.at[r, rows], peer("x", -r)))
            if which == 2:
                region = block(p, q * 16, 16)
                for r in (1, 2, 3):
                    out.append(self.copy(unit, sem + 2 + r, region, region, peer(fast, -r)))
            if which == 3:
                region = block(p, 0, 64)
                out.append(self.copy(unit, sem + 6, region, region, peer(slow, -1)))
                out.append(self.copy(unit, sem + 7, region, region, peer(slow, 1)))
            if which == 4:
                region = block((p + 1) % 4, 0, 32)
                out.append(self.copy(unit, sem + 8, region, region, peer(slow, -1)))
                region = block((p + 3) % 4, 32, 32)
                out.append(self.copy(unit, sem + 9, region, region, peer(slow, 1)))
        return out

    def start(self, unit, which):
        for copy in self.stage(unit, which):
            copy.start()

    def arrived(self, unit, which):
        for copy in self.stage(unit, which):
            copy.wait_recv()

    def finish(self, unit):
        for which in range(6):
            for copy in self.stage(unit, which):
                copy.wait_send()


def scatter_patches(stage, out, send, recv, own, mode):
    z, y, c, t = place()

    def each(i, carry):
        me = (t == z) & (i == y)
        local = pltpu.make_async_copy(stage.at[i], out.at[y], own)
        away = remote(stage.at[i], out.at[y], send.at[i], recv.at[y], (t * 4 + i, c, z))
        back = remote(stage.at[i], out.at[i], send.at[i], recv.at[i], (t * 4 + i, c, z))

        @pl.when(me)
        def _():
            local.start() if mode == "start" else local.wait()

        @pl.when(jnp.logical_not(me))
        def _():
            if mode == "start":
                away.start()
            else:
                back.wait_send()
                back.wait_recv()

        return carry

    lax.fori_loop(0, 4, each, 0)


def dot_nt(a, b):
    return lax.dot_general(a, b, (((1,), (1,)), ((), ())), preferred_element_type=F32)


def dot_tn(a, b):
    return lax.dot_general(a, b, (((0,), (0,)), ((), ())), preferred_element_type=F32)


def dot_nn(a, b):
    return jnp.dot(a, b, preferred_element_type=F32)


def row_blocks(size, body):
    for i in range(HALF // size):
        body(pl.ds(i * size, size))


def norm_rows(src, gain, shift, dst):
    def body(rows):
        x = src[rows]
        mean = jnp.mean(x, axis=-1, keepdims=True)
        centred = x - mean
        spread = jnp.mean(centred * centred, axis=-1, keepdims=True)
        dst[rows] = (centred * lax.rsqrt(spread + EPS) * gain + shift).astype(BF)

    row_blocks(HALF, body)


GELU_A = 0.7978845608028654
GELU_B = 0.044715


PLAN = {
    "start": [
        ("pieces", 0), ("x", 0), ("pieces", 1), ("plane", 0), ("pieces", 2), ("x", 1), ("pass", 0), ("plane", 1),
        ("pieces", 3), ("share", 0), ("x", 2), ("plane", 2), ("ready", 0),
    ],
    (0, "in"): [("pass", 1), ("pieces", 4)],
    (0, "att0"): [("x", 3), ("plane", 3), ("pass", 2)],
    (0, "att1"): [("share", 1), ("x", 4), ("pieces", 5), ("plane", 4)],
    (0, "up"): [("pass", 3), ("share", 2), ("x", 5), ("plane", 5), ("ready", 1)],
    (0, "down"): [("pass", 4), ("share", 3), ("ready", 2)],
    (1, "in"): [("ready", 3), ("share", 4)],
    (1, "att0"): [("pass", 5)],
    (1, "att1"): [("share", 5)],
    (1, "up"): [("ready", 4)],
    (1, "down"): [("ready", 5)],
}


def gather_kernel(
    patch_w,
    text_w,
    in_w,
    out_w,
    up_w,
    down_w,
    vectors,
    gains,
    stamps_q,
    stamps_k,
    patches,
    words,
    w_out,
    patch_out,
    vec_out,
    xs_out,
    mid_out,
    nrm_out,
    fn_out,
    tri_out,
    kvo_out,
    mix_out,
    lse_out,
    pre_out,
    act_out,
    buf,
    vec,
    gain,
    stamp_q,
    stamp_k,
    pstage,
    prow,
    word,
    xs,
    mid,
    nrm,
    fn,
    tri,
    kvo,
    mix,
    lse,
    pre,
    act,
    bias,
    hid,
    pieces,
    local,
    send,
    recv,
    psend,
    precv,
    own,
    vsend,
    vrecv,
    ksend,
    krecv,
    saved,
):
    z, y, c, t = place()
    g = Gather(buf, pieces, send, recv)
    sources = [(patch_w, 0, 192), (text_w, 192, 192)]
    for which in range(NL):
        base = STEM + which * LAYER
        sources += [
            (in_w.at[which], base, 576),
            (out_w.at[which], base + 576, 192),
            (up_w.at[which], base + 768, 768),
            (down_w.at[which], base + 1536, 768),
        ]
    loads = [
        pltpu.make_async_copy(ref, buf.at[0, pl.ds(row, rows)], local.at[2 + k])
        for k, (ref, row, rows) in enumerate(sources)
    ]
    first = [
        pltpu.make_async_copy(patches, pstage, local.at[0]),
        pltpu.make_async_copy(vectors, vec.at[0], local.at[1]),
    ]
    late = [
        pltpu.make_async_copy(words, word, local.at[12]),
        pltpu.make_async_copy(gains, gain, local.at[13]),
        pltpu.make_async_copy(stamps_q, stamp_q, local.at[14]),
        pltpu.make_async_copy(stamps_k, stamp_k, local.at[15]),
    ]
    for k, (unit, colour) in enumerate(PIECES):
        spot = {sem: (row, p, q) for sem, _, p, _, q, row, _ in g.planes(unit)}
        row, p, q = spot[4 + 10 * colour]
        row = row + p * 64 + q * 16
        low = GATHER_UNITS[unit][0] + sum(GATHER_UNITS[unit][1 : 2 + colour])
        for ref, at, rows in sources:
            if at < low + 512 and at + rows > low:

                @pl.when((row >= at) & (row < at + rows))
                def _(ref=ref, at=at, rows=rows):
                    there = jnp.clip(row - at, 0, rows - 16)
                    src = ref.at[pl.ds(pl.multiple_of(there, 16), 16)]
                    pltpu.make_async_copy(src, pieces.at[k], local.at[16 + k]).start()

    for copy in first + loads + late:
        copy.start()
    greet("in")
    for k, (unit, colour) in enumerate(PIECES):
        pltpu.make_async_copy(up_w.at[0, pl.ds(0, 16)], pieces.at[k], local.at[16 + k]).wait()
        if PIECES[k + 1 : k + 2] and PIECES[k + 1][0] == unit:
            continue
        g.start(unit, 1)
    for copy in first:
        copy.wait()
    vec_copies = [
        remote(vec.at[0], vec.at[r], vsend.at[r - 1], vrecv.at[r - 1], peer("x", -r)) for r in (1, 2, 3)
    ]
    for copy in vec_copies:
        copy.start()
    members = [[0, 1, 2, 3], [4], [5], [6, 7], [8], [9]]

    def pieces_on(unit):
        g.arrived(unit, 1)
        g.start(unit, 2)

    def x_on(unit):
        for k in members[unit]:
            loads[k].wait()
        g.start(unit, 0)

    def plane_on(unit):
        g.arrived(unit, 2)
        g.start(unit, 3)

    def pass_on(unit):
        g.arrived(unit, 0)
        g.arrived(unit, 3)
        g.start(unit, 4)

    def share(unit):
        g.arrived(unit, 4)
        g.start(unit, 5)

    saves = []

    def save(k, src, dst):
        copy = pltpu.make_async_copy(src, dst, saved.at[k])
        copy.start()
        saves.append(copy)

    def ready(unit):
        g.arrived(unit, 5)
        rows = pl.ds(GATHER_UNITS[unit][0], sum(GATHER_UNITS[unit][1:]))
        save(14 + unit, buf.at[:, rows], w_out.at[:, rows])

    act_of = {
        "pieces": pieces_on,
        "x": x_on,
        "plane": plane_on,
        "pass": pass_on,
        "share": share,
        "ready": ready,
    }

    def tick(*steps):
        for name, unit in steps:
            act_of[name](unit)

    tick(*PLAN["start"][:4])
    scatter_patches(pstage, prow, psend, precv, own, "start")
    tick(*PLAN["start"][4:5])
    for copy in late:
        copy.wait()

    lse[...] = jnp.zeros_like(lse)

    def see(i, carry):
        rows = pl.ds(pl.multiple_of(i * 64, 64), 64)
        bias[rows] = jnp.where(stamp_k[rows, 0:1] <= stamp_q[0:1, :], 0.0, MASKED)
        return carry

    lax.fori_loop(0, 8, see, 0)

    tick(*PLAN["start"][5:])
    scatter_patches(pstage, prow, psend, precv, own, "wait")
    for copy in vec_copies:
        copy.wait()
    place_in = lax.broadcasted_iota(jnp.int32, (HALF, 1), 0) % (IMG_GROUP + 2)
    parts = []
    for a in range(4):
        s = (a - t) % 4
        picture = dot_nt(prow[...].reshape(HALF, D), buf[s, 0:192]) + vec[s, 2:3, 0:192]
        language = dot_nt(word[...], buf[s, 192:384]) + vec[s, 3:4, 0:192]
        mark = vec[s, 4:5, 0:192]
        part = jnp.where(place_in < IMG_GROUP, picture, jnp.where(place_in == IMG_GROUP, language, mark))
        parts.append(part.astype(BF).astype(F32))
    xs[0] = jnp.concatenate(parts, axis=1)
    save(0, prow, patch_out)
    save(1, vec, vec_out)

    for which in range(NL):
        base = STEM + which * LAYER
        k0 = 20 + 9 * which
        save(k0, xs.at[which], xs_out.at[which])
        tick(*PLAN[which, "in"])
        norm_rows(xs.at[which], gain[which : which + 1], gain[2 + which : 3 + which], nrm.at[which])

        def project(s, carry):
            triple = dot_nt(buf[s, base : base + 576], nrm[which])
            tri[which, s] = triple.astype(BF)
            remote(
                tri.at[which, s, pl.ds(192, 384)],
                kvo.at[which, s],
                ksend.at[which, s],
                krecv.at[which, s],
                sibling(),
            ).start()
            return carry

        lax.fori_loop(0, 4, project, 0)
        save(k0 + 1, nrm.at[which], nrm_out.at[which])
        save(k0 + 2, tri.at[which], tri_out.at[which])
        mid[which] = xs[which]

        def attend(s, carry):
            remote(
                tri.at[which, s, pl.ds(192, 384)],
                kvo.at[which, s],
                ksend.at[which, s],
                krecv.at[which, s],
                sibling(),
            ).wait_recv()
            for h in range(3):
                at = 64 * h
                q = tri[which, s, at : at + 64] * jnp.asarray(HEAD_DIM**-0.5, BF)
                one = dot_tn(tri[which, s, 192 + at : 256 + at], q) + bias[0:256]
                two = dot_tn(kvo[which, s, at : at + 64], q) + bias[256:512]
                top = jnp.maximum(jnp.max(one, axis=0, keepdims=True), jnp.max(two, axis=0, keepdims=True))
                one = jnp.exp(one - top)
                two = jnp.exp(two - top)
                total = jnp.sum(one, axis=0, keepdims=True) + jnp.sum(two, axis=0, keepdims=True)
                lse[which, s, h : h + 1] = top + jnp.log(total)
                scale = 1.0 / total
                one = (one * scale).astype(BF)
                two = (two * scale).astype(BF)
                mixed = dot_nn(tri[which, s, 384 + at : 448 + at], one)
                mixed = mixed + dot_nn(kvo[which, s, 192 + at : 256 + at], two)
                mix[which, s, at : at + 64] = mixed.astype(BF)
            mid[which] += dot_tn(mix[which, s], buf[s, base + 576 : base + 768])
            return carry

        tick(*PLAN[which, "att0"])
        lax.fori_loop(0, 2, attend, 0)
        tick(*PLAN[which, "att1"])
        lax.fori_loop(2, 4, attend, 0)
        save(k0 + 3, kvo.at[which], kvo_out.at[which])
        save(k0 + 4, mix.at[which], mix_out.at[which])
        save(k0 + 5, lse.at[which], lse_out.at[which])
        save(k0 + 6, mid.at[which], mid_out.at[which])
        norm_rows(mid.at[which], gain[4 + which : 5 + which], gain[6 + which : 7 + which], fn.at[which])
        tick(*PLAN[which, "up"])

        def lift(s, carry):
            pre[which, s] = dot_nn(fn[which], buf[s, base + 768 : base + 1536]) + vec[s, which : which + 1]
            return carry

        save(k0 + 7, fn.at[which], fn_out.at[which])
        lax.fori_loop(0, 4, lift, 0)
        save(k0 + 8, pre.at[which], pre_out.at[which])
        xs[which + 1] = mid[which]
        tick(*PLAN[which, "down"])

        def lower(s, carry):
            def body(rows):
                x = pre[which, s, rows]
                hid[rows] = (0.5 * x * (1.0 + jnp.tanh(GELU_A * (x + GELU_B * x * x * x)))).astype(BF)

            row_blocks(HALF, body)
            xs[which + 1] += dot_nn(hid[...], buf[s, base + 1536 : base + 2304])
            return carry

        lax.fori_loop(0, 4, lower, 0)

    flipped = xs[2].astype(BF).T
    for a in range(4):
        act[a] = flipped[192 * a : 192 * a + 192]
    save(13, act, act_out)
    for which in range(NL):
        for s in range(4):
            remote(
                tri.at[which, s, pl.ds(192, 384)],
                kvo.at[which, s],
                ksend.at[which, s],
                krecv.at[which, s],
                sibling(),
            ).wait_send()
    for unit in range(6):
        g.finish(unit)
    for copy in saves:
        copy.wait()


def forward_call(*args):
    any_ = pl.BlockSpec(memory_space=pl.ANY)
    sds = jax.ShapeDtypeStruct
    shapes = [
        ((4, ROWS, D), BF),
        ((4, 64, D), BF),
        ((4, 8, D), F32),
        ((2, HALF, D), F32),
        ((2, HALF, D), F32),
        ((2, HALF, D), BF),
        ((2, HALF, D), BF),
        ((2, 4, 576, HALF), BF),
        ((2, 4, 384, HALF), BF),
        ((2, 4, 192, HALF), BF),
        ((2, 4, 8, HALF), F32),
        ((2, 4, HALF, D), F32),
        ((4, 192, HALF), BF),
    ]
    dma = pltpu.SemaphoreType.DMA
    return pl.pallas_call(
        gather_kernel,
        out_shape=tuple(sds(s, d) for s, d in shapes),
        in_specs=[any_] * 12,
        out_specs=(any_,) * len(shapes),
        scratch_shapes=[
            pltpu.VMEM((4, ROWS, D), BF),
            pltpu.VMEM((4, 8, D), F32),
            pltpu.VMEM((8, D), F32),
            pltpu.VMEM((8, HALF), jnp.int32),
            pltpu.VMEM((L, 128), jnp.int32),
            pltpu.VMEM((4, 64, D), BF),
            pltpu.VMEM((4, 64, D), BF),
            pltpu.VMEM((HALF, D), BF),
            pltpu.VMEM((3, HALF, D), F32),
            pltpu.VMEM((2, HALF, D), F32),
            pltpu.VMEM((2, HALF, D), BF),
            pltpu.VMEM((2, HALF, D), BF),
            pltpu.VMEM((2, 4, 576, HALF), BF),
            pltpu.VMEM((2, 4, 384, HALF), BF),
            pltpu.VMEM((2, 4, 192, HALF), BF),
            pltpu.VMEM((2, 4, 8, HALF), F32),
            pltpu.VMEM((2, 4, HALF, D), F32),
            pltpu.VMEM((4, 192, HALF), BF),
            pltpu.VMEM((L, HALF), F32),
            pltpu.VMEM((HALF, D), BF),
            pltpu.VMEM((7, 16, D), BF),
            dma((23,)),
            dma((6, 27)),
            dma((6, 27)),
            dma((4,)),
            dma((4,)),
            dma,
            dma((3,)),
            dma((3,)),
            dma((2, 4)),
            dma((2, 4)),
            dma((38,)),
        ],
        compiler_params=pltpu.CompilerParams(
            collective_id=0, has_side_effects=True, vmem_limit_bytes=63 * 2**20
        ),
    )(*args)


def prepare(
    patches,
    text_features,
    patch_weight,
    patch_bias,
    text_weight,
    text_bias,
    readout,
    mix_gain,
    mix_shift,
    heads_in_weight,
    heads_out_weight,
    feed_gain,
    feed_shift,
    up_weight,
    up_bias,
    down_weight,
    timesteps,
):
    t = lax.axis_index("tensor")
    c = lax.axis_index("ctx")
    wide = lambda v: jnp.pad(v.astype(F32), (0, D - DEV))[None]
    vectors = jnp.concatenate(
        [up_bias, wide(patch_bias), wide(text_bias), wide(readout), jnp.zeros((3, D), F32)], axis=0
    )
    gains = jnp.concatenate([mix_gain, mix_shift, feed_gain, feed_shift], axis=0)
    stamps = lax.dynamic_slice_in_dim(timesteps, t, 1, 0).reshape(2, HALF)
    mine = lax.dynamic_slice_in_dim(stamps, c, 1, 0)
    other = lax.dynamic_slice_in_dim(stamps, 1 - c, 1, 0)
    stamps_q = jnp.broadcast_to(mine, (8, HALF))
    stamps_k = jnp.broadcast_to(jnp.concatenate([mine, other], 1).reshape(L, 1), (L, 128))
    spaced = lax.dynamic_slice_in_dim(patches, t * 240, 240, 0).reshape(4, 2, IMG_GROUP, D)
    spaced = jnp.pad(spaced, ((0, 0), (0, 0), (0, 2), (0, 0))).reshape(4, 64, D)
    words = lax.dynamic_slice_in_dim(text_features, t, 1, 0).reshape(8, 1, D)
    words = jnp.pad(words, ((0, 0), (IMG_GROUP, 1), (0, 0))).reshape(HALF, D)
    return (
        patch_weight.T,
        text_weight.T,
        heads_in_weight.transpose(0, 2, 3, 1).reshape(NL, 3 * DEV, D),
        heads_out_weight,
        up_weight,
        down_weight,
        vectors,
        gains,
        stamps_q,
        stamps_k,
        spaced,
        words,
    )


SUM_UNITS = [
    (256, 512, "z"),
    (768, 0, "z"),
    (256, 512, "y"),
    (256, 512, "z"),
    (768, 0, "z"),
    (256, 512, "y"),
    (0, 512, "z"),
]
SUM_BASE = [768, 2304, 3840, 0, 1536, 3072, 4608]
NU = len(SUM_UNITS)
STEMS = 6


class Sums:
    def __init__(self, grads, core_in, big, small, out, send, recv, local, credit):
        self.grads, self.core_in, self.big, self.small = grads, core_in, big, small
        self.out, self.send, self.recv, self.local, self.credit = out, send, recv, local, credit

    def where(self, u):
        nx, npl, slow = SUM_UNITS[u]
        z, y, c, t = place()
        fast = "y" if slow == "z" else "z"
        m = lambda v: pl.multiple_of(v, 16)
        return nx // 2, npl // 2, nx + c * (npl // 2), slow, fast, {"z": z, "y": y}, c, t, m

    def copy(self, u, sem, src, dst, device):
        return remote(src, dst, self.send.at[u, sem], self.recv.at[u, sem], device)

    def core(self, u, s):
        n, p, _, slow, fast, at, c, t, m = self.where(u)
        g, into = self.grads.at[u % 3], self.core_in.at[u % 2]
        out = []
        if n:
            src = g.at[s, pl.ds(m((1 - c) * n), n)]
            out.append(self.copy(u, s, src, into.at[s, pl.ds(0, n)], sibling()))
        if p:
            src = g.at[s, pl.ds(m(2 * n + (1 - c) * p), p)]
            out.append(self.copy(u, 4 + s, src, into.at[s, pl.ds(n, p)], sibling()))
        return out

    def begin(self, u):
        if u >= 2:
            pl.semaphore_wait(self.credit, 1)

    def give(self, u, s):
        for copy in self.core(u, s):
            copy.start()

    def cores(self, u):
        return [copy for s in range(4) for copy in self.core(u, s)]

    def across(self, u):
        n, p, row, slow, fast, at, c, t, m = self.where(u)
        g, big = self.grads.at[u % 3], self.big[u % 3]
        out = []
        if n:
            h = n // 2
            out.append(self.copy(u, 8, g.at[2, pl.ds(m(c * n), h)], big["xa"].at[0], peer("x", 1)))
            out.append(self.copy(u, 9, g.at[2, pl.ds(m(c * n + h), h)], big["xa"].at[1], peer("x", -1)))
        if p:
            block = row + (at[slow] + 2) % 4 * 64
            out.append(self.copy(u, 10, g.at[:, pl.ds(m(block), 32)], big["pa"].at[0], peer(slow, 1)))
            out.append(self.copy(u, 11, g.at[:, pl.ds(m(block + 32), 32)], big["pa"].at[1], peer(slow, -1)))
        return out

    def beside(self, u):
        n, p, row, slow, fast, at, c, t, m = self.where(u)
        g, big = self.grads.at[u % 3], self.big[u % 3]
        out = []
        if n:
            rows = pl.ds(m(c * n), n)
            out.append(self.copy(u, 12, g.at[1, rows], big["xr"].at[0], peer("x", 1)))
            out.append(self.copy(u, 13, g.at[3, rows], big["xr"].at[1], peer("x", -1)))
        if p:
            for k, r in ((0, 1), (1, 3)):
                block = row + (at[slow] + r) % 4 * 64
                out.append(self.copy(u, 14 + k, g.at[:, pl.ds(m(block), 64)], big["pr"].at[k], peer(slow, r)))
        return out

    def second(self, u):
        n, p, row, slow, fast, at, c, t, m = self.where(u)
        big, small = self.big[u % 3], self.small[u]
        out = []
        for r in (1, 2, 3):
            if n:
                block = pl.ds(m((at["y"] + r) % 4 * (n // 4)), n // 4)
                out.append(self.copy(u, 15 + r, big["xs"].at[block], small["yr"].at[r - 1], peer("y", r)))
            if p:
                block = pl.ds(m((at[fast] + r) % 4 * 16), 16)
                out.append(self.copy(u, 18 + r, big["ps"].at[:, block], small["qr"].at[r - 1], peer(fast, r)))
        return out

    def third(self, u):
        n, p, row, slow, fast, at, c, t, m = self.where(u)
        small = self.small[u]
        out = []
        for r in (1, 2, 3):
            if n:
                mine = small["zb"].at[at["z"]]
                out.append(self.copy(u, 21 + r, mine, mine, peer("z", r)))
            if p:
                out.append(self.copy(u, 24 + r, small["qs"].at[r], small["tr"].at[r - 1], peer("x", r)))
        return out

    def rows(self, u):
        n, p, row, slow, fast, at, c, t, m = self.where(u)
        base = SUM_BASE[u]
        return (
            pl.ds(m(base + c * n), n),
            pl.ds(m(base + c * n + at["y"] * (n // 4)), n // 4),
            pl.ds(m(base + row), p),
            pl.ds(m(base + row + at[slow] * 64), 64),
            pl.ds(m(base + row + at[slow] * 64 + at[fast] * 16), 16),
        )

    def fourth(self, u):
        n, p, row, slow, fast, at, c, t, m = self.where(u)
        small = self.small[u]
        _, x_own, _, _, p_own = self.rows(u)
        out = []
        for r in (1, 2, 3):
            if n:
                out.append(self.copy(u, 27 + r, small["fx"], self.out.at[x_own], peer("y", r)))
            if p:
                out.append(self.copy(u, 30 + r, small["fp"], self.out.at[p_own], peer(fast, r)))
        return out

    def own(self, u):
        n, p = self.where(u)[:2]
        _, x_own, _, _, p_own = self.rows(u)
        out = []
        if n:
            out.append(pltpu.make_async_copy(self.small[u]["fx"], self.out.at[x_own], self.local.at[u, 0]))
        if p:
            out.append(pltpu.make_async_copy(self.small[u]["fp"], self.out.at[p_own], self.local.at[u, 1]))
        return out

    def fifth(self, u):
        n, p, row, slow, fast, at, c, t, m = self.where(u)
        if not p:
            return []
        region = self.out.at[self.rows(u)[3]]
        return [self.copy(u, 33 + r, region, region, peer(slow, r)) for r in (1, 2, 3)]

    def sixth(self, u):
        n, p = self.where(u)[:2]
        x_all, _, p_all, _, _ = self.rows(u)
        out = []
        if n:
            region = self.out.at[x_all]
            out.append(self.copy(u, 37, region, region, sibling()))
        if p:
            region = self.out.at[p_all]
            out.append(self.copy(u, 38, region, region, sibling()))
        return out

    def add(self, u, count, size, terms, result):
        def step(i, carry):
            total = None
            for ref, index in terms(i):
                v = ref[index].astype(F32)
                total = v if total is None else total + v
            ref, index = result(i)
            ref[index] = total.astype(BF)
            return carry

        if count == 1:
            step(0, 0)
        else:
            lax.fori_loop(0, count, step, 0)

    def step(self, k, u):
        n, p, row, slow, fast, at, c, t, m = self.where(u)
        g, big, small = self.grads.at[u % 3], self.big[u % 3], self.small[u]
        if k == 1:
            for copy in self.cores(u):
                copy.wait_recv()
            for first, there, rows in ((c * n, 0, n), (row, n, p)):
                if rows:
                    per = rows // 128
                    mine = lambda i: (g, (i // per, pl.ds(m(first + i % per * 128), 128)))
                    its = lambda i: (self.core_in.at[u % 2], (i // per, pl.ds(m(there + i % per * 128), 128)))
                    self.add(u, 4 * per, 128, lambda i: [mine(i), its(i)], mine)
            if u + 2 < NU:
                pl.semaphore_signal(self.credit, inc=1, device_id=sibling(), device_id_type=MESH)
            for copy in self.across(u):
                copy.start()
        if k == 2:
            for copy in self.across(u):
                copy.wait_recv()
            if n:
                h = n // 2
                for k, slot, first in ((0, 1, c * n), (1, 3, c * n + h)):
                    mine = lambda i: (g, (slot, pl.ds(m(first + i * 64), 64)))
                    its = lambda i: (big["xa"], (k, pl.ds(m(i * 64), 64)))
                    self.add(u, h // 64, 64, lambda i: [mine(i), its(i)], mine)
            if p:
                for k, r in ((0, 1), (1, 3)):
                    first = row + (at[slow] + r) % 4 * 64 + 32 * k
                    mine = lambda i: (g, (i, pl.ds(m(first), 32)))
                    its = lambda i: (big["pa"], (k, i))
                    self.add(u, 4, 32, lambda i: [mine(i), its(i)], mine)
            for copy in self.beside(u):
                copy.start()
        if k == 3:
            for copy in self.beside(u):
                copy.wait_recv()
            if n:
                self.add(
                    u,
                    n // 64,
                    64,
                    lambda i: [(g, (0, pl.ds(m(c * n + i * 64), 64)))]
                    + [(big["xr"], (r, pl.ds(m(i * 64), 64))) for r in range(2)],
                    lambda i: (big["xs"], pl.ds(m(i * 64), 64)),
                )
            if p:
                first = row + at[slow] * 64
                self.add(
                    u,
                    4,
                    64,
                    lambda i: [(g, (i, pl.ds(m(first), 64)))] + [(big["pr"], (r, i)) for r in range(2)],
                    lambda i: (big["ps"], i),
                )
            for copy in self.second(u):
                copy.start()
            for copy in self.cores(u) + self.across(u) + self.beside(u):
                copy.wait_send()
        if k == 4:
            for copy in self.second(u):
                copy.wait_recv()
            if n:
                own = pl.ds(m(at["y"] * (n // 4)), n // 4)
                self.add(
                    u,
                    1,
                    n // 4,
                    lambda i: [(big["xs"], own)] + [(small["yr"], r) for r in range(3)],
                    lambda i: (small["zb"], at["z"]),
                )
            if p:
                own = pl.ds(m(at[fast] * 16), 16)
                self.add(
                    u,
                    4,
                    16,
                    lambda i: [(big["ps"], (i, own))] + [(small["qr"], (r, i)) for r in range(3)],
                    lambda i: (small["qs"], i),
                )
            for copy in self.third(u):
                copy.start()
            for copy in self.second(u):
                copy.wait_send()
        if k == 5:
            for copy in self.third(u):
                copy.wait_recv()
            if n:
                self.add(
                    u, 1, n // 4, lambda i: [(small["zb"], r) for r in range(4)], lambda i: (small["fx"], slice(None))
                )
            if p:
                self.add(
                    u,
                    1,
                    16,
                    lambda i: [(small["qs"], 0)] + [(small["tr"], r) for r in range(3)],
                    lambda i: (small["fp"], slice(None)),
                )
            for copy in self.fourth(u) + self.own(u):
                copy.start()
        if k == 6:
            for copy in self.fourth(u):
                copy.wait_recv()
            for copy in self.own(u):
                copy.wait()
            for copy in self.fifth(u) if p else self.sixth(u):
                copy.start()
        if k == 7 and p:
            for copy in self.fifth(u):
                copy.wait_recv()
            for copy in self.sixth(u):
                copy.start()
        if k == 8:
            for copy in self.sixth(u):
                copy.wait_recv()
            for copy in self.third(u) + self.fourth(u) + self.fifth(u) + self.sixth(u):
                copy.wait_send()


def big_shapes():
    out = []
    for nx, npl, _ in SUM_UNITS[:3]:
        n, p = nx // 2, npl // 2
        shapes = {}
        if n:
            shapes |= {"xa": (2, n // 2, D), "xr": (2, n, D), "xs": (n, D)}
        if p:
            shapes |= {"pa": (2, 4, 32, D), "pr": (2, 4, 64, D), "ps": (4, 64, D)}
        out.append(shapes)
    return out


def small_shapes():
    out = []
    for nx, npl, _ in SUM_UNITS:
        q = nx // 8
        shapes = {}
        if nx:
            shapes |= {"yr": (3, q, D), "zb": (4, q, D), "fx": (q, D)}
        if npl:
            shapes |= {"qr": (3, 4, 16, D), "qs": (4, 16, D), "tr": (3, 16, D), "fp": (16, D)}
        out.append(shapes)
    return out


def norm_back(x, grad, base, gain, out, sums, gain_row, shift_row):
    zero = jnp.zeros((1, D), F32)
    sums[gain_row : gain_row + 1] = zero
    sums[shift_row : shift_row + 1] = zero

    def body(rows):
        v = x[rows]
        g = grad[rows]
        mean = jnp.mean(v, axis=-1, keepdims=True)
        centred = v - mean
        spread = jnp.mean(centred * centred, axis=-1, keepdims=True)
        inv = lax.rsqrt(spread + EPS)
        hat = centred * inv
        sums[gain_row : gain_row + 1] += jnp.sum(g * hat, axis=0, keepdims=True)
        sums[shift_row : shift_row + 1] += jnp.sum(g, axis=0, keepdims=True)
        d = g * gain
        first = jnp.mean(d, axis=-1, keepdims=True)
        second = jnp.mean(d * hat, axis=-1, keepdims=True)
        out[rows] = base[rows] + inv * (d - first - hat * second)

    row_blocks(HALF, body)


def returns(act, act_out, pgs, pg_out, tgs, tg_out, send, recv, own, mode, which):
    z, y, c, t = place()
    d = z * 4 + y
    if which == 0:
        for r in (1, 2, 3):
            a = (t + r) % 4
            copy = remote(act.at[a], act_out.at[t], send.at[r], recv.at[r], (d, c, a))
            copy.start() if mode == "start" else copy.wait()
        copy = pltpu.make_async_copy(act.at[t], act_out.at[t], own.at[0])
        copy.start() if mode == "start" else copy.wait()
        return
    for r in (1, 2, 3):
        a = (t + r) % 4
        copy = remote(tgs.at[a], tg_out.at[t], send.at[4 + r], recv.at[4 + r], (d, c, a))
        copy.start() if mode == "start" else copy.wait()
    copy = pltpu.make_async_copy(tgs.at[t], tg_out.at[t], own.at[1])
    copy.start() if mode == "start" else copy.wait()

    def each(i, carry):
        a, yy = i % 4, i // 4
        to_me = (t == z) & (yy == y) & (a == t)
        src = pgs.at[a, pl.ds(pl.multiple_of(yy * 64, 64), 64)]
        local = pltpu.make_async_copy(src, pg_out.at[d], own.at[2])
        away = remote(src, pg_out.at[d], send.at[8 + i], recv.at[8 + d], (t * 4 + yy, c, a))

        @pl.when(to_me)
        def _():
            local.start() if mode == "start" else local.wait()

        @pl.when(jnp.logical_not(to_me))
        def _():
            away.start() if mode == "start" else away.wait_send()

        return carry

    lax.fori_loop(0, 16, each, 0)
    if mode == "wait":

        def arrive(i, carry):
            from_me = (t == z) & (i == d)

            @pl.when(jnp.logical_not(from_me))
            def _():
                remote(pg_out.at[i], pg_out.at[i], send.at[8 + i], recv.at[8 + i], (i, c, z)).wait_recv()

            return carry

        lax.fori_loop(0, 16, arrive, 0)


SUM_PLAN = {
    (1, "down"): [(1, 0)],
    (1, "up"): [(2, 0), (1, 1)],
    (1, "att1"): [],
    (1, "att2"): [(3, 0), (2, 1)],
    (1, "in"): [(1, 2), (4, 0)],
    (0, "down"): [(1, 3), (5, 0), (2, 2), (3, 1)],
    (0, "up"): [(2, 3), (1, 4), (6, 0), (3, 2)],
    (0, "att1"): [(4, 1), (2, 4), (3, 3), (7, 0)],
    (0, "att2"): [(4, 2), (5, 1)],
    (0, "in"): [(1, 5), (3, 4), (4, 3), (6, 1), (5, 2)],
    "stem": [(1, 6), (2, 5), (4, 4), (2, 6), (5, 3), (6, 2)],
    "end": [
        (3, 5), (3, 6), (5, 4), (4, 5), (4, 6), (5, 5), (5, 6), (7, 2), (6, 3), (6, 4), (6, 5), (6, 6), (7, 3), (7, 5),
        (7, 6),
    ],
}


def backward_kernel(
    w_in,
    patch_in,
    xs_in,
    mid_in,
    nrm_in,
    fn_in,
    tri_in,
    kvo_in,
    mix_in,
    lse_in,
    pre_in,
    act_in,
    gains,
    stamps_q,
    stamps_k,
    words,
    cotangent,
    row_scale,
    out,
    act_out,
    pg_out,
    tg_out,
    wb,
    gain,
    stamp_q,
    stamp_k,
    prow,
    word,
    cot,
    rscale,
    xs,
    mid,
    nrm,
    fn,
    tri,
    kvo,
    mix,
    lse,
    pre,
    bias,
    up,
    low,
    back,
    hgrad,
    hid,
    pgrad,
    fnt,
    kvg,
    kvs,
    rkv,
    tgrad,
    sums,
    vec,
    pgs,
    tgs,
    grads,
    core_in,
    big,
    small,
    wsem,
    psem,
    lsem,
    send,
    recv,
    local,
    credit,
    ksend,
    krecv,
    rsend,
    rrecv,
    rown,
):
    z, y, c, t = place()
    copy_in = pltpu.make_async_copy

    def section(row, rows, s):
        return copy_in(w_in.at[s, pl.ds(row, rows)], wb.at[s, pl.ds(0, rows)], wsem.at[s])

    sections = []
    for which in (1, 0):
        base = STEM + which * LAYER
        sections += [(base + 1536, 768), (base + 768, 768), (base, 768)]
    sections.append((0, STEM))

    def kept_pre(which, s):
        return copy_in(pre_in.at[which, s], pre.at[s], psem.at[s])

    def acts(which):
        return [
            copy_in(fn_in.at[which], fn, lsem.at[1]),
            copy_in(mid_in.at[which], mid, lsem.at[2]),
            copy_in(tri_in.at[which], tri, lsem.at[3]),
            copy_in(kvo_in.at[which], kvo, lsem.at[4]),
            copy_in(mix_in.at[which], mix, lsem.at[5]),
            copy_in(lse_in.at[which], lse, lsem.at[6]),
            copy_in(nrm_in.at[which], nrm, lsem.at[7]),
            copy_in(xs_in.at[which], xs, lsem.at[8]),
        ]

    head = [
        copy_in(cotangent.at[t], cot, lsem.at[9]),
        copy_in(row_scale, rscale, lsem.at[10]),
    ]
    for copy in head:
        copy.start()
    for s in range(4):
        section(*sections[0], s).start()
    for s in range(4):
        kept_pre(1, s).start()
    for copy in acts(1):
        copy.start()
    rest = [
        copy_in(gains, gain, lsem.at[11]),
        copy_in(stamps_q, stamp_q, lsem.at[12]),
        copy_in(stamps_k, stamp_k, lsem.at[13]),
        copy_in(patch_in, prow, lsem.at[14]),
        copy_in(words, word, lsem.at[15]),
    ]
    for copy in rest:
        copy.start()
    greet("out")
    returns(act_in, act_out, pgs, pg_out, tgs, tg_out, rsend, rrecv, rown, "start", 0)
    total = Sums(grads, core_in, big, small, out, send, recv, local, credit)

    def comm(key):
        for k, u in SUM_PLAN[key]:
            total.step(k, u)

    for copy in head:
        copy.wait()

    def first_up(rows):
        up[rows] = cot[rows].astype(F32) * rscale[rows, 0:1]

    row_blocks(HALF, first_up)
    vec[...] = jnp.zeros_like(vec)
    sums[...] = jnp.zeros_like(sums)
    for copy in rest:
        copy.wait()

    def see(i, carry):
        rows = pl.ds(pl.multiple_of(i * 64, 64), 64)
        bias[rows] = jnp.where(stamp_k[rows, 0:1] <= stamp_q[0:1, :], 0.0, MASKED)
        return carry

    lax.fori_loop(0, 8, see, 0)

    for which in (1, 0):
        u0 = 0 if which else 3
        loads = [None] + acts(which)

        def round_up(rows):
            low[rows] = up[rows].astype(BF)

        row_blocks(HALF, round_up)
        b = u0 % 3
        after = sections[u0 + 1]

        def down(s, carry):
            section(*sections[u0], s).wait()
            hgrad[...] = dot_nt(low[...], wb[s])
            section(*after, s).start()

            def body(rows):
                x = pre[s, rows]
                th = jnp.tanh(GELU_A * (x + GELU_B * x * x * x))
                hid[rows] = (0.5 * x * (1.0 + th)).astype(BF)
                slope = 0.5 * (1.0 + th) + 0.5 * x * (1.0 - th * th) * (GELU_A * (1.0 + 3.0 * GELU_B * x * x))
                pgrad[s, rows] = (hgrad[rows] * slope).astype(BF)

            row_blocks(HALF, body)
            for j in range(3):
                grads[b, s, 256 * j : 256 * j + 256] = dot_tn(hid[:, 256 * j : 256 * j + 256], low[...]).astype(BF)
            total.give(u0, s)
            vec[s, which : which + 1] = jnp.sum(pgrad[s].astype(F32), axis=0, keepdims=True)
            return carry

        for s in range(4):
            kept_pre(which, s).wait()
        total.begin(u0)
        lax.fori_loop(0, 4, down, 0)
        if which:
            for s in range(4):
                kept_pre(0, s).start()
        comm((which, "down"))

        b = (u0 + 1) % 3
        after = sections[u0 + 2]
        loads[1].wait()
        fnt[...] = fn[...].T
        back[...] = jnp.zeros_like(back)

        def lift(s, carry):
            section(*sections[u0 + 1], s).wait()
            back[...] += dot_nt(pgrad[s], wb[s])
            section(*after, s).start()
            for j in range(3):
                grads[b, s, 256 * j : 256 * j + 256] = dot_nn(fnt[256 * j : 256 * j + 256], pgrad[s]).astype(BF)
            total.give(u0 + 1, s)
            return carry

        total.begin(u0 + 1)
        lax.fori_loop(0, 4, lift, 0)
        if which:
            acts(0)[0].start()
        comm((which, "up"))

        loads[2].wait()
        norm_back(mid, back, up, gain[4 + which : 5 + which], up, sums, 6 + which, 8 + which)
        if which:
            acts(0)[1].start()
        row_blocks(HALF, round_up)
        for k in (3, 4, 5, 6):
            loads[k].wait()
        b = (u0 + 2) % 3
        after = sections[u0 + 3]

        def share(s):
            return remote(kvs.at[which, s], rkv.at[which, s], ksend.at[which, s], krecv.at[which, s], sibling())

        def attend(s, carry):
            section(*sections[u0 + 2], s).wait()
            grads[b, s, 576:768] = dot_nn(mix[s], low[...]).astype(BF)
            mixed = dot_nt(wb[s, 576:768], low[...]).astype(BF)
            for h in range(3):
                at = 64 * h
                q = tri[s, at : at + 64] * jnp.asarray(HEAD_DIM**-0.5, BF)
                do = mixed[at : at + 64]
                k1, v1 = tri[s, 192 + at : 256 + at], tri[s, 384 + at : 448 + at]
                k2, v2 = kvo[s, at : at + 64], kvo[s, 192 + at : 256 + at]
                log_total = lse[s, h : h + 1]
                p1 = jnp.exp(dot_tn(k1, q) + bias[0:256] - log_total)
                p2 = jnp.exp(dot_tn(k2, q) + bias[256:512] - log_total)
                d1 = dot_tn(v1, do)
                d2 = dot_tn(v2, do)
                delta = jnp.sum(p1 * d1, axis=0, keepdims=True) + jnp.sum(p2 * d2, axis=0, keepdims=True)
                g1 = (p1 * (d1 - delta)).astype(BF)
                g2 = (p2 * (d2 - delta)).astype(BF)
                dq = (dot_nn(k1, g1) + dot_nn(k2, g2)) * HEAD_DIM**-0.5
                tgrad[s, at : at + 64] = dq.astype(BF)
                kvg[s, at : at + 64] = dot_nt(q, g1)
                kvs[which, s, at : at + 64] = dot_nt(q, g2).astype(BF)
                kvg[s, 192 + at : 256 + at] = dot_nt(do, p1.astype(BF))
                kvs[which, s, 192 + at : 256 + at] = dot_nt(do, p2.astype(BF)).astype(BF)
            share(s).start()
            return carry

        lax.fori_loop(0, 2, attend, 0)
        comm((which, "att1"))
        lax.fori_loop(2, 4, attend, 0)
        if which:
            for k in (3, 4, 5, 6):
                acts(0)[k - 1].start()
        comm((which, "att2"))
        loads[7].wait()
        back[...] = jnp.zeros_like(back)

        def lead(s, carry):
            share(s).wait_recv()
            tgrad[s, 192:576] = (kvg[s] + rkv[which, s].astype(F32)).astype(BF)
            grads[b, s, 0:576] = dot_nn(tgrad[s], nrm[...]).astype(BF)
            total.give(u0 + 2, s)
            back[...] += dot_tn(tgrad[s], wb[s, 0:576])
            section(*after, s).start()
            return carry

        total.begin(u0 + 2)
        lax.fori_loop(0, 4, lead, 0)
        if which:
            acts(0)[6].start()
        comm((which, "in"))
        loads[8].wait()
        norm_back(xs, back, up, gain[which : which + 1], up, sums, 2 + which, 4 + which)
        if which:
            acts(0)[7].start()

    row_blocks(HALF, round_up)
    place_in = lax.broadcasted_iota(jnp.int32, (HALF, 1), 0) % (IMG_GROUP + 2)
    rounded = low[...].astype(F32)
    sums[10:11] = jnp.sum(jnp.where(place_in < IMG_GROUP, rounded, 0.0), axis=0, keepdims=True)
    sums[11:12] = jnp.sum(jnp.where(place_in == IMG_GROUP, rounded, 0.0), axis=0, keepdims=True)
    sums[12:13] = jnp.sum(jnp.where(place_in > IMG_GROUP, up[...], 0.0), axis=0, keepdims=True)
    fnt[...] = low[...].T
    b = STEMS % 3
    back[...] = jnp.zeros_like(back)
    hgrad[...] = jnp.zeros_like(hgrad)
    total.begin(STEMS)
    for a in range(4):
        s = (a - t) % 4
        section(*sections[6], s).wait()
        mine = fnt[192 * a : 192 * a + 192]
        grads[b, s, 0:192] = dot_nn(mine, prow[...].reshape(HALF, D)).astype(BF)
        grads[b, s, 192:384] = dot_nn(mine, word[...]).astype(BF)
        vec[s, 2:16] = sums[2:16]
        grads[b, s, 384:400] = vec[s].astype(BF)
        grads[b, s, 400:512] = jnp.zeros((112, D), BF)
        back[...] += dot_tn(mine, wb[s, 0:192])
        hgrad[...] += dot_tn(mine, wb[s, 192:384])
    for s in range(4):
        total.give(STEMS, s)
    comm("stem")
    for a in range(4):
        pgs[a] = back[:, 192 * a : 192 * a + 192].astype(BF)
    for h in range(8):
        row = hgrad[32 * h + 30 : 32 * h + 31]
        for a in range(4):
            tgs[a, h : h + 1] = row[:, 192 * a : 192 * a + 192]
    returns(act_in, act_out, pgs, pg_out, tgs, tg_out, rsend, rrecv, rown, "start", 1)
    comm("end")
    returns(act_in, act_out, pgs, pg_out, tgs, tg_out, rsend, rrecv, rown, "wait", 0)
    returns(act_in, act_out, pgs, pg_out, tgs, tg_out, rsend, rrecv, rown, "wait", 1)
    for which in range(NL):
        for s in range(4):
            remote(kvs.at[which, s], rkv.at[which, s], ksend.at[which, s], krecv.at[which, s], sibling()).wait_send()
    for u in range(NU):
        total.step(8, u)


def backward_call(*args):
    any_ = pl.BlockSpec(memory_space=pl.ANY)
    sds = jax.ShapeDtypeStruct
    dma = pltpu.SemaphoreType.DMA
    v = pltpu.VMEM
    return pl.pallas_call(
        backward_kernel,
        out_shape=(
            sds((6 * D + 512, D), BF),
            sds((4, 192, HALF), BF),
            sds((16, 64, 192), BF),
            sds((4, 8, 192), F32),
        ),
        in_specs=[any_] * 18,
        out_specs=(any_,) * 4,
        scratch_shapes=[
            v((4, D, D), BF),
            v((8, D), F32),
            v((8, HALF), jnp.int32),
            v((L, 128), jnp.int32),
            v((4, 64, D), BF),
            v((HALF, D), BF),
            v((HALF, D), BF),
            v((HALF, 128), F32),
            v((HALF, D), F32),
            v((HALF, D), F32),
            v((HALF, D), BF),
            v((HALF, D), BF),
            v((4, 576, HALF), BF),
            v((4, 384, HALF), BF),
            v((4, 192, HALF), BF),
            v((4, 8, HALF), F32),
            v((4, HALF, D), F32),
            v((L, HALF), F32),
            v((HALF, D), F32),
            v((HALF, D), BF),
            v((HALF, D), F32),
            v((HALF, D), F32),
            v((HALF, D), BF),
            v((4, HALF, D), BF),
            v((D, HALF), BF),
            v((4, 384, HALF), F32),
            v((2, 4, 384, HALF), BF),
            v((2, 4, 384, HALF), BF),
            v((4, 576, HALF), BF),
            v((16, D), F32),
            v((4, 16, D), F32),
            v((4, HALF, DEV), BF),
            v((4, 8, DEV), F32),
            v((3, 4, D, D), BF),
            v((2, 4, 384, D), BF),
            [{k: v(shape, BF) for k, shape in shapes.items()} for shapes in big_shapes()],
            [{k: v(shape, BF) for k, shape in shapes.items()} for shapes in small_shapes()],
            dma((4,)),
            dma((4,)),
            dma((16,)),
            dma((NU, 39)),
            dma((NU, 39)),
            dma((NU, 2)),
            pltpu.SemaphoreType.REGULAR,
            dma((2, 4)),
            dma((2, 4)),
            dma((24,)),
            dma((24,)),
            dma((3,)),
        ],
        compiler_params=pltpu.CompilerParams(
            collective_id=1, has_side_effects=True, vmem_limit_bytes=63 * 2**20
        ),
    )(*args)


def shards(*args):
    (datasets, dataset_weights, action_mask, cotangent) = args[17:]
    t = lax.axis_index("tensor")
    ops = prepare(*args[:17])
    gains, stamps_q, stamps_k, words = ops[7], ops[8], ops[9], ops[11]
    kept = forward_call(*ops)
    mask = lax.dynamic_slice_in_dim(action_mask, t, 1, 0)[0]
    dataset = lax.dynamic_slice_in_dim(datasets, t, 1, 0)[0]
    weight = lax.dynamic_slice_in_dim(dataset_weights, dataset, 1, 0)[0]
    scale = weight.astype(F32) * mask.astype(F32)
    last = jnp.arange(IMG_GROUP + 2) == IMG_GROUP + 1
    row_scale = jnp.where(last[None, :], scale[:, None], 1.0).reshape(HALF, 1)
    row_scale = jnp.broadcast_to(row_scale, (HALF, 128))
    out, act, pg, tg = backward_call(
        kept[0], kept[1], *kept[3:], gains, stamps_q, stamps_k, words, cotangent, row_scale
    )
    part = lambda a, b: out[a:b].astype(F32)
    down_grad = part(0, 2 * D).reshape(NL, D, D)
    up_grad = part(2 * D, 4 * D).reshape(NL, D, D)
    heads = out[4 * D : 6 * D].reshape(NL, D, D)
    heads_in = heads[:, :576].astype(F32).reshape(NL, 3, DEV, D).transpose(0, 3, 1, 2)
    heads_out = heads[:, 576:].astype(F32)
    vectors = part(6 * D + 384, 6 * D + 400)
    own = lax.dynamic_slice_in_dim(vectors, t * DEV, DEV, 1)
    pg = pg.reshape(16, 2, IMG_GROUP + 2, DEV)[:, :, :IMG_GROUP].reshape(960, DEV).astype(F32)
    return (
        act.transpose(0, 2, 1),
        pg,
        tg,
        part(6 * D, 6 * D + 192).T,
        own[10],
        part(6 * D + 192, 6 * D + 384).T,
        own[11],
        own[12],
        own[2:4],
        own[4:6],
        heads_in,
        heads_out,
        own[6:8],
        own[8:10],
        up_grad,
        vectors[0:2],
        down_grad,
    )


def solution(mesh):
    in_specs = (
        P(("dp", "ctx"), None),
        P("dp", "ctx", None),
        P(None, "tensor"),
        P("tensor"),
        P(None, "tensor"),
        P("tensor"),
        P("tensor"),
        P(),
        P(),
        P(None, None, None, "tensor"),
        P(None, "tensor", None),
        P(),
        P(),
        P(None, None, "tensor"),
        P(None, "tensor"),
        P(None, "tensor", None),
        P("dp", None),
        P("dp"),
        P(),
        P("dp", "ctx"),
        P("dp", "ctx", None),
    )
    out_specs = (
        P("dp", "ctx", "tensor"),
        P(("dp", "ctx"), "tensor"),
        P("dp", "ctx", "tensor"),
        P(None, "tensor"),
        P("tensor"),
        P(None, "tensor"),
        P("tensor"),
        P("tensor"),
        P(None, "tensor"),
        P(None, "tensor"),
        P(None, None, None, "tensor"),
        P(None, "tensor", None),
        P(None, "tensor"),
        P(None, "tensor"),
        P(None, None, "tensor"),
        P(None, "tensor"),
        P(None, "tensor", None),
    )
    return jax.shard_map(shards, mesh=mesh, in_specs=in_specs, out_specs=out_specs, check_vma=False)
```

```python
import jax
import jax.numpy as jnp
from jax import lax
from jax.experimental import pallas as pl
from jax.experimental.pallas import tpu as pltpu
from jax.sharding import PartitionSpec as P

HEAD_DIM = 64
HEADS = 12
NL = 2
L = 512
HALF = 256
D = 768
DEV = 192
IMG_GROUP = 30
EPS = 1e-06
MASKED = -1e30
MESH = pl.DeviceIdType.MESH
BF = jnp.bfloat16
F32 = jnp.float32

STEM = 384
LAYER = 2304
ROWS = STEM + NL * LAYER

GATHER_UNITS = [
    (0, 128, 512, 512),
    (1152, 256, 512, 0),
    (1920, 256, 0, 512),
    (2688, 256, 512, 0),
    (3456, 256, 0, 512),
    (4224, 256, 512, 0),
]

PIECES = [(0, 0), (0, 1), (1, 0), (2, 1), (3, 0), (4, 1), (5, 0)]

GRAD_ROWS = NL * LAYER + 512


def place():
    d = lax.axis_index("dp")
    c = lax.axis_index("ctx")
    t = lax.axis_index("tensor")
    return d // 4, d % 4, c, t


def peer(axis, r):
    z, y, c, t = place()
    if axis == "x":
        return (z * 4 + y, c, (t + r) % 4)
    if axis == "y":
        return (z * 4 + (y + r) % 4, c, t)
    return (((z + r) % 4) * 4 + y, c, t)


def sibling():
    z, y, c, t = place()
    return (z * 4 + y, 1 - c, t)


def greet(stem):
    z, y, c, t = place()
    bar = pltpu.get_barrier_semaphore()
    for axis in "xyz":
        for r in (1, 2, 3):
            pl.semaphore_signal(bar, inc=1, device_id=peer(axis, r), device_id_type=MESH)
    pl.semaphore_signal(bar, inc=1, device_id=sibling(), device_id_type=MESH)
    count = 4 if stem == "in" else 16

    def hello(i, carry):
        if stem == "in":
            other = (t * 4 + i, c, z)
        else:
            other = (i, c, z)
        me = (z * 4 + y == other[0]) & (t == other[2])

        @pl.when(jnp.logical_not(me))
        def _():
            pl.semaphore_signal(bar, inc=1, device_id=other, device_id_type=MESH)

        return carry

    lax.fori_loop(0, count, hello, 0)
    own = t == z

    @pl.when(own)
    def _():
        pl.semaphore_wait(bar, 9 + count)

    @pl.when(jnp.logical_not(own))
    def _():
        pl.semaphore_wait(bar, 10 + count)


def remote(src, dst, send, recv, device):
    return pltpu.make_async_remote_copy(
        src_ref=src, dst_ref=dst, send_sem=send, recv_sem=recv, device_id=device, device_id_type=MESH
    )


class Gather:
    def __init__(self, buf, pieces, send, recv):
        self.buf, self.pieces, self.send, self.recv = buf, pieces, send, recv

    def copy(self, unit, sem, src, dst, device):
        return remote(src, dst, self.send.at[unit, sem], self.recv.at[unit, sem], device)

    def planes(self, unit):
        first, nx, nyz, nzy = GATHER_UNITS[unit]
        z, y, c, t = place()
        out = []
        if nyz:
            out.append((4, "z", z, "y", y, first + nx + c * 256, PIECES.index((unit, 0))))
        if nzy:
            out.append((14, "y", y, "z", z, first + nx + nyz + c * 256, PIECES.index((unit, 1))))
        return out

    def stage(self, unit, which):
        first, nx, nyz, nzy = GATHER_UNITS[unit]
        z, y, c, t = place()
        m = lambda v: pl.multiple_of(v, 16)
        buf = self.buf
        n = nx // 2
        row = first + c * n
        out = []
        if which == 0:
            rows = pl.ds(m(row), n)
            out.append(self.copy(unit, 0, buf.at[0, rows], buf.at[1, rows], peer("x", -1)))
            out.append(self.copy(unit, 1, buf.at[0, rows], buf.at[3, rows], peer("x", 1)))
        if which == 4:
            rows = pl.ds(m(row), n // 2)
            out.append(self.copy(unit, 2, buf.at[1, rows], buf.at[2, rows], peer("x", -1)))
            rows = pl.ds(m(row + n // 2), n // 2)
            out.append(self.copy(unit, 3, buf.at[3, rows], buf.at[2, rows], peer("x", 1)))
        if which == 5:
            for k, (at, rows) in enumerate([(first, nx), (first + nx, nyz), (first + nx + nyz, nzy)]):
                if rows:
                    region = buf.at[pl.ds(1, 3), pl.ds(m(at + c * (rows // 2)), rows // 2)]
                    out.append(self.copy(unit, 24 + k, region, region, sibling()))
        for sem, slow, p, fast, q, row, k in self.planes(unit):
            block = lambda p, o, rows: buf.at[pl.ds(1, 3), pl.ds(m(row + p * 64 + o), rows)]
            if which == 1:
                rows = pl.ds(m(row + p * 64 + q * 16), 16)
                for r in (1, 2, 3):
                    out.append(self.copy(unit, sem + r - 1, self.pieces.at[k], buf.at[r, rows], peer("x", -r)))
            if which == 2:
                region = block(p, q * 16, 16)
                for r in (1, 2, 3):
                    out.append(self.copy(unit, sem + 2 + r, region, region, peer(fast, -r)))
            if which == 3:
                region = block(p, 0, 64)
                out.append(self.copy(unit, sem + 6, region, region, peer(slow, -1)))
                out.append(self.copy(unit, sem + 7, region, region, peer(slow, 1)))
            if which == 4:
                region = block((p + 1) % 4, 0, 32)
                out.append(self.copy(unit, sem + 8, region, region, peer(slow, -1)))
                region = block((p + 3) % 4, 32, 32)
                out.append(self.copy(unit, sem + 9, region, region, peer(slow, 1)))
        return out

    def start(self, unit, which):
        for copy in self.stage(unit, which):
            copy.start()

    def arrived(self, unit, which):
        for copy in self.stage(unit, which):
            copy.wait_recv()

    def finish(self, unit):
        for which in range(6):
            for copy in self.stage(unit, which):
                copy.wait_send()


def scatter_patches(stage, out, send, recv, own, mode):
    z, y, c, t = place()

    def each(i, carry):
        me = (t == z) & (i == y)
        local = pltpu.make_async_copy(stage.at[i], out.at[y], own)
        away = remote(stage.at[i], out.at[y], send.at[i], recv.at[y], (t * 4 + i, c, z))
        back = remote(stage.at[i], out.at[i], send.at[i], recv.at[i], (t * 4 + i, c, z))

        @pl.when(me)
        def _():
            local.start() if mode == "start" else local.wait()

        @pl.when(jnp.logical_not(me))
        def _():
            if mode == "start":
                away.start()
            else:
                back.wait_send()
                back.wait_recv()

        return carry

    lax.fori_loop(0, 4, each, 0)


def dot_nt(a, b):
    return lax.dot_general(a, b, (((1,), (1,)), ((), ())), preferred_element_type=F32)


def dot_tn(a, b):
    return lax.dot_general(a, b, (((0,), (0,)), ((), ())), preferred_element_type=F32)


def dot_nn(a, b):
    return jnp.dot(a, b, preferred_element_type=F32)


def row_blocks(size, body):
    for i in range(HALF // size):
        body(pl.ds(i * size, size))


def norm_rows(src, gain, shift, dst):
    def body(rows):
        x = src[rows]
        mean = jnp.mean(x, axis=-1, keepdims=True)
        centred = x - mean
        spread = jnp.mean(centred * centred, axis=-1, keepdims=True)
        dst[rows] = (centred * lax.rsqrt(spread + EPS) * gain + shift).astype(BF)

    row_blocks(HALF, body)


GELU_A = 0.7978845608028654
GELU_B = 0.044715


PLAN = {
    "start": [
        ("pieces", 0), ("x", 0), ("pieces", 1), ("plane", 0), ("pieces", 2), ("x", 1), ("pass", 0), ("plane", 1),
        ("pieces", 3), ("share", 0), ("x", 2), ("plane", 2), ("ready", 0),
    ],
    (0, "in"): [("pass", 1), ("pieces", 4)],
    (0, "att0"): [("x", 3), ("plane", 3), ("pass", 2)],
    (0, "att1"): [("share", 1), ("x", 4), ("pieces", 5), ("plane", 4)],
    (0, "up"): [("pass", 3), ("share", 2), ("x", 5), ("plane", 5), ("ready", 1)],
    (0, "down"): [("pass", 4), ("share", 3), ("ready", 2)],
    (1, "in"): [("ready", 3), ("share", 4)],
    (1, "att0"): [("pass", 5)],
    (1, "att1"): [("share", 5)],
    (1, "up"): [("ready", 4)],
    (1, "down"): [("ready", 5)],
}


def gather_kernel(
    patch_w,
    text_w,
    in_w,
    out_w,
    up_w,
    down_w,
    vectors,
    gains,
    stamps_q,
    stamps_k,
    patches,
    words,
    w_out,
    patch_out,
    vec_out,
    xs_out,
    mid_out,
    nrm_out,
    fn_out,
    tri_out,
    kvo_out,
    mix_out,
    lse_out,
    pre_out,
    act_out,
    buf,
    vec,
    gain,
    stamp_q,
    stamp_k,
    pstage,
    prow,
    word,
    xs,
    mid,
    nrm,
    fn,
    tri,
    kvo,
    mix,
    lse,
    pre,
    act,
    bias,
    hid,
    pieces,
    local,
    send,
    recv,
    psend,
    precv,
    own,
    vsend,
    vrecv,
    ksend,
    krecv,
    saved,
):
    z, y, c, t = place()
    g = Gather(buf, pieces, send, recv)
    sources = [(patch_w, 0, 192), (text_w, 192, 192)]
    for which in range(NL):
        base = STEM + which * LAYER
        sources += [
            (in_w.at[which], base, 576),
            (out_w.at[which], base + 576, 192),
            (up_w.at[which], base + 768, 768),
            (down_w.at[which], base + 1536, 768),
        ]
    loads = [
        pltpu.make_async_copy(ref, buf.at[0, pl.ds(row, rows)], local.at[2 + k])
        for k, (ref, row, rows) in enumerate(sources)
    ]
    first = [
        pltpu.make_async_copy(patches, pstage, local.at[0]),
        pltpu.make_async_copy(vectors, vec.at[0], local.at[1]),
    ]
    late = [
        pltpu.make_async_copy(words, word, local.at[12]),
        pltpu.make_async_copy(gains, gain, local.at[13]),
        pltpu.make_async_copy(stamps_q, stamp_q, local.at[14]),
        pltpu.make_async_copy(stamps_k, stamp_k, local.at[15]),
    ]
    for k, (unit, colour) in enumerate(PIECES):
        spot = {sem: (row, p, q) for sem, _, p, _, q, row, _ in g.planes(unit)}
        row, p, q = spot[4 + 10 * colour]
        row = row + p * 64 + q * 16
        low = GATHER_UNITS[unit][0] + sum(GATHER_UNITS[unit][1 : 2 + colour])
        for ref, at, rows in sources:
            if at < low + 512 and at + rows > low:

                @pl.when((row >= at) & (row < at + rows))
                def _(ref=ref, at=at, rows=rows):
                    there = jnp.clip(row - at, 0, rows - 16)
                    src = ref.at[pl.ds(pl.multiple_of(there, 16), 16)]
                    pltpu.make_async_copy(src, pieces.at[k], local.at[16 + k]).start()

    for copy in first + loads + late:
        copy.start()
    greet("in")
    for k, (unit, colour) in enumerate(PIECES):
        pltpu.make_async_copy(up_w.at[0, pl.ds(0, 16)], pieces.at[k], local.at[16 + k]).wait()
        if PIECES[k + 1 : k + 2] and PIECES[k + 1][0] == unit:
            continue
        g.start(unit, 1)
    for copy in first:
        copy.wait()
    vec_copies = [
        remote(vec.at[0], vec.at[r], vsend.at[r - 1], vrecv.at[r - 1], peer("x", -r)) for r in (1, 2, 3)
    ]
    for copy in vec_copies:
        copy.start()
    members = [[0, 1, 2, 3], [4], [5], [6, 7], [8], [9]]

    def pieces_on(unit):
        g.arrived(unit, 1)
        g.start(unit, 2)

    def x_on(unit):
        for k in members[unit]:
            loads[k].wait()
        g.start(unit, 0)

    def plane_on(unit):
        g.arrived(unit, 2)
        g.start(unit, 3)

    def pass_on(unit):
        g.arrived(unit, 0)
        g.arrived(unit, 3)
        g.start(unit, 4)

    def share(unit):
        g.arrived(unit, 4)
        g.start(unit, 5)

    saves = []

    def save(k, src, dst):
        copy = pltpu.make_async_copy(src, dst, saved.at[k])
        copy.start()
        saves.append(copy)

    def ready(unit):
        g.arrived(unit, 5)
        rows = pl.ds(GATHER_UNITS[unit][0], sum(GATHER_UNITS[unit][1:]))
        save(14 + unit, buf.at[:, rows], w_out.at[:, rows])

    act_of = {
        "pieces": pieces_on,
        "x": x_on,
        "plane": plane_on,
        "pass": pass_on,
        "share": share,
        "ready": ready,
    }

    def tick(*steps):
        for name, unit in steps:
            act_of[name](unit)

    tick(*PLAN["start"][:4])
    scatter_patches(pstage, prow, psend, precv, own, "start")
    tick(*PLAN["start"][4:5])
    for copy in late:
        copy.wait()

    lse[...] = jnp.zeros_like(lse)

    def see(i, carry):
        rows = pl.ds(pl.multiple_of(i * 64, 64), 64)
        bias[rows] = jnp.where(stamp_k[rows, 0:1] <= stamp_q[0:1, :], 0.0, MASKED)
        return carry

    lax.fori_loop(0, 8, see, 0)

    tick(*PLAN["start"][5:])
    scatter_patches(pstage, prow, psend, precv, own, "wait")
    for copy in vec_copies:
        copy.wait()
    place_in = lax.broadcasted_iota(jnp.int32, (HALF, 1), 0) % (IMG_GROUP + 2)
    parts = []
    for a in range(4):
        s = (a - t) % 4
        picture = dot_nt(prow[...].reshape(HALF, D), buf[s, 0:192]) + vec[s, 2:3, 0:192]
        language = dot_nt(word[...], buf[s, 192:384]) + vec[s, 3:4, 0:192]
        mark = vec[s, 4:5, 0:192]
        part = jnp.where(place_in < IMG_GROUP, picture, jnp.where(place_in == IMG_GROUP, language, mark))
        parts.append(part.astype(BF).astype(F32))
    xs[0] = jnp.concatenate(parts, axis=1)
    save(0, prow, patch_out)
    save(1, vec, vec_out)

    for which in range(NL):
        base = STEM + which * LAYER
        k0 = 20 + 9 * which
        save(k0, xs.at[which], xs_out.at[which])
        tick(*PLAN[which, "in"])
        norm_rows(xs.at[which], gain[which : which + 1], gain[2 + which : 3 + which], nrm.at[which])

        def project(s, carry):
            triple = dot_nt(buf[s, base : base + 576], nrm[which])
            tri[which, s] = triple.astype(BF)
            remote(
                tri.at[which, s, pl.ds(192, 384)],
                kvo.at[which, s],
                ksend.at[which, s],
                krecv.at[which, s],
                sibling(),
            ).start()
            return carry

        lax.fori_loop(0, 4, project, 0)
        save(k0 + 1, nrm.at[which], nrm_out.at[which])
        save(k0 + 2, tri.at[which], tri_out.at[which])
        mid[which] = xs[which]

        def attend(s, carry):
            remote(
                tri.at[which, s, pl.ds(192, 384)],
                kvo.at[which, s],
                ksend.at[which, s],
                krecv.at[which, s],
                sibling(),
            ).wait_recv()
            for h in range(3):
                at = 64 * h
                q = tri[which, s, at : at + 64] * jnp.asarray(HEAD_DIM**-0.5, BF)
                one = dot_tn(tri[which, s, 192 + at : 256 + at], q) + bias[0:256]
                two = dot_tn(kvo[which, s, at : at + 64], q) + bias[256:512]
                top = jnp.maximum(jnp.max(one, axis=0, keepdims=True), jnp.max(two, axis=0, keepdims=True))
                one = jnp.exp(one - top)
                two = jnp.exp(two - top)
                total = jnp.sum(one, axis=0, keepdims=True) + jnp.sum(two, axis=0, keepdims=True)
                lse[which, s, h : h + 1] = top + jnp.log(total)
                scale = 1.0 / total
                one = (one * scale).astype(BF)
                two = (two * scale).astype(BF)
                mixed = dot_nn(tri[which, s, 384 + at : 448 + at], one)
                mixed = mixed + dot_nn(kvo[which, s, 192 + at : 256 + at], two)
                mix[which, s, at : at + 64] = mixed.astype(BF)
            mid[which] += dot_tn(mix[which, s], buf[s, base + 576 : base + 768])
            return carry

        tick(*PLAN[which, "att0"])
        lax.fori_loop(0, 2, attend, 0)
        tick(*PLAN[which, "att1"])
        lax.fori_loop(2, 4, attend, 0)
        save(k0 + 3, kvo.at[which], kvo_out.at[which])
        save(k0 + 4, mix.at[which], mix_out.at[which])
        save(k0 + 5, lse.at[which], lse_out.at[which])
        save(k0 + 6, mid.at[which], mid_out.at[which])
        norm_rows(mid.at[which], gain[4 + which : 5 + which], gain[6 + which : 7 + which], fn.at[which])
        tick(*PLAN[which, "up"])

        def lift(s, carry):
            pre[which, s] = dot_nn(fn[which], buf[s, base + 768 : base + 1536]) + vec[s, which : which + 1]
            return carry

        save(k0 + 7, fn.at[which], fn_out.at[which])
        lax.fori_loop(0, 4, lift, 0)
        save(k0 + 8, pre.at[which], pre_out.at[which])
        xs[which + 1] = mid[which]
        tick(*PLAN[which, "down"])

        def lower(s, carry):
            def body(rows):
                x = pre[which, s, rows]
                hid[rows] = (0.5 * x * (1.0 + jnp.tanh(GELU_A * (x + GELU_B * x * x * x)))).astype(BF)

            row_blocks(HALF, body)
            xs[which + 1] += dot_nn(hid[...], buf[s, base + 1536 : base + 2304])
            return carry

        lax.fori_loop(0, 4, lower, 0)

    flipped = xs[2].astype(BF).T
    for a in range(4):
        act[a] = flipped[192 * a : 192 * a + 192]
    save(13, act, act_out)
    for which in range(NL):
        for s in range(4):
            remote(
                tri.at[which, s, pl.ds(192, 384)],
                kvo.at[which, s],
                ksend.at[which, s],
                krecv.at[which, s],
                sibling(),
            ).wait_send()
    for unit in range(6):
        g.finish(unit)
    for copy in saves:
        copy.wait()


def forward_call(*args):
    any_ = pl.BlockSpec(memory_space=pl.ANY)
    sds = jax.ShapeDtypeStruct
    shapes = [
        ((4, ROWS, D), BF),
        ((4, 64, D), BF),
        ((4, 8, D), F32),
        ((2, HALF, D), F32),
        ((2, HALF, D), F32),
        ((2, HALF, D), BF),
        ((2, HALF, D), BF),
        ((2, 4, 576, HALF), BF),
        ((2, 4, 384, HALF), BF),
        ((2, 4, 192, HALF), BF),
        ((2, 4, 8, HALF), F32),
        ((2, 4, HALF, D), F32),
        ((4, 192, HALF), BF),
    ]
    dma = pltpu.SemaphoreType.DMA
    return pl.pallas_call(
        gather_kernel,
        out_shape=tuple(sds(s, d) for s, d in shapes),
        in_specs=[any_] * 12,
        out_specs=(any_,) * len(shapes),
        scratch_shapes=[
            pltpu.VMEM((4, ROWS, D), BF),
            pltpu.VMEM((4, 8, D), F32),
            pltpu.VMEM((8, D), F32),
            pltpu.VMEM((8, HALF), jnp.int32),
            pltpu.VMEM((L, 128), jnp.int32),
            pltpu.VMEM((4, 64, D), BF),
            pltpu.VMEM((4, 64, D), BF),
            pltpu.VMEM((HALF, D), BF),
            pltpu.VMEM((3, HALF, D), F32),
            pltpu.VMEM((2, HALF, D), F32),
            pltpu.VMEM((2, HALF, D), BF),
            pltpu.VMEM((2, HALF, D), BF),
            pltpu.VMEM((2, 4, 576, HALF), BF),
            pltpu.VMEM((2, 4, 384, HALF), BF),
            pltpu.VMEM((2, 4, 192, HALF), BF),
            pltpu.VMEM((2, 4, 8, HALF), F32),
            pltpu.VMEM((2, 4, HALF, D), F32),
            pltpu.VMEM((4, 192, HALF), BF),
            pltpu.VMEM((L, HALF), F32),
            pltpu.VMEM((HALF, D), BF),
            pltpu.VMEM((7, 16, D), BF),
            dma((23,)),
            dma((6, 27)),
            dma((6, 27)),
            dma((4,)),
            dma((4,)),
            dma,
            dma((3,)),
            dma((3,)),
            dma((2, 4)),
            dma((2, 4)),
            dma((38,)),
        ],
        compiler_params=pltpu.CompilerParams(
            collective_id=0, has_side_effects=True, vmem_limit_bytes=63 * 2**20
        ),
    )(*args)


def prepare(
    patches,
    text_features,
    patch_weight,
    patch_bias,
    text_weight,
    text_bias,
    readout,
    mix_gain,
    mix_shift,
    heads_in_weight,
    heads_out_weight,
    feed_gain,
    feed_shift,
    up_weight,
    up_bias,
    down_weight,
    timesteps,
):
    t = lax.axis_index("tensor")
    c = lax.axis_index("ctx")
    wide = lambda v: jnp.pad(v.astype(F32), (0, D - DEV))[None]
    vectors = jnp.concatenate(
        [up_bias, wide(patch_bias), wide(text_bias), wide(readout), jnp.zeros((3, D), F32)], axis=0
    )
    gains = jnp.concatenate([mix_gain, mix_shift, feed_gain, feed_shift], axis=0)
    stamps = lax.dynamic_slice_in_dim(timesteps, t, 1, 0).reshape(2, HALF)
    mine = lax.dynamic_slice_in_dim(stamps, c, 1, 0)
    other = lax.dynamic_slice_in_dim(stamps, 1 - c, 1, 0)
    stamps_q = jnp.broadcast_to(mine, (8, HALF))
    stamps_k = jnp.broadcast_to(jnp.concatenate([mine, other], 1).reshape(L, 1), (L, 128))
    spaced = lax.dynamic_slice_in_dim(patches, t * 240, 240, 0).reshape(4, 2, IMG_GROUP, D)
    spaced = jnp.pad(spaced, ((0, 0), (0, 0), (0, 2), (0, 0))).reshape(4, 64, D)
    words = lax.dynamic_slice_in_dim(text_features, t, 1, 0).reshape(8, 1, D)
    words = jnp.pad(words, ((0, 0), (IMG_GROUP, 1), (0, 0))).reshape(HALF, D)
    return (
        patch_weight.T,
        text_weight.T,
        heads_in_weight.transpose(0, 2, 3, 1).reshape(NL, 3 * DEV, D),
        heads_out_weight,
        up_weight,
        down_weight,
        vectors,
        gains,
        stamps_q,
        stamps_k,
        spaced,
        words,
    )


SUM_UNITS = [
    (256, 512, "z"),
    (768, 0, "z"),
    (256, 512, "y"),
    (256, 512, "z"),
    (768, 0, "z"),
    (256, 512, "y"),
    (0, 512, "z"),
]
SUM_BASE = [768, 2304, 3840, 0, 1536, 3072, 4608]
NU = len(SUM_UNITS)
STEMS = 6


class Sums:
    def __init__(self, grads, core_in, big, small, out, send, recv, local, credit):
        self.grads, self.core_in, self.big, self.small = grads, core_in, big, small
        self.out, self.send, self.recv, self.local, self.credit = out, send, recv, local, credit

    def where(self, u):
        nx, npl, slow = SUM_UNITS[u]
        z, y, c, t = place()
        fast = "y" if slow == "z" else "z"
        m = lambda v: pl.multiple_of(v, 16)
        return nx // 2, npl // 2, nx + c * (npl // 2), slow, fast, {"z": z, "y": y}, c, t, m

    def copy(self, u, sem, src, dst, device):
        return remote(src, dst, self.send.at[u, sem], self.recv.at[u, sem], device)

    def core(self, u, s):
        n, p, _, slow, fast, at, c, t, m = self.where(u)
        g, into = self.grads.at[u % 3], self.core_in.at[u % 2]
        out = []
        if n:
            src = g.at[s, pl.ds(m((1 - c) * n), n)]
            out.append(self.copy(u, s, src, into.at[s, pl.ds(0, n)], sibling()))
        if p:
            src = g.at[s, pl.ds(m(2 * n + (1 - c) * p), p)]
            out.append(self.copy(u, 4 + s, src, into.at[s, pl.ds(n, p)], sibling()))
        return out

    def begin(self, u):
        if u >= 2:
            pl.semaphore_wait(self.credit, 1)

    def give(self, u, s):
        for copy in self.core(u, s):
            copy.start()

    def cores(self, u):
        return [copy for s in range(4) for copy in self.core(u, s)]

    def across(self, u):
        n, p, row, slow, fast, at, c, t, m = self.where(u)
        g, big = self.grads.at[u % 3], self.big[u % 3]
        out = []
        if n:
            h = n // 2
            out.append(self.copy(u, 8, g.at[2, pl.ds(m(c * n), h)], big["xa"].at[0], peer("x", 1)))
            out.append(self.copy(u, 9, g.at[2, pl.ds(m(c * n + h), h)], big["xa"].at[1], peer("x", -1)))
        if p:
            block = row + (at[slow] + 2) % 4 * 64
            out.append(self.copy(u, 10, g.at[:, pl.ds(m(block), 32)], big["pa"].at[0], peer(slow, 1)))
            out.append(self.copy(u, 11, g.at[:, pl.ds(m(block + 32), 32)], big["pa"].at[1], peer(slow, -1)))
        return out

    def beside(self, u):
        n, p, row, slow, fast, at, c, t, m = self.where(u)
        g, big = self.grads.at[u % 3], self.big[u % 3]
        out = []
        if n:
            rows = pl.ds(m(c * n), n)
            out.append(self.copy(u, 12, g.at[1, rows], big["xr"].at[0], peer("x", 1)))
            out.append(self.copy(u, 13, g.at[3, rows], big["xr"].at[1], peer("x", -1)))
        if p:
            for k, r in ((0, 1), (1, 3)):
                block = row + (at[slow] + r) % 4 * 64
                out.append(self.copy(u, 14 + k, g.at[:, pl.ds(m(block), 64)], big["pr"].at[k], peer(slow, r)))
        return out

    def second(self, u):
        n, p, row, slow, fast, at, c, t, m = self.where(u)
        big, small = self.big[u % 3], self.small[u]
        out = []
        for r in (1, 2, 3):
            if n:
                block = pl.ds(m((at["y"] + r) % 4 * (n // 4)), n // 4)
                out.append(self.copy(u, 15 + r, big["xs"].at[block], small["yr"].at[r - 1], peer("y", r)))
            if p:
                block = pl.ds(m((at[fast] + r) % 4 * 16), 16)
                out.append(self.copy(u, 18 + r, big["ps"].at[:, block], small["qr"].at[r - 1], peer(fast, r)))
        return out

    def third(self, u):
        n, p, row, slow, fast, at, c, t, m = self.where(u)
        small = self.small[u]
        out = []
        for r in (1, 2, 3):
            if n:
                mine = small["zb"].at[at["z"]]
                out.append(self.copy(u, 21 + r, mine, mine, peer("z", r)))
            if p:
                out.append(self.copy(u, 24 + r, small["qs"].at[r], small["tr"].at[r - 1], peer("x", r)))
        return out

    def rows(self, u):
        n, p, row, slow, fast, at, c, t, m = self.where(u)
        base = SUM_BASE[u]
        return (
            pl.ds(m(base + c * n), n),
            pl.ds(m(base + c * n + at["y"] * (n // 4)), n // 4),
            pl.ds(m(base + row), p),
            pl.ds(m(base + row + at[slow] * 64), 64),
            pl.ds(m(base + row + at[slow] * 64 + at[fast] * 16), 16),
        )

    def fourth(self, u):
        n, p, row, slow, fast, at, c, t, m = self.where(u)
        small = self.small[u]
        _, x_own, _, _, p_own = self.rows(u)
        out = []
        for r in (1, 2, 3):
            if n:
                out.append(self.copy(u, 27 + r, small["fx"], self.out.at[x_own], peer("y", r)))
            if p:
                out.append(self.copy(u, 30 + r, small["fp"], self.out.at[p_own], peer(fast, r)))
        return out

    def own(self, u):
        n, p = self.where(u)[:2]
        _, x_own, _, _, p_own = self.rows(u)
        out = []
        if n:
            out.append(pltpu.make_async_copy(self.small[u]["fx"], self.out.at[x_own], self.local.at[u, 0]))
        if p:
            out.append(pltpu.make_async_copy(self.small[u]["fp"], self.out.at[p_own], self.local.at[u, 1]))
        return out

    def fifth(self, u):
        n, p, row, slow, fast, at, c, t, m = self.where(u)
        if not p:
            return []
        region = self.out.at[self.rows(u)[3]]
        return [self.copy(u, 33 + r, region, region, peer(slow, r)) for r in (1, 2, 3)]

    def sixth(self, u):
        n, p = self.where(u)[:2]
        x_all, _, p_all, _, _ = self.rows(u)
        out = []
        if n:
            region = self.out.at[x_all]
            out.append(self.copy(u, 37, region, region, sibling()))
        if p:
            region = self.out.at[p_all]
            out.append(self.copy(u, 38, region, region, sibling()))
        return out

    def add(self, u, count, size, terms, result):
        def step(i, carry):
            total = None
            for ref, index in terms(i):
                v = ref[index].astype(F32)
                total = v if total is None else total + v
            ref, index = result(i)
            ref[index] = total.astype(BF)
            return carry

        if count == 1:
            step(0, 0)
        else:
            lax.fori_loop(0, count, step, 0)

    def step(self, k, u):
        n, p, row, slow, fast, at, c, t, m = self.where(u)
        g, big, small = self.grads.at[u % 3], self.big[u % 3], self.small[u]
        if k == 1:
            for copy in self.cores(u):
                copy.wait_recv()
            for first, there, rows in ((c * n, 0, n), (row, n, p)):
                if rows:
                    per = rows // 128
                    mine = lambda i: (g, (i // per, pl.ds(m(first + i % per * 128), 128)))
                    its = lambda i: (self.core_in.at[u % 2], (i // per, pl.ds(m(there + i % per * 128), 128)))
                    self.add(u, 4 * per, 128, lambda i: [mine(i), its(i)], mine)
            if u + 2 < NU:
                pl.semaphore_signal(self.credit, inc=1, device_id=sibling(), device_id_type=MESH)
            for copy in self.across(u):
                copy.start()
        if k == 2:
            for copy in self.across(u):
                copy.wait_recv()
            if n:
                h = n // 2
                for k, slot, first in ((0, 1, c * n), (1, 3, c * n + h)):
                    mine = lambda i: (g, (slot, pl.ds(m(first + i * 64), 64)))
                    its = lambda i: (big["xa"], (k, pl.ds(m(i * 64), 64)))
                    self.add(u, h // 64, 64, lambda i: [mine(i), its(i)], mine)
            if p:
                for k, r in ((0, 1), (1, 3)):
                    first = row + (at[slow] + r) % 4 * 64 + 32 * k
                    mine = lambda i: (g, (i, pl.ds(m(first), 32)))
                    its = lambda i: (big["pa"], (k, i))
                    self.add(u, 4, 32, lambda i: [mine(i), its(i)], mine)
            for copy in self.beside(u):
                copy.start()
        if k == 3:
            for copy in self.beside(u):
                copy.wait_recv()
            if n:
                self.add(
                    u,
                    n // 64,
                    64,
                    lambda i: [(g, (0, pl.ds(m(c * n + i * 64), 64)))]
                    + [(big["xr"], (r, pl.ds(m(i * 64), 64))) for r in range(2)],
                    lambda i: (big["xs"], pl.ds(m(i * 64), 64)),
                )
            if p:
                first = row + at[slow] * 64
                self.add(
                    u,
                    4,
                    64,
                    lambda i: [(g, (i, pl.ds(m(first), 64)))] + [(big["pr"], (r, i)) for r in range(2)],
                    lambda i: (big["ps"], i),
                )
            for copy in self.second(u):
                copy.start()
            for copy in self.cores(u) + self.across(u) + self.beside(u):
                copy.wait_send()
        if k == 4:
            for copy in self.second(u):
                copy.wait_recv()
            if n:
                own = pl.ds(m(at["y"] * (n // 4)), n // 4)
                self.add(
                    u,
                    1,
                    n // 4,
                    lambda i: [(big["xs"], own)] + [(small["yr"], r) for r in range(3)],
                    lambda i: (small["zb"], at["z"]),
                )
            if p:
                own = pl.ds(m(at[fast] * 16), 16)
                self.add(
                    u,
                    4,
                    16,
                    lambda i: [(big["ps"], (i, own))] + [(small["qr"], (r, i)) for r in range(3)],
                    lambda i: (small["qs"], i),
                )
            for copy in self.third(u):
                copy.start()
            for copy in self.second(u):
                copy.wait_send()
        if k == 5:
            for copy in self.third(u):
                copy.wait_recv()
            if n:
                self.add(
                    u, 1, n // 4, lambda i: [(small["zb"], r) for r in range(4)], lambda i: (small["fx"], slice(None))
                )
            if p:
                self.add(
                    u,
                    1,
                    16,
                    lambda i: [(small["qs"], 0)] + [(small["tr"], r) for r in range(3)],
                    lambda i: (small["fp"], slice(None)),
                )
            for copy in self.fourth(u) + self.own(u):
                copy.start()
        if k == 6:
            for copy in self.fourth(u):
                copy.wait_recv()
            for copy in self.own(u):
                copy.wait()
            for copy in self.fifth(u) if p else self.sixth(u):
                copy.start()
        if k == 7 and p:
            for copy in self.fifth(u):
                copy.wait_recv()
            for copy in self.sixth(u):
                copy.start()
        if k == 8:
            for copy in self.sixth(u):
                copy.wait_recv()
            for copy in self.third(u) + self.fourth(u) + self.fifth(u) + self.sixth(u):
                copy.wait_send()


def big_shapes():
    out = []
    for nx, npl, _ in SUM_UNITS[:3]:
        n, p = nx // 2, npl // 2
        shapes = {}
        if n:
            shapes |= {"xa": (2, n // 2, D), "xr": (2, n, D), "xs": (n, D)}
        if p:
            shapes |= {"pa": (2, 4, 32, D), "pr": (2, 4, 64, D), "ps": (4, 64, D)}
        out.append(shapes)
    return out


def small_shapes():
    out = []
    for nx, npl, _ in SUM_UNITS:
        q = nx // 8
        shapes = {}
        if nx:
            shapes |= {"yr": (3, q, D), "zb": (4, q, D), "fx": (q, D)}
        if npl:
            shapes |= {"qr": (3, 4, 16, D), "qs": (4, 16, D), "tr": (3, 16, D), "fp": (16, D)}
        out.append(shapes)
    return out


def norm_back(x, grad, base, gain, out, sums, gain_row, shift_row):
    zero = jnp.zeros((1, D), F32)
    sums[gain_row : gain_row + 1] = zero
    sums[shift_row : shift_row + 1] = zero

    def body(rows):
        v = x[rows]
        g = grad[rows]
        mean = jnp.mean(v, axis=-1, keepdims=True)
        centred = v - mean
        spread = jnp.mean(centred * centred, axis=-1, keepdims=True)
        inv = lax.rsqrt(spread + EPS)
        hat = centred * inv
        sums[gain_row : gain_row + 1] += jnp.sum(g * hat, axis=0, keepdims=True)
        sums[shift_row : shift_row + 1] += jnp.sum(g, axis=0, keepdims=True)
        d = g * gain
        first = jnp.mean(d, axis=-1, keepdims=True)
        second = jnp.mean(d * hat, axis=-1, keepdims=True)
        out[rows] = base[rows] + inv * (d - first - hat * second)

    row_blocks(HALF, body)


def returns(act, act_out, pgs, pg_out, tgs, tg_out, send, recv, own, mode, which):
    z, y, c, t = place()
    d = z * 4 + y
    if which == 0:
        for r in (1, 2, 3):
            a = (t + r) % 4
            copy = remote(act.at[a], act_out.at[t], send.at[r], recv.at[r], (d, c, a))
            copy.start() if mode == "start" else copy.wait()
        copy = pltpu.make_async_copy(act.at[t], act_out.at[t], own.at[0])
        copy.start() if mode == "start" else copy.wait()
        return
    for r in (1, 2, 3):
        a = (t + r) % 4
        copy = remote(tgs.at[a], tg_out.at[t], send.at[4 + r], recv.at[4 + r], (d, c, a))
        copy.start() if mode == "start" else copy.wait()
    copy = pltpu.make_async_copy(tgs.at[t], tg_out.at[t], own.at[1])
    copy.start() if mode == "start" else copy.wait()

    def each(i, carry):
        a, yy = i % 4, i // 4
        to_me = (t == z) & (yy == y) & (a == t)
        src = pgs.at[a, pl.ds(pl.multiple_of(yy * 64, 64), 64)]
        local = pltpu.make_async_copy(src, pg_out.at[d], own.at[2])
        away = remote(src, pg_out.at[d], send.at[8 + i], recv.at[8 + d], (t * 4 + yy, c, a))

        @pl.when(to_me)
        def _():
            local.start() if mode == "start" else local.wait()

        @pl.when(jnp.logical_not(to_me))
        def _():
            away.start() if mode == "start" else away.wait_send()

        return carry

    lax.fori_loop(0, 16, each, 0)
    if mode == "wait":

        def arrive(i, carry):
            from_me = (t == z) & (i == d)

            @pl.when(jnp.logical_not(from_me))
            def _():
                remote(pg_out.at[i], pg_out.at[i], send.at[8 + i], recv.at[8 + i], (i, c, z)).wait_recv()

            return carry

        lax.fori_loop(0, 16, arrive, 0)


SUM_PLAN = {
    (1, "down"): [(1, 0)],
    (1, "up"): [(2, 0), (1, 1)],
    (1, "att1"): [],
    (1, "att2"): [(3, 0), (2, 1)],
    (1, "in"): [(1, 2), (4, 0)],
    (0, "down"): [(1, 3), (5, 0), (2, 2), (3, 1)],
    (0, "up"): [(2, 3), (1, 4), (6, 0), (3, 2)],
    (0, "att1"): [(4, 1), (2, 4), (3, 3), (7, 0)],
    (0, "att2"): [(4, 2), (5, 1)],
    (0, "in"): [(1, 5), (3, 4), (4, 3), (6, 1), (5, 2)],
    "stem": [(1, 6), (2, 5), (4, 4), (2, 6), (5, 3), (6, 2)],
    "end": [
        (3, 5), (3, 6), (4, 5), (4, 6), (6, 3), (5, 5), (5, 6), (5, 4), (6, 5), (6, 6), (7, 2), (6, 4), (7, 3), (7, 5),
        (7, 6),
    ],
}


def backward_kernel(
    w_in,
    patch_in,
    xs_in,
    mid_in,
    nrm_in,
    fn_in,
    tri_in,
    kvo_in,
    mix_in,
    lse_in,
    pre_in,
    act_in,
    gains,
    stamps_q,
    stamps_k,
    words,
    cotangent,
    row_scale,
    out,
    act_out,
    pg_out,
    tg_out,
    wb,
    gain,
    stamp_q,
    stamp_k,
    prow,
    word,
    cot,
    rscale,
    xs,
    mid,
    nrm,
    fn,
    tri,
    kvo,
    mix,
    lse,
    pre,
    bias,
    up,
    low,
    back,
    hgrad,
    hid,
    pgrad,
    fnt,
    kvg,
    kvs,
    rkv,
    tgrad,
    sums,
    vec,
    pgs,
    tgs,
    grads,
    core_in,
    big,
    small,
    wsem,
    psem,
    lsem,
    send,
    recv,
    local,
    credit,
    ksend,
    krecv,
    rsend,
    rrecv,
    rown,
):
    z, y, c, t = place()
    copy_in = pltpu.make_async_copy

    def section(row, rows, s):
        return copy_in(w_in.at[s, pl.ds(row, rows)], wb.at[s, pl.ds(0, rows)], wsem.at[s])

    sections = []
    for which in (1, 0):
        base = STEM + which * LAYER
        sections += [(base + 1536, 768), (base + 768, 768), (base, 768)]
    sections.append((0, STEM))

    def kept_pre(which, s):
        return copy_in(pre_in.at[which, s], pre.at[s], psem.at[s])

    def acts(which):
        return [
            copy_in(fn_in.at[which], fn, lsem.at[1]),
            copy_in(mid_in.at[which], mid, lsem.at[2]),
            copy_in(tri_in.at[which], tri, lsem.at[3]),
            copy_in(kvo_in.at[which], kvo, lsem.at[4]),
            copy_in(mix_in.at[which], mix, lsem.at[5]),
            copy_in(lse_in.at[which], lse, lsem.at[6]),
            copy_in(nrm_in.at[which], nrm, lsem.at[7]),
            copy_in(xs_in.at[which], xs, lsem.at[8]),
        ]

    head = [
        copy_in(cotangent.at[t], cot, lsem.at[9]),
        copy_in(row_scale, rscale, lsem.at[10]),
    ]
    for copy in head:
        copy.start()
    for s in range(4):
        section(*sections[0], s).start()
    for s in range(4):
        kept_pre(1, s).start()
    for copy in acts(1):
        copy.start()
    rest = [
        copy_in(gains, gain, lsem.at[11]),
        copy_in(stamps_q, stamp_q, lsem.at[12]),
        copy_in(stamps_k, stamp_k, lsem.at[13]),
        copy_in(patch_in, prow, lsem.at[14]),
        copy_in(words, word, lsem.at[15]),
    ]
    for copy in rest:
        copy.start()
    greet("out")
    returns(act_in, act_out, pgs, pg_out, tgs, tg_out, rsend, rrecv, rown, "start", 0)
    total = Sums(grads, core_in, big, small, out, send, recv, local, credit)

    def comm(key):
        for k, u in SUM_PLAN[key]:
            total.step(k, u)

    for copy in head:
        copy.wait()

    def first_up(rows):
        up[rows] = cot[rows].astype(F32) * rscale[rows, 0:1]

    row_blocks(HALF, first_up)
    vec[...] = jnp.zeros_like(vec)
    sums[...] = jnp.zeros_like(sums)
    for copy in rest:
        copy.wait()

    def see(i, carry):
        rows = pl.ds(pl.multiple_of(i * 64, 64), 64)
        bias[rows] = jnp.where(stamp_k[rows, 0:1] <= stamp_q[0:1, :], 0.0, MASKED)
        return carry

    lax.fori_loop(0, 8, see, 0)

    for which in (1, 0):
        u0 = 0 if which else 3
        loads = [None] + acts(which)

        def round_up(rows):
            low[rows] = up[rows].astype(BF)

        row_blocks(HALF, round_up)
        b = u0 % 3
        after = sections[u0 + 1]

        def down(s, carry):
            section(*sections[u0], s).wait()
            hgrad[...] = dot_nt(low[...], wb[s])
            section(*after, s).start()

            def body(rows):
                x = pre[s, rows]
                th = jnp.tanh(GELU_A * (x + GELU_B * x * x * x))
                hid[rows] = (0.5 * x * (1.0 + th)).astype(BF)
                slope = 0.5 * (1.0 + th) + 0.5 * x * (1.0 - th * th) * (GELU_A * (1.0 + 3.0 * GELU_B * x * x))
                pgrad[s, rows] = (hgrad[rows] * slope).astype(BF)

            row_blocks(HALF, body)
            for j in range(3):
                grads[b, s, 256 * j : 256 * j + 256] = dot_tn(hid[:, 256 * j : 256 * j + 256], low[...]).astype(BF)
            total.give(u0, s)
            vec[s, which : which + 1] = jnp.sum(pgrad[s].astype(F32), axis=0, keepdims=True)
            return carry

        for s in range(4):
            kept_pre(which, s).wait()
        total.begin(u0)
        lax.fori_loop(0, 4, down, 0)
        if which:
            for s in range(4):
                kept_pre(0, s).start()
        comm((which, "down"))

        b = (u0 + 1) % 3
        after = sections[u0 + 2]
        loads[1].wait()
        fnt[...] = fn[...].T
        back[...] = jnp.zeros_like(back)

        def lift(s, carry):
            section(*sections[u0 + 1], s).wait()
            back[...] += dot_nt(pgrad[s], wb[s])
            section(*after, s).start()
            for j in range(3):
                grads[b, s, 256 * j : 256 * j + 256] = dot_nn(fnt[256 * j : 256 * j + 256], pgrad[s]).astype(BF)
            total.give(u0 + 1, s)
            return carry

        total.begin(u0 + 1)
        lax.fori_loop(0, 4, lift, 0)
        if which:
            acts(0)[0].start()
        comm((which, "up"))

        loads[2].wait()
        norm_back(mid, back, up, gain[4 + which : 5 + which], up, sums, 6 + which, 8 + which)
        if which:
            acts(0)[1].start()
        row_blocks(HALF, round_up)
        for k in (3, 4, 5, 6):
            loads[k].wait()
        b = (u0 + 2) % 3
        after = sections[u0 + 3]

        def share(s):
            return remote(kvs.at[which, s], rkv.at[which, s], ksend.at[which, s], krecv.at[which, s], sibling())

        def attend(s, carry):
            section(*sections[u0 + 2], s).wait()
            grads[b, s, 576:768] = dot_nn(mix[s], low[...]).astype(BF)
            mixed = dot_nt(wb[s, 576:768], low[...]).astype(BF)
            for h in range(3):
                at = 64 * h
                q = tri[s, at : at + 64] * jnp.asarray(HEAD_DIM**-0.5, BF)
                do = mixed[at : at + 64]
                k1, v1 = tri[s, 192 + at : 256 + at], tri[s, 384 + at : 448 + at]
                k2, v2 = kvo[s, at : at + 64], kvo[s, 192 + at : 256 + at]
                log_total = lse[s, h : h + 1]
                p1 = jnp.exp(dot_tn(k1, q) + bias[0:256] - log_total)
                p2 = jnp.exp(dot_tn(k2, q) + bias[256:512] - log_total)
                d1 = dot_tn(v1, do)
                d2 = dot_tn(v2, do)
                delta = jnp.sum(p1 * d1, axis=0, keepdims=True) + jnp.sum(p2 * d2, axis=0, keepdims=True)
                g1 = (p1 * (d1 - delta)).astype(BF)
                g2 = (p2 * (d2 - delta)).astype(BF)
                dq = (dot_nn(k1, g1) + dot_nn(k2, g2)) * HEAD_DIM**-0.5
                tgrad[s, at : at + 64] = dq.astype(BF)
                kvg[s, at : at + 64] = dot_nt(q, g1)
                kvs[which, s, at : at + 64] = dot_nt(q, g2).astype(BF)
                kvg[s, 192 + at : 256 + at] = dot_nt(do, p1.astype(BF))
                kvs[which, s, 192 + at : 256 + at] = dot_nt(do, p2.astype(BF)).astype(BF)
            share(s).start()
            return carry

        lax.fori_loop(0, 2, attend, 0)
        comm((which, "att1"))
        lax.fori_loop(2, 4, attend, 0)
        if which:
            for k in (3, 4, 5, 6):
                acts(0)[k - 1].start()
        comm((which, "att2"))
        loads[7].wait()
        back[...] = jnp.zeros_like(back)

        def lead(s, carry):
            share(s).wait_recv()
            tgrad[s, 192:576] = (kvg[s] + rkv[which, s].astype(F32)).astype(BF)
            grads[b, s, 0:576] = dot_nn(tgrad[s], nrm[...]).astype(BF)
            total.give(u0 + 2, s)
            back[...] += dot_tn(tgrad[s], wb[s, 0:576])
            section(*after, s).start()
            return carry

        total.begin(u0 + 2)
        lax.fori_loop(0, 4, lead, 0)
        if which:
            acts(0)[6].start()
        comm((which, "in"))
        loads[8].wait()
        norm_back(xs, back, up, gain[which : which + 1], up, sums, 2 + which, 4 + which)
        if which:
            acts(0)[7].start()

    row_blocks(HALF, round_up)
    place_in = lax.broadcasted_iota(jnp.int32, (HALF, 1), 0) % (IMG_GROUP + 2)
    rounded = low[...].astype(F32)
    sums[10:11] = jnp.sum(jnp.where(place_in < IMG_GROUP, rounded, 0.0), axis=0, keepdims=True)
    sums[11:12] = jnp.sum(jnp.where(place_in == IMG_GROUP, rounded, 0.0), axis=0, keepdims=True)
    sums[12:13] = jnp.sum(jnp.where(place_in > IMG_GROUP, up[...], 0.0), axis=0, keepdims=True)
    fnt[...] = low[...].T
    b = STEMS % 3
    back[...] = jnp.zeros_like(back)
    hgrad[...] = jnp.zeros_like(hgrad)
    total.begin(STEMS)
    for a in range(4):
        s = (a - t) % 4
        section(*sections[6], s).wait()
        mine = fnt[192 * a : 192 * a + 192]
        grads[b, s, 0:192] = dot_nn(mine, prow[...].reshape(HALF, D)).astype(BF)
        grads[b, s, 192:384] = dot_nn(mine, word[...]).astype(BF)
        vec[s, 2:16] = sums[2:16]
        grads[b, s, 384:400] = vec[s].astype(BF)
        grads[b, s, 400:512] = jnp.zeros((112, D), BF)
        back[...] += dot_tn(mine, wb[s, 0:192])
        hgrad[...] += dot_tn(mine, wb[s, 192:384])
    for s in range(4):
        total.give(STEMS, s)
    comm("stem")
    for a in range(4):
        pgs[a] = back[:, 192 * a : 192 * a + 192].astype(BF)
    for h in range(8):
        row = hgrad[32 * h + 30 : 32 * h + 31]
        for a in range(4):
            tgs[a, h : h + 1] = row[:, 192 * a : 192 * a + 192]
    returns(act_in, act_out, pgs, pg_out, tgs, tg_out, rsend, rrecv, rown, "start", 1)
    comm("end")
    returns(act_in, act_out, pgs, pg_out, tgs, tg_out, rsend, rrecv, rown, "wait", 0)
    returns(act_in, act_out, pgs, pg_out, tgs, tg_out, rsend, rrecv, rown, "wait", 1)
    for which in range(NL):
        for s in range(4):
            remote(kvs.at[which, s], rkv.at[which, s], ksend.at[which, s], krecv.at[which, s], sibling()).wait_send()
    for u in range(NU):
        total.step(8, u)


def backward_call(*args):
    any_ = pl.BlockSpec(memory_space=pl.ANY)
    sds = jax.ShapeDtypeStruct
    dma = pltpu.SemaphoreType.DMA
    v = pltpu.VMEM
    return pl.pallas_call(
        backward_kernel,
        out_shape=(
            sds((6 * D + 512, D), BF),
            sds((4, 192, HALF), BF),
            sds((16, 64, 192), BF),
            sds((4, 8, 192), F32),
        ),
        in_specs=[any_] * 18,
        out_specs=(any_,) * 4,
        scratch_shapes=[
            v((4, D, D), BF),
            v((8, D), F32),
            v((8, HALF), jnp.int32),
            v((L, 128), jnp.int32),
            v((4, 64, D), BF),
            v((HALF, D), BF),
            v((HALF, D), BF),
            v((HALF, 128), F32),
            v((HALF, D), F32),
            v((HALF, D), F32),
            v((HALF, D), BF),
            v((HALF, D), BF),
            v((4, 576, HALF), BF),
            v((4, 384, HALF), BF),
            v((4, 192, HALF), BF),
            v((4, 8, HALF), F32),
            v((4, HALF, D), F32),
            v((L, HALF), F32),
            v((HALF, D), F32),
            v((HALF, D), BF),
            v((HALF, D), F32),
            v((HALF, D), F32),
            v((HALF, D), BF),
            v((4, HALF, D), BF),
            v((D, HALF), BF),
            v((4, 384, HALF), F32),
            v((2, 4, 384, HALF), BF),
            v((2, 4, 384, HALF), BF),
            v((4, 576, HALF), BF),
            v((16, D), F32),
            v((4, 16, D), F32),
            v((4, HALF, DEV), BF),
            v((4, 8, DEV), F32),
            v((3, 4, D, D), BF),
            v((2, 4, 384, D), BF),
            [{k: v(shape, BF) for k, shape in shapes.items()} for shapes in big_shapes()],
            [{k: v(shape, BF) for k, shape in shapes.items()} for shapes in small_shapes()],
            dma((4,)),
            dma((4,)),
            dma((16,)),
            dma((NU, 39)),
            dma((NU, 39)),
            dma((NU, 2)),
            pltpu.SemaphoreType.REGULAR,
            dma((2, 4)),
            dma((2, 4)),
            dma((24,)),
            dma((24,)),
            dma((3,)),
        ],
        compiler_params=pltpu.CompilerParams(
            collective_id=1, has_side_effects=True, vmem_limit_bytes=63 * 2**20
        ),
    )(*args)


def shards(*args):
    (datasets, dataset_weights, action_mask, cotangent) = args[17:]
    t = lax.axis_index("tensor")
    ops = prepare(*args[:17])
    gains, stamps_q, stamps_k, words = ops[7], ops[8], ops[9], ops[11]
    kept = forward_call(*ops)
    mask = lax.dynamic_slice_in_dim(action_mask, t, 1, 0)[0]
    dataset = lax.dynamic_slice_in_dim(datasets, t, 1, 0)[0]
    weight = lax.dynamic_slice_in_dim(dataset_weights, dataset, 1, 0)[0]
    scale = weight.astype(F32) * mask.astype(F32)
    last = jnp.arange(IMG_GROUP + 2) == IMG_GROUP + 1
    row_scale = jnp.where(last[None, :], scale[:, None], 1.0).reshape(HALF, 1)
    row_scale = jnp.broadcast_to(row_scale, (HALF, 128))
    out, act, pg, tg = backward_call(
        kept[0], kept[1], *kept[3:], gains, stamps_q, stamps_k, words, cotangent, row_scale
    )
    part = lambda a, b: out[a:b].astype(F32)
    down_grad = part(0, 2 * D).reshape(NL, D, D)
    up_grad = part(2 * D, 4 * D).reshape(NL, D, D)
    heads = out[4 * D : 6 * D].reshape(NL, D, D)
    heads_in = heads[:, :576].astype(F32).reshape(NL, 3, DEV, D).transpose(0, 3, 1, 2)
    heads_out = heads[:, 576:].astype(F32)
    vectors = part(6 * D + 384, 6 * D + 400)
    own = lax.dynamic_slice_in_dim(vectors, t * DEV, DEV, 1)
    pg = pg.reshape(16, 2, IMG_GROUP + 2, DEV)[:, :, :IMG_GROUP].reshape(960, DEV).astype(F32)
    return (
        act.transpose(0, 2, 1),
        pg,
        tg,
        part(6 * D, 6 * D + 192).T,
        own[10],
        part(6 * D + 192, 6 * D + 384).T,
        own[11],
        own[12],
        own[2:4],
        own[4:6],
        heads_in,
        heads_out,
        own[6:8],
        own[8:10],
        up_grad,
        vectors[0:2],
        down_grad,
    )


def solution(mesh):
    in_specs = (
        P(("dp", "ctx"), None),
        P("dp", "ctx", None),
        P(None, "tensor"),
        P("tensor"),
        P(None, "tensor"),
        P("tensor"),
        P("tensor"),
        P(),
        P(),
        P(None, None, None, "tensor"),
        P(None, "tensor", None),
        P(),
        P(),
        P(None, None, "tensor"),
        P(None, "tensor"),
        P(None, "tensor", None),
        P("dp", None),
        P("dp"),
        P(),
        P("dp", "ctx"),
        P("dp", "ctx", None),
    )
    out_specs = (
        P("dp", "ctx", "tensor"),
        P(("dp", "ctx"), "tensor"),
        P("dp", "ctx", "tensor"),
        P(None, "tensor"),
        P("tensor"),
        P(None, "tensor"),
        P("tensor"),
        P("tensor"),
        P(None, "tensor"),
        P(None, "tensor"),
        P(None, None, None, "tensor"),
        P(None, "tensor", None),
        P(None, "tensor"),
        P(None, "tensor"),
        P(None, None, "tensor"),
        P(None, "tensor"),
        P(None, "tensor", None),
    )
    return jax.shard_map(shards, mesh=mesh, in_specs=in_specs, out_specs=out_specs, check_vma=False)
```
